256 devices in a mesh: space: 64 (over y_lo, z, x), group: 4 (over y_hi, core).
Axes of the slice: x: 4, y: 4 (y_hi: 2, y_lo: 2; y = y_hi * 2 + y_lo), z: 8, core: 2. Of those that a mesh axis runs over, the one named last changes fastest.
Arguments:
- species: float32 [54, 256, 128, 128], P(None, 'space', 'group'), may hold values from 0 to 0.4
- diffusion: float32 [54], replicated, may hold values from 0.01 to 0.1
- gas_temp: float32 [256, 128, 128], P('space', 'group'), may hold values from 0.6 to 1.6
- gas_density: float32 [256, 128, 128], P('space', 'group'), may hold values from 0.5 to 2
- gas_velocity: float32 [3, 256, 128, 128], P(None, 'space', 'group'), may hold values from -1 to 1
- drop_radius: float32 [1048576], P(('space', 'group')), may hold values from 0.5 to 2
- drop_temp: float32 [1048576], P(('space', 'group')), may hold values from 0.6 to 1.2
- drop_velocity: float32 [3, 1048576], P(None, ('space', 'group')), may hold values from -2 to 2
- parcel_cells: int32 [8, 1048576], P(None, ('space', 'group')), may hold values from 0 to 98303, as said below
- parcel_weights: float32 [8, 1048576], P(None, ('space', 'group')), as said below
- parcel_counts: int32 [64], P('space'), may hold values from 2048 to 16384, as said below
Outputs:
- species_next: float32 [54, 256, 128, 128], P(None, 'space', 'group')
- gas_sources: float32 [7, 256, 128, 128], P(None, 'space', 'group')
- parcel_state: float32 [5, 1048576], P(None, ('space', 'group'))
The draws below stay inside these ranges and needn't reach their ends.
Inputs may be any that keep to these rules, and one draw needn't show every extreme that they name: `parcel_cells`: the eight global indices of a parcel are the corners of one box of 2 x 2 x 2 cells, corner c at offsets (c // 4, c // 2 % 2, c % 2) from the first; that first cell lies in the parcel's slab or in the plane just before it, and the box lies inside the grid. `parcel_weights`: the eight weights of a parcel are non-negative trilinear weights and sum to one. `parcel_counts`: some slab is full in every draw.
All inputs are finite; a program needn't handle non-finite values.
Results may differ from the reference program's by a relative error of at most 0.000058.
Values sent between devices are 32-bit elements; how exact they have to be, the bound alone decides.
No kernel may reach another device: no remote copies, remote signals or barrier semaphores. Data moves between devices by JAX's collectives and lax.ppermute only.
A program may use at most 256 MiB of HBM per device.

```python
import math
import jax
import jax.numpy as jnp
from jax import lax

S = 54
SX = 4
NZ = 128
PCAP = 4096
NX = 256
NY = 128
NSLAB = 64
SLAB_PARCELS = 16384
PARCELS = 1048576


def draw_parcel_cells(key, part):
    key = jax.random.fold_in(key, 11)
    key_x, key_y, key_z = jax.random.split(key, 3)
    slots = jnp.arange(PARCELS, dtype=jnp.int32)
    slab_of = slots // SLAB_PARCELS
    base_x = slab_of * SX - 1 + jax.random.randint(key_x, (PARCELS,), 0, SX + 1, dtype=jnp.int32)
    base_x = jnp.clip(base_x, 0, NX - 2)
    base_y = jax.random.randint(key_y, (PARCELS,), 0, NY - 1, dtype=jnp.int32)
    base_z = jax.random.randint(key_z, (PARCELS,), 0, NZ - 1, dtype=jnp.int32)
    first_slot = slots == 0
    last_slot = slots == PARCELS - 1
    base_x = jnp.where(first_slot, 0, jnp.where(last_slot, NX - 2, base_x))
    base_y = jnp.where(first_slot, 0, jnp.where(last_slot, NY - 2, base_y))
    base_z = jnp.where(first_slot, 0, jnp.where(last_slot, NZ - 2, base_z))
    local_x = base_x - (slab_of * SX - 1)
    corner = jnp.arange(8, dtype=jnp.int32)
    offset_x = (corner // 4)[:, None]
    offset_y = (corner // 2 % 2)[:, None]
    offset_z = (corner % 2)[:, None]
    cells = (local_x[None] + offset_x) * (NY * NZ) + (base_y[None] + offset_y) * NZ + (base_z[None] + offset_z)
    return cells.astype(jnp.int32)


def draw_parcel_weights(key, part):
    key = jax.random.fold_in(key, 23)
    fractions = jax.random.uniform(key, (3, PARCELS), jnp.float32)
    corner = jnp.arange(8, dtype=jnp.int32)
    weights = jnp.ones((8, PARCELS), jnp.float32)
    for axis, step_bit in ((0, 4), (1, 2), (2, 1)):
        chosen = (corner // step_bit % 2 == 1)[:, None]
        weights = weights * jnp.where(chosen, fractions[axis][None], 1.0 - fractions[axis][None])
    return weights.astype(jnp.float32)


def draw_parcel_counts(key, part):
    key = jax.random.fold_in(key, 37)
    key_count, key_full = jax.random.split(key)
    counts = jax.random.randint(key_count, (NSLAB,), PCAP // 2, SLAB_PARCELS + 1, dtype=jnp.int32)
    full_slab = jax.random.randint(key_full, (), 0, NSLAB, dtype=jnp.int32)
    counts = jnp.where(jnp.arange(NSLAB, dtype=jnp.int32) == full_slab, SLAB_PARCELS, counts)
    return counts.astype(jnp.int32)


def shard_levels(own_key, shape, shards, low, high):
    level, own = 1.0, jax.random.fold_in(own_key, 6)
    for axis_at, parts in shards:
        steps = jnp.exp(jax.random.uniform(jax.random.fold_in(own, axis_at), (parts,), jnp.float32, low / len(shards), high / len(shards)))
        level = level * jnp.repeat(steps, shape[axis_at] // parts).reshape([-1 if axis == axis_at else 1 for axis in range(len(shape))])
    return level


def setup_inputs(seed: int = 0) -> dict:
    splits = jax.random.split(jax.random.key(seed), 12)
    return {
        "species": jnp.clip(0.4 * jax.random.uniform(splits[0], (S, NX, NY, NZ), jnp.float32) ** shard_levels(splits[0], (S, NX, NY, NZ), ((1, 64), (2, 4)), -0.2, 0.2), 0.0, 0.4),
        "diffusion": jnp.clip(jnp.exp(jax.random.uniform(splits[1], (S,), jnp.float32, math.log(0.01), math.log(0.1))), 0.01, 0.1),
        "gas_temp": jnp.clip(0.6 + 1.0 * jax.random.uniform(splits[2], (NX, NY, NZ), jnp.float32) ** shard_levels(splits[2], (NX, NY, NZ), ((0, 64), (1, 4)), -0.2, 0.2), 0.6, 1.6),
        "gas_density": jnp.clip(0.5 + 1.5 * jax.random.uniform(splits[3], (NX, NY, NZ), jnp.float32) ** shard_levels(splits[3], (NX, NY, NZ), ((0, 64), (1, 4)), -0.2, 0.2), 0.5, 2.0),
        "gas_velocity": jnp.clip(jax.random.uniform(splits[4], (3, NX, NY, NZ), jnp.float32, -1.0, 1.0) * shard_levels(splits[4], (3, NX, NY, NZ), ((1, 64), (2, 4)), -0.4, 0.0), -1.0, 1.0),
        "drop_radius": jnp.clip(jnp.exp(math.log(2.0) - 1.3862944 * jax.random.uniform(splits[5], (PARCELS,), jnp.float32) ** shard_levels(splits[5], (PARCELS,), ((0, 256),), -0.2, 0.2)), 0.5, 2.0),
        "drop_temp": jnp.clip(0.6 + 0.6 * jax.random.uniform(splits[6], (PARCELS,), jnp.float32) ** shard_levels(splits[6], (PARCELS,), ((0, 256),), -0.2, 0.2), 0.6, 1.2),
        "drop_velocity": jnp.clip(jax.random.uniform(splits[7], (3, PARCELS), jnp.float32, -2.0, 2.0) * shard_levels(splits[7], (3, PARCELS), ((1, 256),), -0.4, 0.0), -2.0, 2.0),
        "parcel_cells": draw_parcel_cells(jax.random.fold_in(splits[11], 71), 0),
        "parcel_weights": draw_parcel_weights(jax.random.fold_in(splits[11], 71), 0),
        "parcel_counts": draw_parcel_counts(jax.random.fold_in(splits[11], 71), 0),
    }


time_step = 0.05
evap_coef = 0.5
heat_coef = 0.15
latent_coef = 0.2
enthalpy_coef = 1.3
source_coef = 0.5
courant = 0.3


def parcel_physics(interp, radius, drop_temp, drop_velocity):
    gas_heat = interp[0]
    density = interp[1]
    gas_speed = interp[2:5]
    fuel_vapour = interp[5]
    slip = gas_speed - drop_velocity
    slip_square = jnp.sum(slip * slip, axis=0)
    reynolds = density * radius * slip_square
    sherwood = 2.0 + 0.6 * (1.0 + reynolds) ** 0.25
    surface_fuel = 0.5 * jax.nn.sigmoid(4.0 * (drop_temp - 1.0))
    evap_rate = evap_coef * radius * density * sherwood * jnp.log((1.0 - fuel_vapour) / (1.0 - surface_fuel))
    drop_mass = radius * radius * radius
    mass_ratio = 1.0 - time_step * evap_rate / drop_mass
    new_radius = radius * mass_ratio ** (1.0 / 3.0)
    relax_time = 2.0 * radius * radius / (1.0 + 0.15 * (1.0 + reynolds) ** 0.35)
    new_velocity = drop_velocity + (time_step / relax_time) * slip
    heat_rate = heat_coef * sherwood / (radius * radius)
    new_temp = drop_temp + time_step * (heat_rate * (gas_heat - drop_temp) - latent_coef * evap_rate / drop_mass)
    vapour_mass = time_step * evap_rate
    momentum = drop_mass * (drop_velocity - new_velocity) + vapour_mass * drop_velocity
    heat_gain = -time_step * drop_mass * heat_rate * (gas_heat - drop_temp)
    enthalpy = enthalpy_coef * vapour_mass * new_temp
    drag_work = jnp.sum(drop_mass * (drop_velocity - new_velocity) * gas_speed, axis=0)
    sources = jnp.concatenate([vapour_mass[None], momentum, heat_gain[None], enthalpy[None], drag_work[None]], axis=0)
    new_state = jnp.concatenate([new_radius[None], new_temp[None], new_velocity], axis=0)
    return new_state, sources


def shifted(padded, axis, offset):
    result = padded
    for which in (-3, -2, -1):
        extent = padded.shape[which]
        start_at = 2 + offset if which == axis else 2
        result = lax.slice_in_dim(result, start_at, start_at + extent - 4, axis=result.ndim + which)
    return result


def transport(padded, diffusion, speed_x, density, vapour_source, fuel_flag):
    center = shifted(padded, -1, 0)
    laplace = jnp.zeros_like(center)
    for axis in (-3, -2, -1):
        laplace = laplace + (-shifted(padded, axis, 2) + 16.0 * shifted(padded, axis, 1) - 30.0 * center
                             + 16.0 * shifted(padded, axis, -1) - shifted(padded, axis, -2)) / 12.0
    gradient = (-shifted(padded, -3, 2) + 8.0 * shifted(padded, -3, 1)
                - 8.0 * shifted(padded, -3, -1) + shifted(padded, -3, -2)) / 12.0
    return (center + diffusion * laplace - courant * speed_x * gradient
            + source_coef * vapour_source * (fuel_flag - center) / density)


def reference(species, diffusion, gas_temp, gas_density, gas_velocity, drop_radius, drop_temp, drop_velocity, parcel_cells, parcel_weights, parcel_counts):
    fields = jnp.concatenate([gas_temp[None], gas_density[None], gas_velocity, species[0:1]], axis=0).reshape(6, -1)
    slots = jnp.arange(PARCELS, dtype=jnp.int32)
    slab_of = (slots // SLAB_PARCELS).astype(jnp.int32)
    offsets = ((slab_of * SX - 1) * (NY * NZ)).astype(jnp.int32)
    global_cells = (parcel_cells + offsets[None]).astype(jnp.int32)
    flat_cells = global_cells.reshape(-1)
    corner_values = jnp.take(fields, flat_cells, axis=1).reshape(6, 8, -1)
    interp = jnp.sum(corner_values * parcel_weights[None], axis=1)
    live = (slots % SLAB_PARCELS) < parcel_counts[slab_of]
    new_state, sources = parcel_physics(interp, drop_radius, drop_temp, drop_velocity)
    old_state = jnp.concatenate([drop_radius[None], drop_temp[None], drop_velocity], axis=0)
    parcel_state = jnp.where(live[None], new_state, old_state)
    sources = jnp.where(live[None], sources, jnp.zeros_like(sources))
    terms = (parcel_weights[None] * sources[:, None, :]).reshape(7, -1)
    deposit = jnp.zeros((7, NX * NY * NZ), jnp.float32).at[:, flat_cells].add(terms)
    gas_sources = deposit.reshape(7, NX, NY, NZ)
    flags = (jnp.arange(S, dtype=jnp.int32) == 0).astype(jnp.float32)

    def one_species(item):
        field, coef, flag = item
        padded = jnp.pad(field, 2)
        return transport(padded, coef, gas_velocity[0], gas_density, gas_sources[0], flag)

    species_next = lax.map(one_species, (species, diffusion, flags))
    return species_next, gas_sources, parcel_state
```

```python
import jax
import jax.numpy as jnp
from jax import lax
from jax.experimental import pallas as pl
from jax.experimental.pallas import tpu as pltpu
from jax.sharding import PartitionSpec as P

time_step = 0.05
evap_coef = 0.5
heat_coef = 0.15
latent_coef = 0.2
enthalpy_coef = 1.3
source_coef = 0.5
courant = 0.3

LANES = 128
CHUNK = 512
PHYS = 1024
WINDOW = 256
YPAD = 40
F32 = jnp.float32
BF16 = jnp.bfloat16
NT = (((1,), (1,)), ((), ()))


def halves(value):
    high = value.astype(BF16)
    return high, (value - high.astype(F32)).astype(BF16)


def hat(index, start, fraction):
    away = index - start
    return jnp.where(away == 0.0, 1.0 - fraction, jnp.where(away == 1.0, fraction, 0.0))


def iota(shape, dim):
    return lax.broadcasted_iota(jnp.int32, shape, dim)


def one_hot(dst_row, aligned):
    rel = dst_row - aligned.astype(F32)
    return jnp.where(iota((WINDOW, LANES), 0).astype(F32) == rel, 1.0, 0.0).astype(BF16)


def physics(interp, radius, drop_temp, velocity):
    heat, density, speed, fuel = interp[0], interp[1], interp[2:5], interp[5]
    slip = [g - v for g, v in zip(speed, velocity)]
    slip_square = slip[0] * slip[0] + slip[1] * slip[1] + slip[2] * slip[2]
    log_flow = jnp.log(1.0 + density * radius * slip_square)
    sherwood = 2.0 + 0.6 * jnp.exp(0.25 * log_flow)
    surface = 0.5 / (1.0 + jnp.exp(-4.0 * (drop_temp - 1.0)))
    evap = evap_coef * radius * density * sherwood * jnp.log((1.0 - fuel) / (1.0 - surface))
    mass = radius * radius * radius
    ratio = 1.0 - time_step * evap / mass
    new_radius = radius * jnp.exp(jnp.log(ratio) * (1.0 / 3.0))
    rate = time_step * (1.0 + 0.15 * jnp.exp(0.35 * log_flow)) / (2.0 * radius * radius)
    change = [rate * s for s in slip]
    new_velocity = [v + c for v, c in zip(velocity, change)]
    heat_rate = heat_coef * sherwood / (radius * radius)
    new_temp = drop_temp + time_step * (
        heat_rate * (heat - drop_temp) - latent_coef * evap / mass
    )
    vapour = time_step * evap
    lost = [mass * (v - n) for v, n in zip(velocity, new_velocity)]
    momentum = [m + vapour * v for m, v in zip(lost, velocity)]
    heat_gain = -time_step * mass * heat_rate * (heat - drop_temp)
    enthalpy = enthalpy_coef * vapour * new_temp
    drag = lost[0] * speed[0] + lost[1] * speed[1] + lost[2] * speed[2]
    return [new_radius, new_temp] + new_velocity, [vapour] + momentum + [heat_gain, enthalpy, drag]


def parcel_kernel(
    info_ref,
    pk_ref,
    lo_ref,
    temp_ref,
    dens_ref,
    vel_ref,
    fuel_ref,
    hi_ref,
    yrow_ref,
    main_ref,
    dlo_ref,
    dhi_ref,
    dy_ref,
    state_ref,
    dst_ref,
    off_ref,
    cell_scr,
    off_smem,
    sem,
    pieces,
    cv,
    row_scr,
    ft,
    a_hi,
    a_lo,
    interp,
    src,
    dep,
):
    slots = pk_ref.shape[1]
    blocks = slots // LANES
    count, group = info_ref[0], info_ref[1]

    for b in range(blocks):
        cell_scr[b : b + 1, :] = pk_ref[8:9, b * LANES : (b + 1) * LANES]
    cell = cell_scr[...].astype(jnp.int32)
    slot = iota((blocks, LANES), 0) * LANES + iota((blocks, LANES), 1)
    mine = jnp.logical_and(slot < count, ((cell >> 12) & 3) == group)
    ones = jnp.where(mine, 1.0, 0.0).astype(BF16)
    before = jnp.where(iota((LANES, LANES), 0) < iota((LANES, LANES), 1), 1.0, 0.0).astype(BF16)
    after = jnp.where(iota((LANES, LANES), 1) < iota((LANES, LANES), 0), 1.0, 0.0).astype(BF16)
    full = jnp.ones((LANES, LANES), BF16)
    within = jnp.dot(ones, before, preferred_element_type=F32)
    row_sum = jnp.dot(ones, full, preferred_element_type=F32).astype(BF16)
    offset = jnp.dot(after, row_sum, preferred_element_type=F32)
    dst_ref[...] = jnp.where(mine, within + offset, -1.0)
    counts = lax.dot_general(jnp.ones((16, LANES), BF16), ones, NT, preferred_element_type=F32)
    counts = counts.astype(BF16)
    starts = jnp.dot(counts, before, preferred_element_type=F32)
    total = jnp.dot(counts, full, preferred_element_type=F32)
    first = iota((8, LANES), 0) == 0
    off_ref[...] = jnp.where(first, starts[0:8], total[0:8]).astype(jnp.int32)
    copy = pltpu.make_async_copy(off_ref, off_smem, sem)
    copy.start()

    def split(c, carry):
        at = pl.ds(pl.multiple_of(c * 2048, 2048), 2048)
        cells = jnp.broadcast_to(pk_ref[8:9, at], (8, 2048)).astype(jnp.int32)
        row = iota((8, 2048), 0)
        place = jnp.where(
            row == 0, cells >> 14, jnp.where(row == 1, (cells >> 7) & 31, cells & 127)
        ).astype(F32)
        high, low = halves(jnp.concatenate([pk_ref[0:8, at], place], axis=0))
        pieces[0:16, at] = high
        pieces[16:32, at] = low
        return carry

    lax.fori_loop(0, slots // 2048, split, 0)

    zero = jnp.zeros((256, LANES), F32)
    own = [temp_ref, dens_ref, vel_ref.at[0], vel_ref.at[1], vel_ref.at[2], fuel_ref.at[0]]
    planes = temp_ref.shape[0]
    rows = temp_ref.shape[1]
    for f in range(6):
        row_scr[...] = zero
        for x in range(planes + 2):
            if x == 0:
                block = lo_ref[f, 0]
            elif x == planes + 1:
                block = hi_ref[f, 0]
            else:
                block = own[f][x - 1]
            row_scr[x * YPAD : x * YPAD + rows, :] = block
            row_scr[x * YPAD + rows : x * YPAD + rows + 1, :] = yrow_ref[f, x]
        high, low = halves(row_scr[...].T)
        at = slice(f * LANES, (f + 1) * LANES)
        ft[at, 0:256] = high
        ft[at, 256:512] = low
        ft[at, 512:768] = high

    cv[...] = jnp.zeros(cv.shape, F32)
    state_ref[...] = jnp.zeros(state_ref.shape, F32)
    dep[...] = jnp.zeros(dep.shape, F32)
    copy.wait()
    live = off_smem[1, 0]

    def compact(i, carry):
        got = []
        for j in range(8):
            b = i * 8 + j
            aligned = (off_smem[0, b] >> 7) << 7
            hot = one_hot(dst_ref[pl.ds(b, 1), :], aligned)
            block = pieces[:, pl.ds(pl.multiple_of(b * LANES, LANES), LANES)]
            got.append((aligned, lax.dot_general(block, hot, NT, preferred_element_type=F32)))
        for aligned, both in got:
            at = pl.ds(pl.multiple_of(aligned, LANES), WINDOW)
            cv[:, at] += both[0:16] + both[16:32]
        return carry

    lax.fori_loop(0, blocks // 8, compact, 0)

    def gather(c, carry):
        at = pl.ds(pl.multiple_of(c * CHUNK, CHUNK), CHUNK)
        valid = c * CHUNK + iota((1, CHUNK), 1) < live
        fx, fy, fz = cv[0:1, at], cv[1:2, at], cv[2:3, at]
        x0, z0 = cv[8:9, at], cv[10:11, at]
        y0 = jnp.where(valid, cv[9:10, at], 1000.0)
        wy = hat(iota((YPAD, CHUNK), 0).astype(F32), y0, fy)
        parts = [wy * hat(float(x), x0, fx) for x in range(planes + 2)]
        parts.append(jnp.zeros((256 - (planes + 2) * YPAD, CHUNK), F32))
        high, low = halves(jnp.concatenate(parts, axis=0))
        a_hi[c] = high
        a_lo[c] = low
        stacked = jnp.concatenate([high, high, low], axis=0)
        lines = jnp.dot(ft[...], stacked, preferred_element_type=F32)
        wz = hat(iota((LANES, CHUNK), 0).astype(F32), z0, fz)
        for f in range(6):
            interp[f : f + 1, at] = jnp.sum(
                lines[f * LANES : (f + 1) * LANES] * wz, axis=0, keepdims=True
            )
        return carry

    chunks = (live + CHUNK - 1) // CHUNK
    lax.fori_loop(0, chunks, gather, 0)

    def step(c, carry):
        at = pl.ds(pl.multiple_of(c * PHYS, PHYS), PHYS)
        valid = c * PHYS + iota((1, PHYS), 1) < live
        inside = [jnp.where(valid, interp[f : f + 1, at], 0.0) for f in range(6)]
        radius = jnp.where(valid, cv[3:4, at], 1.0)
        velocity = [cv[d : d + 1, at] for d in (5, 6, 7)]
        new, sources = physics(inside, radius, cv[4:5, at], velocity)
        for s in range(5):
            state_ref[s : s + 1, at] = jnp.where(valid, new[s], 0.0)
        for k in range(7):
            src[k : k + 1, at] = jnp.where(valid, sources[k], 0.0)
        return carry

    lax.fori_loop(0, (live + PHYS - 1) // PHYS, step, 0)

    def deposit(c, carry):
        at = pl.ds(pl.multiple_of(c * CHUNK, CHUNK), CHUNK)
        wz = hat(iota((LANES, CHUNK), 0).astype(F32), cv[10:11, at], cv[2:3, at])
        high, low = halves(jnp.concatenate([wz * src[k : k + 1, at] for k in range(7)], axis=0))
        left = jnp.concatenate([high, low, high], axis=1)
        right = jnp.concatenate([a_hi[c], a_hi[c], a_lo[c]], axis=1)
        dep[...] += lax.dot_general(left, right, NT, preferred_element_type=F32)
        return carry

    lax.fori_loop(0, chunks, deposit, 0)

    for k in range(7):
        cells = dep[k * LANES : (k + 1) * LANES, :].T
        for x in range(planes + 2):
            block = cells[x * YPAD : x * YPAD + rows]
            if x == 0:
                dlo_ref[k, 0] = block
            elif x == planes + 1:
                dhi_ref[k, 0] = block
            else:
                main_ref[k, x - 1] = block
            dy_ref[k, x] = cells[x * YPAD + rows : x * YPAD + rows + 1]


def spread_kernel(off_ref, dst_ref, state_ref, out_ref, both_scr):
    high, low = halves(state_ref[...])
    both_scr[0:16, :] = jnp.concatenate([high, low], axis=0)

    def spread(i, carry):
        for j in range(8):
            b = i * 8 + j
            aligned = (off_ref[0, b] >> 7) << 7
            hot = one_hot(dst_ref[pl.ds(b, 1), :], aligned)
            block = both_scr[:, pl.ds(pl.multiple_of(aligned, LANES), WINDOW)]
            got = jnp.dot(block, hot, preferred_element_type=F32)
            out_ref[:, pl.ds(pl.multiple_of(b * LANES, LANES), LANES)] = got[0:8] + got[8:16]
        return carry

    lax.fori_loop(0, dst_ref.shape[0] // 8, spread, 0)


def species_kernel(
    diff_ref, y_ref, xlo_ref, xhi_ref, ylo_ref, yhi_ref, ux_ref, dens_ref, vap_ref, out_ref, pad
):
    species, planes, rows, depth = y_ref.shape
    at = iota((rows, depth), 1)
    left1 = jnp.where(at >= 1, 16.0, 0.0)
    left2 = jnp.where(at >= 2, -1.0, 0.0)
    right1 = jnp.where(at < depth - 1, 16.0, 0.0)
    right2 = jnp.where(at < depth - 2, -1.0, 0.0)
    first = pl.program_id(0) * species
    for x in range(planes):
        speed = ux_ref[x] * (courant / 12.0)
        gain = source_coef * vap_ref[x] / dens_ref[x]

        def one(s, carry):
            d12 = diff_ref[first + s] * (1.0 / 12.0)

            def plane(i):
                if i < 0:
                    return xlo_ref[s, i + 2]
                if i >= planes:
                    return xhi_ref[s, i - planes]
                return y_ref[s, i]

            center = plane(x)
            up1, up2, dn1, dn2 = plane(x + 1), plane(x + 2), plane(x - 1), plane(x - 2)
            pad[6:8, :] = ylo_ref[s, x]
            pad[8 : 8 + rows, :] = center
            pad[8 + rows : 10 + rows, :] = yhi_ref[s, x]
            near = up1 + dn1 + pad[7 : 7 + rows, :] + pad[9 : 9 + rows, :]
            far = up2 + dn2 + pad[6 : 6 + rows, :] + pad[10 : 10 + rows, :]
            along = (
                left1 * pltpu.roll(center, 1, 1)
                + right1 * pltpu.roll(center, depth - 1, 1)
                + left2 * pltpu.roll(center, 2, 1)
                + right2 * pltpu.roll(center, depth - 2, 1)
            )
            slope = 8.0 * (up1 - dn1) - (up2 - dn2)
            flag = jnp.where(first + s == 0, 1.0, 0.0)
            laplace = 16.0 * near - far + along - 90.0 * center
            out_ref[s, x] = center + d12 * laplace - speed * slope + gain * (flag - center)
            return carry

        lax.fori_loop(0, species, one, 0, unroll=True)


def per_device(
    species,
    diffusion,
    gas_temp,
    gas_density,
    gas_velocity,
    drop_radius,
    drop_temp,
    drop_velocity,
    parcel_cells,
    parcel_weights,
    parcel_counts,
):
    count_s = lax.axis_size("space")
    groups = lax.axis_size("group")
    planes, rows, depth = gas_temp.shape
    kinds = species.shape[0]
    capacity = drop_radius.shape[0]
    slots = capacity * groups
    blocks = slots // LANES
    ahead = [(i, i + 1) for i in range(count_s - 1)]
    back = [(b, a) for a, b in ahead]
    g_ahead = [(i, i + 1) for i in range(groups - 1)]
    g_back = [(b, a) for a, b in g_ahead]
    group = lax.axis_index("group")

    def upper(chosen):
        return sum(parcel_weights[c : c + 1] for c in chosen)

    packed = jnp.concatenate(
        [
            upper((4, 5, 6, 7)),
            upper((2, 3, 6, 7)),
            upper((1, 3, 5, 7)),
            drop_radius[None],
            drop_temp[None],
            drop_velocity,
            parcel_cells[0:1].astype(F32),
        ],
        axis=0,
    )
    parcels = lax.all_gather(packed, "group", axis=1, tiled=True)

    def rim(x):
        return jnp.concatenate(
            [gas_temp[None, x : x + 1], gas_density[None, x : x + 1], gas_velocity[:, x : x + 1],
             species[0:1, x : x + 1]],
            axis=0,
        )

    field_lo = lax.ppermute(rim(planes - 1), "space", ahead)
    field_hi = lax.ppermute(rim(0), "space", back)
    own_row = jnp.concatenate(
        [gas_temp[None, :, 0:1], gas_density[None, :, 0:1], gas_velocity[:, :, 0:1],
         species[0:1, :, 0:1]],
        axis=0,
    )
    row = jnp.concatenate([field_lo[:, :, 0:1], own_row, field_hi[:, :, 0:1]], axis=1)
    row = lax.ppermute(row, "group", g_back)

    x_lo = lax.ppermute(species[:, planes - 2 :], "space", ahead)
    x_hi = lax.ppermute(species[:, 0:2], "space", back)
    y_lo = lax.ppermute(species[:, :, rows - 2 :], "group", g_ahead)
    y_hi = lax.ppermute(species[:, :, 0:2], "group", g_back)

    info = jnp.stack([parcel_counts[0], group.astype(jnp.int32)])
    whole = lambda shape: pl.BlockSpec(shape, lambda i, n=len(shape): (0,) * n)
    smem = pl.BlockSpec(memory_space=pltpu.SMEM)
    reach = slots + WINDOW
    main, dep_lo, dep_hi, dep_y, state, dst, off = pl.pallas_call(
        parcel_kernel,
        grid=(1,),
        in_specs=[
            smem,
            whole((9, slots)),
            whole((6, 1, rows, depth)),
            whole((planes, rows, depth)),
            whole((planes, rows, depth)),
            whole((3, planes, rows, depth)),
            whole((1, planes, rows, depth)),
            whole((6, 1, rows, depth)),
            whole((6, planes + 2, 1, depth)),
        ],
        out_specs=[
            whole((7, planes, rows, depth)),
            whole((7, 1, rows, depth)),
            whole((7, 1, rows, depth)),
            whole((7, planes + 2, 1, depth)),
            whole((8, reach)),
            whole((blocks, LANES)),
            whole((8, LANES)),
        ],
        out_shape=[
            jax.ShapeDtypeStruct((7, planes, rows, depth), F32),
            jax.ShapeDtypeStruct((7, 1, rows, depth), F32),
            jax.ShapeDtypeStruct((7, 1, rows, depth), F32),
            jax.ShapeDtypeStruct((7, planes + 2, 1, depth), F32),
            jax.ShapeDtypeStruct((8, reach), F32),
            jax.ShapeDtypeStruct((blocks, LANES), F32),
            jax.ShapeDtypeStruct((8, LANES), jnp.int32),
        ],
        scratch_shapes=[
            pltpu.VMEM((blocks, LANES), F32),
            pltpu.SMEM((8, LANES), jnp.int32),
            pltpu.SemaphoreType.DMA,
            pltpu.VMEM((32, slots), BF16),
            pltpu.VMEM((16, reach), F32),
            pltpu.VMEM((256, LANES), F32),
            pltpu.VMEM((6 * LANES, 768), BF16),
            pltpu.VMEM((slots // CHUNK, 256, CHUNK), BF16),
            pltpu.VMEM((slots // CHUNK, 256, CHUNK), BF16),
            pltpu.VMEM((8, slots), F32),
            pltpu.VMEM((8, slots), F32),
            pltpu.VMEM((7 * LANES, 256), F32),
        ],
        compiler_params=pltpu.CompilerParams(vmem_limit_bytes=50 * 2**20),
        name="parcels",
    )(info, parcels, field_lo, gas_temp, gas_density, gas_velocity, species, field_hi, row)

    from_y = lax.ppermute(dep_y, "group", g_ahead)
    dep_lo = dep_lo.at[:, :, 0:1].add(from_y[:, 0:1])
    dep_hi = dep_hi.at[:, :, 0:1].add(from_y[:, planes + 1 :])
    from_below = lax.ppermute(dep_hi, "space", ahead)
    from_above = lax.ppermute(dep_lo, "space", back)
    gas_sources = main.at[:, :, 0:1].add(from_y[:, 1 : planes + 1])
    gas_sources = gas_sources.at[:, 0:1].add(from_below)
    gas_sources = gas_sources.at[:, planes - 1 :].add(from_above)

    spread = pl.pallas_call(
        spread_kernel,
        grid=(1,),
        in_specs=[smem, whole((blocks, LANES)), whole((8, reach))],
        out_specs=whole((8, slots)),
        out_shape=jax.ShapeDtypeStruct((8, slots), F32),
        scratch_shapes=[pltpu.VMEM((16, reach), BF16)],
        compiler_params=pltpu.CompilerParams(vmem_limit_bytes=24 * 2**20),
        name="spread",
    )(off, dst, state)

    def part(owner):
        return lax.dynamic_slice_in_dim(spread, owner * capacity, capacity, axis=1)

    new_state = part(group)
    for d in range(1, groups):
        route = [(i, (i + d) % groups) for i in range(groups)]
        new_state = new_state + lax.ppermute(part((group + d) % groups), "group", route)
    old_state = jnp.concatenate([drop_radius[None], drop_temp[None], drop_velocity], axis=0)
    slot = group * capacity + jnp.arange(capacity, dtype=jnp.int32)
    live = slot < parcel_counts[0]
    parcel_state = jnp.where(live[None], new_state[0:5], old_state)

    many = 6
    by_kind = lambda *shape: pl.BlockSpec((many,) + shape, lambda i: (i, 0, 0, 0))
    gas = pl.BlockSpec((planes, rows, depth), lambda i: (0, 0, 0))
    species_next = pl.pallas_call(
        species_kernel,
        grid=(kinds // many,),
        in_specs=[
            smem,
            by_kind(planes, rows, depth),
            by_kind(2, rows, depth),
            by_kind(2, rows, depth),
            by_kind(planes, 2, depth),
            by_kind(planes, 2, depth),
            pl.BlockSpec((None, planes, rows, depth), lambda i: (0, 0, 0, 0)),
            gas,
            pl.BlockSpec((None, planes, rows, depth), lambda i: (0, 0, 0, 0)),
        ],
        out_specs=by_kind(planes, rows, depth),
        out_shape=jax.ShapeDtypeStruct(species.shape, F32),
        scratch_shapes=[pltpu.VMEM((rows + 16, depth), F32)],
        compiler_params=pltpu.CompilerParams(vmem_limit_bytes=24 * 2**20),
        name="transport",
    )(diffusion, species, x_lo, x_hi, y_lo, y_hi, gas_velocity, gas_density, gas_sources)
    return (species_next, gas_sources, parcel_state)


def solution(mesh):
    in_specs = (
        P(None, "space", "group", None),
        P(),
        P("space", "group", None),
        P("space", "group", None),
        P(None, "space", "group", None),
        P(("space", "group")),
        P(("space", "group")),
        P(None, ("space", "group")),
        P(None, ("space", "group")),
        P(None, ("space", "group")),
        P("space"),
    )
    out_specs = (
        P(None, "space", "group", None),
        P(None, "space", "group", None),
        P(None, ("space", "group")),
    )
    return jax.shard_map(
        per_device, mesh=mesh, in_specs=in_specs, out_specs=out_specs, check_vma=False
    )
```

```python
import functools

import jax
import jax.numpy as jnp
from jax import lax
from jax.experimental import pallas as pl
from jax.experimental.pallas import tpu as pltpu
from jax.sharding import PartitionSpec as P

time_step = 0.05
evap_coef = 0.5
heat_coef = 0.15
latent_coef = 0.2
enthalpy_coef = 1.3
source_coef = 0.5
courant = 0.3

LANES = 128
PARTS = (54,)
MANY = 6
CHUNK = 512
PHYS = 1024
WINDOW = 256
YPAD = 40
F32 = jnp.float32
BF16 = jnp.bfloat16
NT = (((1,), (1,)), ((), ()))


def halves(value):
    high = value.astype(BF16)
    return high, (value - high.astype(F32)).astype(BF16)


def hat(index, start, fraction):
    away = index - start
    return jnp.where(away == 0.0, 1.0 - fraction, jnp.where(away == 1.0, fraction, 0.0))


def iota(shape, dim):
    return lax.broadcasted_iota(jnp.int32, shape, dim)


def one_hot(dst_row, aligned):
    rel = dst_row - aligned.astype(F32)
    return jnp.where(iota((WINDOW, LANES), 0).astype(F32) == rel, 1.0, 0.0).astype(BF16)


def physics(interp, radius, drop_temp, velocity):
    heat, density, speed, fuel = interp[0], interp[1], interp[2:5], interp[5]
    slip = [g - v for g, v in zip(speed, velocity)]
    slip_square = slip[0] * slip[0] + slip[1] * slip[1] + slip[2] * slip[2]
    log_flow = jnp.log(1.0 + density * radius * slip_square)
    sherwood = 2.0 + 0.6 * jnp.exp(0.25 * log_flow)
    surface = 0.5 / (1.0 + jnp.exp(-4.0 * (drop_temp - 1.0)))
    evap = evap_coef * radius * density * sherwood * jnp.log((1.0 - fuel) / (1.0 - surface))
    mass = radius * radius * radius
    ratio = 1.0 - time_step * evap / mass
    new_radius = radius * jnp.exp(jnp.log(ratio) * (1.0 / 3.0))
    rate = time_step * (1.0 + 0.15 * jnp.exp(0.35 * log_flow)) / (2.0 * radius * radius)
    change = [rate * s for s in slip]
    new_velocity = [v + c for v, c in zip(velocity, change)]
    heat_rate = heat_coef * sherwood / (radius * radius)
    new_temp = drop_temp + time_step * (
        heat_rate * (heat - drop_temp) - latent_coef * evap / mass
    )
    vapour = time_step * evap
    lost = [mass * (v - n) for v, n in zip(velocity, new_velocity)]
    momentum = [m + vapour * v for m, v in zip(lost, velocity)]
    heat_gain = -time_step * mass * heat_rate * (heat - drop_temp)
    enthalpy = enthalpy_coef * vapour * new_temp
    drag = lost[0] * speed[0] + lost[1] * speed[1] + lost[2] * speed[2]
    return [new_radius, new_temp] + new_velocity, [vapour] + momentum + [heat_gain, enthalpy, drag]


def parcel_kernel(
    info_ref,
    pk_ref,
    lo_ref,
    temp_ref,
    dens_ref,
    vel_ref,
    fuel_ref,
    hi_ref,
    ynext_ref,
    ylast_ref,
    main_ref,
    dlo_ref,
    dhi_ref,
    state_ref,
    own_dst_ref,
    off_ref,
    dst_ref,
    cell_scr,
    off_smem,
    sem,
    pieces,
    cv,
    row_scr,
    ft,
    a_hi,
    a_lo,
    interp,
    src,
    dep,
):
    slots = pk_ref.shape[1]
    blocks = slots // LANES
    count, group = info_ref[0], info_ref[1]

    for b in range(blocks):
        cell_scr[b : b + 1, :] = pk_ref[8:9, b * LANES : (b + 1) * LANES]
    cell = cell_scr[...].astype(jnp.int32)
    slot = iota((blocks, LANES), 0) * LANES + iota((blocks, LANES), 1)
    y_of = ((cell >> 7) & 127) - group * 32
    mine = jnp.logical_and(slot < count, jnp.logical_and(y_of >= -1, y_of < 32))
    ones = jnp.where(mine, 1.0, 0.0).astype(BF16)
    before = jnp.where(iota((LANES, LANES), 0) < iota((LANES, LANES), 1), 1.0, 0.0).astype(BF16)
    after = jnp.where(iota((LANES, LANES), 1) < iota((LANES, LANES), 0), 1.0, 0.0).astype(BF16)
    full = jnp.ones((LANES, LANES), BF16)
    within = jnp.dot(ones, before, preferred_element_type=F32)
    row_sum = jnp.dot(ones, full, preferred_element_type=F32).astype(BF16)
    offset = jnp.dot(after, row_sum, preferred_element_type=F32)
    dst = jnp.where(mine, within + offset, -1.0)
    dst_ref[...] = dst
    own_dst_ref[...] = jnp.where(y_of >= 0, dst, -1.0)
    counts = lax.dot_general(jnp.ones((16, LANES), BF16), ones, NT, preferred_element_type=F32)
    counts = counts.astype(BF16)
    starts = jnp.dot(counts, before, preferred_element_type=F32)
    total = jnp.dot(counts, full, preferred_element_type=F32)
    first = iota((8, LANES), 0) == 0
    off_ref[...] = jnp.where(first, starts[0:8], total[0:8]).astype(jnp.int32)
    copy = pltpu.make_async_copy(off_ref, off_smem, sem)
    copy.start()

    def split(c, carry):
        at = pl.ds(pl.multiple_of(c * 2048, 2048), 2048)
        cells = jnp.broadcast_to(pk_ref[8:9, at], (8, 2048)).astype(jnp.int32)
        row = iota((8, 2048), 0)
        place = jnp.where(
            row == 0, cells >> 14, jnp.where(row == 1, ((cells >> 7) & 127) - group * 32, cells & 127)
        ).astype(F32)
        high, low = halves(jnp.concatenate([pk_ref[0:8, at], place], axis=0))
        pieces[0:16, at] = high
        pieces[16:32, at] = low
        return carry

    lax.fori_loop(0, slots // 2048, split, 0)

    zero = jnp.zeros((256, LANES), F32)
    own = [temp_ref, dens_ref, vel_ref.at[0], vel_ref.at[1], vel_ref.at[2], fuel_ref.at[0]]
    planes = temp_ref.shape[0]
    rows = temp_ref.shape[1]
    for f in range(6):
        row_scr[...] = zero
        for x in range(planes + 2):
            if x == 0:
                block = lo_ref[f, 0]
            elif x == planes + 1:
                block = hi_ref[f, 0]
            else:
                block = own[f][x - 1]
            row_scr[x * YPAD : x * YPAD + rows, :] = block
            row_scr[x * YPAD + rows : x * YPAD + rows + 1, :] = ynext_ref[f, x]
            row_scr[(x + 1) * YPAD - 1 : (x + 1) * YPAD, :] = ylast_ref[f, x]
        high, low = halves(row_scr[...].T)
        at = slice(f * LANES, (f + 1) * LANES)
        ft[at, 0:256] = high
        ft[at, 256:512] = low
        ft[at, 512:768] = high

    cv[...] = jnp.zeros(cv.shape, F32)
    state_ref[...] = jnp.zeros(state_ref.shape, F32)
    dep[...] = jnp.zeros(dep.shape, F32)
    copy.wait()
    live = off_smem[1, 0]

    def compact(i, carry):
        got = []
        for j in range(8):
            b = i * 8 + j
            aligned = (off_smem[0, b] >> 7) << 7
            hot = one_hot(dst_ref[pl.ds(b, 1), :], aligned)
            block = pieces[:, pl.ds(pl.multiple_of(b * LANES, LANES), LANES)]
            got.append((aligned, lax.dot_general(block, hot, NT, preferred_element_type=F32)))
        for aligned, both in got:
            at = pl.ds(pl.multiple_of(aligned, LANES), WINDOW)
            cv[:, at] += both[0:16] + both[16:32]
        return carry

    lax.fori_loop(0, blocks // 8, compact, 0)

    def gather(c, carry):
        at = pl.ds(pl.multiple_of(c * CHUNK, CHUNK), CHUNK)
        valid = c * CHUNK + iota((1, CHUNK), 1) < live
        fx, fy, fz = cv[0:1, at], cv[1:2, at], cv[2:3, at]
        x0, z0 = cv[8:9, at], cv[10:11, at]
        y0 = jnp.where(valid, cv[9:10, at], 1000.0)
        line = iota((YPAD, CHUNK), 0)
        wy = hat(jnp.where(line == YPAD - 1, -1, line).astype(F32), y0, fy)
        parts = [wy * hat(float(x), x0, fx) for x in range(planes + 2)]
        parts.append(jnp.zeros((256 - (planes + 2) * YPAD, CHUNK), F32))
        high, low = halves(jnp.concatenate(parts, axis=0))
        a_hi[c] = high
        a_lo[c] = low
        stacked = jnp.concatenate([high, high, low], axis=0)
        lines = jnp.dot(ft[...], stacked, preferred_element_type=F32)
        wz = hat(iota((LANES, CHUNK), 0).astype(F32), z0, fz)
        for f in range(6):
            interp[f : f + 1, at] = jnp.sum(
                lines[f * LANES : (f + 1) * LANES] * wz, axis=0, keepdims=True
            )
        return carry

    chunks = (live + CHUNK - 1) // CHUNK
    lax.fori_loop(0, chunks, gather, 0)

    def step(c, carry):
        at = pl.ds(pl.multiple_of(c * PHYS, PHYS), PHYS)
        valid = c * PHYS + iota((1, PHYS), 1) < live
        inside = [jnp.where(valid, interp[f : f + 1, at], 0.0) for f in range(6)]
        radius = jnp.where(valid, cv[3:4, at], 1.0)
        velocity = [cv[d : d + 1, at] for d in (5, 6, 7)]
        new, sources = physics(inside, radius, cv[4:5, at], velocity)
        for s in range(5):
            state_ref[s : s + 1, at] = jnp.where(valid, new[s], 0.0)
        for k in range(7):
            src[k : k + 1, at] = jnp.where(valid, sources[k], 0.0)
        return carry

    lax.fori_loop(0, (live + PHYS - 1) // PHYS, step, 0)

    def deposit(c, carry):
        at = pl.ds(pl.multiple_of(c * CHUNK, CHUNK), CHUNK)
        wz = hat(iota((LANES, CHUNK), 0).astype(F32), cv[10:11, at], cv[2:3, at])
        high, low = halves(jnp.concatenate([wz * src[k : k + 1, at] for k in range(7)], axis=0))
        left = jnp.concatenate([high, low, high], axis=1)
        right = jnp.concatenate([a_hi[c], a_hi[c], a_lo[c]], axis=1)
        dep[...] += lax.dot_general(left, right, NT, preferred_element_type=F32)
        return carry

    lax.fori_loop(0, chunks, deposit, 0)

    for k in range(7):
        cells = dep[k * LANES : (k + 1) * LANES, :].T
        for x in range(planes + 2):
            block = cells[x * YPAD : x * YPAD + rows]
            if x == 0:
                dlo_ref[k, 0] = block
            elif x == planes + 1:
                dhi_ref[k, 0] = block
            else:
                main_ref[k, x - 1] = block


def spread_kernel(info_ref, off_ref, dst_ref, state_ref, *outs_and_scratch):
    outs, both_scr = outs_and_scratch[:-1], outs_and_scratch[-1]
    high, low = halves(state_ref[...])
    both_scr[0:16, :] = jnp.concatenate([high, low], axis=0)
    group = info_ref[1]
    each = dst_ref.shape[0] // len(outs)
    for d, out in enumerate(outs):
        owner = lax.rem(group + d, len(outs))

        def spread(i, carry):
            for j in range(8):
                b = owner * each + i * 8 + j
                aligned = (off_ref[0, b] >> 7) << 7
                hot = one_hot(dst_ref[pl.ds(b, 1), :], aligned)
                block = both_scr[:, pl.ds(pl.multiple_of(aligned, LANES), WINDOW)]
                got = jnp.dot(block, hot, preferred_element_type=F32)
                at = pl.ds(pl.multiple_of((i * 8 + j) * LANES, LANES), LANES)
                out[:, at] = got[0:8] + got[8:16]
            return carry

        lax.fori_loop(0, each // 8, spread, 0)


def prepare_kernel(
    cells_ref,
    weights_ref,
    radius_ref,
    temp_ref,
    velocity_ref,
    gas_temp_ref,
    dens_ref,
    vel_ref,
    fuel_ref,
    species_ref,
    packed_ref,
    top_ref,
    bottom_ref,
    *outs_and_sems,
):
    outs, sems = outs_and_sems[:-1], outs_and_sems[-1]
    planes = gas_temp_ref.shape[0]
    rows = gas_temp_ref.shape[1]
    copies = []

    def take(source, target):
        copies.append(pltpu.make_async_copy(source, target, sems.at[len(copies)]))
        copies[-1].start()

    at = 0
    for c, size in enumerate(PARTS):
        take(species_ref.at[at : at + size, planes - 2 : planes], outs[2 * c])
        take(species_ref.at[at : at + size, 0:2], outs[2 * c + 1])
        at += size
    take(species_ref.at[:, :, rows - 2 : rows], outs[2 * len(PARTS)])
    take(species_ref.at[:, :, 0:2], outs[2 * len(PARTS) + 1])
    w = [weights_ref[c : c + 1, :] for c in range(8)]
    packed_ref[0:1, :] = (w[4] + w[5]) + (w[6] + w[7])
    packed_ref[1:2, :] = (w[2] + w[3]) + (w[6] + w[7])
    packed_ref[2:3, :] = (w[1] + w[3]) + (w[5] + w[7])
    packed_ref[3:4, :] = radius_ref[...].reshape(1, -1)
    packed_ref[4:5, :] = temp_ref[...].reshape(1, -1)
    packed_ref[5:8, :] = velocity_ref[...]
    packed_ref[8:9, :] = cells_ref[0:1, :].astype(F32)
    own = [gas_temp_ref, dens_ref, vel_ref.at[0], vel_ref.at[1], vel_ref.at[2], fuel_ref.at[0]]
    for f in range(6):
        top_ref[f, 0] = own[f][planes - 1]
        bottom_ref[f, 0] = own[f][0]
    for copy in copies:
        copy.wait()


def transport_kernel(
    first_part,
    first_block,
    edge_ref,
    diff_ref,
    y_ref,
    xlo_ref,
    xhi_ref,
    ylo_ref,
    yhi_ref,
    ux_ref,
    dens_ref,
    *rest,
):
    if first_part:
        main_ref, below_ref, above_ref, out_ref, gas_ref, pad = rest

        @pl.when(pl.program_id(0) == 0)
        def _():
            last = main_ref.shape[1] - 1
            for k in range(main_ref.shape[0]):
                for x in range(last + 1):
                    total = main_ref[k, x]
                    if x == 0:
                        total = total + below_ref[k, 0]
                    if x == last:
                        total = total + above_ref[k, 0]
                    gas_ref[k, x] = total

        vap_ref = gas_ref.at[0]
    else:
        vap_ref, _, out_ref, pad = rest
    species, planes, rows, depth = y_ref.shape
    at = iota((rows, depth), 1)
    left1 = jnp.where(at >= 1, 16.0, 0.0)
    left2 = jnp.where(at >= 2, -1.0, 0.0)
    right1 = jnp.where(at < depth - 1, 16.0, 0.0)
    right2 = jnp.where(at < depth - 2, -1.0, 0.0)
    first = (first_block + pl.program_id(0)) * species
    for x in range(planes):
        speed = ux_ref[x] * (courant / 12.0)
        gain = source_coef * vap_ref[x] / dens_ref[x]

        def one(s, carry):
            d12 = diff_ref[first + s] * (1.0 / 12.0)

            def plane(i):
                if i < 0:
                    return xlo_ref[s, i + 2] * edge_ref[0]
                if i >= planes:
                    return xhi_ref[s, i - planes] * edge_ref[1]
                return y_ref[s, i]

            center = plane(x)
            up1, up2, dn1, dn2 = plane(x + 1), plane(x + 2), plane(x - 1), plane(x - 2)
            pad[6:8, :] = ylo_ref[s, x] * edge_ref[2]
            pad[8 : 8 + rows, :] = center
            pad[8 + rows : 10 + rows, :] = yhi_ref[s, x] * edge_ref[3]
            near = up1 + dn1 + pad[7 : 7 + rows, :] + pad[9 : 9 + rows, :]
            far = up2 + dn2 + pad[6 : 6 + rows, :] + pad[10 : 10 + rows, :]
            along = (
                left1 * pltpu.roll(center, 1, 1)
                + right1 * pltpu.roll(center, depth - 1, 1)
                + left2 * pltpu.roll(center, 2, 1)
                + right2 * pltpu.roll(center, depth - 2, 1)
            )
            slope = 8.0 * (up1 - dn1) - (up2 - dn2)
            flag = jnp.where(first + s == 0, 1.0, 0.0)
            laplace = 16.0 * near - far + along - 90.0 * center
            out_ref[s, x] = center + d12 * laplace - speed * slope + gain * (flag - center)
            return carry

        lax.fori_loop(0, species, one, 0, unroll=True)


def per_device(
    species,
    diffusion,
    gas_temp,
    gas_density,
    gas_velocity,
    drop_radius,
    drop_temp,
    drop_velocity,
    parcel_cells,
    parcel_weights,
    parcel_counts,
):
    count_s = lax.axis_size("space")
    groups = lax.axis_size("group")
    planes, rows, depth = gas_temp.shape
    kinds = species.shape[0]
    capacity = drop_radius.shape[0]
    slots = capacity * groups
    blocks = slots // LANES
    ahead = [(i, (i + 1) % count_s) for i in range(count_s)]
    back = [(b, a) for a, b in ahead]
    g_ahead = [(i, (i + 1) % groups) for i in range(groups)]
    g_back = [(b, a) for a, b in g_ahead]
    space, group = lax.axis_index("space"), lax.axis_index("group")
    info = jnp.stack([parcel_counts[0], group.astype(jnp.int32)])
    edge = jnp.stack([space > 0, space < count_s - 1, group > 0, group < groups - 1]).astype(F32)

    whole = lambda shape: pl.BlockSpec(shape, lambda i, n=len(shape): (0,) * n)
    smem = pl.BlockSpec(memory_space=pltpu.SMEM)
    hbm = pl.BlockSpec(memory_space=pl.ANY)
    shaped = lambda *shape: jax.ShapeDtypeStruct(shape, F32)
    limit = pltpu.CompilerParams(vmem_limit_bytes=62 * 2**20)

    sizes = [size for size in PARTS for _ in range(2)]
    prepared = pl.pallas_call(
        prepare_kernel,
        grid=(1,),
        in_specs=[
            whole((8, capacity)),
            whole((8, capacity)),
            whole((capacity,)),
            whole((capacity,)),
            whole((3, capacity)),
            whole((planes, rows, depth)),
            whole((planes, rows, depth)),
            whole((3, planes, rows, depth)),
            whole((1, planes, rows, depth)),
            hbm,
        ],
        out_specs=[whole((9, capacity)), whole((6, 1, rows, depth)), whole((6, 1, rows, depth))]
        + [hbm] * (len(sizes) + 2),
        out_shape=[shaped(9, capacity), shaped(6, 1, rows, depth), shaped(6, 1, rows, depth)]
        + [shaped(size, 2, rows, depth) for size in sizes]
        + [shaped(kinds, planes, 2, depth)] * 2,
        scratch_shapes=[pltpu.SemaphoreType.DMA((len(sizes) + 2,))],
        compiler_params=limit,
        name="prepare",
    )(
        parcel_cells, parcel_weights, drop_radius, drop_temp, drop_velocity,
        gas_temp, gas_density, gas_velocity, species, species,
    )
    packed, top, bottom = prepared[0:3]
    parcels = lax.all_gather(packed, "group", axis=1, tiled=True)
    field_lo = lax.ppermute(top, "space", ahead)
    field_hi = lax.ppermute(bottom, "space", back)

    def line(y):
        at = slice(y, y + 1)
        own = [gas_temp[None, :, at], gas_density[None, :, at], gas_velocity[:, :, at],
               species[0:1, :, at]]
        own = jnp.concatenate(own, axis=0)
        return jnp.concatenate([field_lo[:, :, at], own, field_hi[:, :, at]], axis=1)

    y_next = lax.ppermute(line(0), "group", g_back)
    y_last = lax.ppermute(line(rows - 1), "group", g_ahead)
    x_lo = [lax.ppermute(prepared[3 + 2 * c], "space", ahead) for c in range(len(PARTS))]
    x_hi = [lax.ppermute(prepared[4 + 2 * c], "space", back) for c in range(len(PARTS))]
    y_lo = lax.ppermute(prepared[-2], "group", g_ahead)
    y_hi = lax.ppermute(prepared[-1], "group", g_back)

    reach = slots + WINDOW
    main, dep_lo, dep_hi, state, dst, off = pl.pallas_call(
        parcel_kernel,
        grid=(1,),
        in_specs=[
            smem,
            whole((9, slots)),
            whole((6, 1, rows, depth)),
            whole((planes, rows, depth)),
            whole((planes, rows, depth)),
            whole((3, planes, rows, depth)),
            whole((1, planes, rows, depth)),
            whole((6, 1, rows, depth)),
            whole((6, planes + 2, 1, depth)),
            whole((6, planes + 2, 1, depth)),
        ],
        out_specs=[
            whole((7, planes, rows, depth)),
            whole((7, 1, rows, depth)),
            whole((7, 1, rows, depth)),
            whole((8, reach)),
            whole((blocks, LANES)),
            whole((8, LANES)),
        ],
        out_shape=[
            shaped(7, planes, rows, depth),
            shaped(7, 1, rows, depth),
            shaped(7, 1, rows, depth),
            shaped(8, reach),
            shaped(blocks, LANES),
            jax.ShapeDtypeStruct((8, LANES), jnp.int32),
        ],
        scratch_shapes=[
            pltpu.VMEM((blocks, LANES), F32),
            pltpu.VMEM((blocks, LANES), F32),
            pltpu.SMEM((8, LANES), jnp.int32),
            pltpu.SemaphoreType.DMA,
            pltpu.VMEM((32, slots), BF16),
            pltpu.VMEM((16, reach), F32),
            pltpu.VMEM((256, LANES), F32),
            pltpu.VMEM((6 * LANES, 768), BF16),
            pltpu.VMEM((slots // CHUNK, 256, CHUNK), BF16),
            pltpu.VMEM((slots // CHUNK, 256, CHUNK), BF16),
            pltpu.VMEM((8, slots), F32),
            pltpu.VMEM((8, slots), F32),
            pltpu.VMEM((7 * LANES, 256), F32),
        ],
        compiler_params=limit,
        name="parcels",
    )(info, parcels, field_lo, gas_temp, gas_density, gas_velocity, species, field_hi, y_next, y_last)

    from_below = lax.ppermute(dep_hi, "space", ahead)
    from_above = lax.ppermute(dep_lo, "space", back)

    spread = pl.pallas_call(
        spread_kernel,
        grid=(1,),
        in_specs=[smem, smem, whole((blocks, LANES)), whole((8, reach))],
        out_specs=[whole((8, capacity))] * groups,
        out_shape=[shaped(8, capacity)] * groups,
        scratch_shapes=[pltpu.VMEM((16, reach), BF16)],
        compiler_params=limit,
        name="spread",
    )(info, off, dst, state)
    new_state = spread[0]
    for d in range(1, groups):
        route = [(i, (i + d) % groups) for i in range(groups)]
        new_state = new_state + lax.ppermute(spread[d], "group", route)
    old_state = jnp.concatenate([drop_radius[None], drop_temp[None], drop_velocity], axis=0)
    slot = group * capacity + jnp.arange(capacity, dtype=jnp.int32)
    live = slot < parcel_counts[0]
    parcel_state = jnp.where(live[None], new_state[0:5], old_state)

    def by_kind(first, *shape):
        return pl.BlockSpec((MANY,) + shape, lambda i: (first + i, 0, 0, 0))

    gas = pl.BlockSpec((planes, rows, depth), lambda i: (0, 0, 0))
    row0 = pl.BlockSpec((None, planes, rows, depth), lambda i: (0, 0, 0, 0))
    all_gas = whole((7, planes, rows, depth))
    rim = whole((7, 1, rows, depth))
    species_next = gas_sources = None
    at = 0
    for c, size in enumerate(PARTS):
        first = at // MANY
        at += size
        out_specs = [by_kind(first, planes, rows, depth)]
        out_shape = [shaped(*species.shape)]
        if c == 0:
            extra, extra_specs = (main, from_below, from_above), [all_gas, rim, rim]
            out_specs.append(all_gas)
            out_shape.append(shaped(7, planes, rows, depth))
        else:
            extra, extra_specs = (gas_sources, species_next), [row0, hbm]
        got = pl.pallas_call(
            functools.partial(transport_kernel, c == 0, first),
            grid=(size // MANY,),
            in_specs=[
                smem,
                smem,
                by_kind(first, planes, rows, depth),
                by_kind(0, 2, rows, depth),
                by_kind(0, 2, rows, depth),
                by_kind(first, planes, 2, depth),
                by_kind(first, planes, 2, depth),
                row0,
                gas,
            ]
            + extra_specs,
            out_specs=out_specs,
            out_shape=out_shape,
            input_output_aliases={} if c == 0 else {10: 0},
            scratch_shapes=[pltpu.VMEM((rows + 16, depth), F32)],
            compiler_params=limit,
            name="transport",
        )(edge, diffusion, species, x_lo[c], x_hi[c], y_lo, y_hi, gas_velocity, gas_density, *extra)
        species_next = got[0]
        if c == 0:
            gas_sources = got[1]
    return (species_next, gas_sources, parcel_state)


def solution(mesh):
    in_specs = (
        P(None, "space", "group", None),
        P(),
        P("space", "group", None),
        P("space", "group", None),
        P(None, "space", "group", None),
        P(("space", "group")),
        P(("space", "group")),
        P(None, ("space", "group")),
        P(None, ("space", "group")),
        P(None, ("space", "group")),
        P("space"),
    )
    out_specs = (
        P(None, "space", "group", None),
        P(None, "space", "group", None),
        P(None, ("space", "group")),
    )
    return jax.shard_map(
        per_device, mesh=mesh, in_specs=in_specs, out_specs=out_specs, check_vma=False
    )
```

```python
import functools

import jax
import jax.numpy as jnp
from jax import lax
from jax.experimental import pallas as pl
from jax.experimental.pallas import tpu as pltpu
from jax.sharding import PartitionSpec as P

time_step = 0.05
evap_coef = 0.5
heat_coef = 0.15
latent_coef = 0.2
enthalpy_coef = 1.3
source_coef = 0.5
courant = 0.3

LANES = 128
PARTS = (54,)
MANY = 6
CHUNK = 512
PHYS = 1024
WINDOW = 256
YPAD = 40
F32 = jnp.float32
BF16 = jnp.bfloat16
NT = (((1,), (1,)), ((), ()))


def halves(value):
    high = value.astype(BF16)
    return high, (value - high.astype(F32)).astype(BF16)


def hat(index, start, fraction):
    away = index - start
    return jnp.where(away == 0.0, 1.0 - fraction, jnp.where(away == 1.0, fraction, 0.0))


def iota(shape, dim):
    return lax.broadcasted_iota(jnp.int32, shape, dim)


def one_hot(dst_row, aligned):
    rel = dst_row - aligned.astype(F32)
    return jnp.where(iota((WINDOW, LANES), 0).astype(F32) == rel, 1.0, 0.0).astype(BF16)


def physics(interp, radius, drop_temp, velocity):
    heat, density, speed, fuel = interp[0], interp[1], interp[2:5], interp[5]
    slip = [g - v for g, v in zip(speed, velocity)]
    slip_square = slip[0] * slip[0] + slip[1] * slip[1] + slip[2] * slip[2]
    log_flow = jnp.log(1.0 + density * radius * slip_square)
    sherwood = 2.0 + 0.6 * jnp.exp(0.25 * log_flow)
    surface = 0.5 / (1.0 + jnp.exp(-4.0 * (drop_temp - 1.0)))
    evap = evap_coef * radius * density * sherwood * jnp.log((1.0 - fuel) / (1.0 - surface))
    mass = radius * radius * radius
    ratio = 1.0 - time_step * evap / mass
    new_radius = radius * jnp.exp(jnp.log(ratio) * (1.0 / 3.0))
    rate = time_step * (1.0 + 0.15 * jnp.exp(0.35 * log_flow)) / (2.0 * radius * radius)
    change = [rate * s for s in slip]
    new_velocity = [v + c for v, c in zip(velocity, change)]
    heat_rate = heat_coef * sherwood / (radius * radius)
    new_temp = drop_temp + time_step * (
        heat_rate * (heat - drop_temp) - latent_coef * evap / mass
    )
    vapour = time_step * evap
    lost = [mass * (v - n) for v, n in zip(velocity, new_velocity)]
    momentum = [m + vapour * v for m, v in zip(lost, velocity)]
    heat_gain = -time_step * mass * heat_rate * (heat - drop_temp)
    enthalpy = enthalpy_coef * vapour * new_temp
    drag = lost[0] * speed[0] + lost[1] * speed[1] + lost[2] * speed[2]
    return [new_radius, new_temp] + new_velocity, [vapour] + momentum + [heat_gain, enthalpy, drag]


def parcel_kernel(
    info_ref,
    pk_ref,
    lo_ref,
    temp_ref,
    dens_ref,
    vel_ref,
    fuel_ref,
    hi_ref,
    ynext_ref,
    ylast_ref,
    main_ref,
    dlo_ref,
    dhi_ref,
    state_ref,
    own_dst_ref,
    off_ref,
    dst_ref,
    cell_scr,
    off_smem,
    sem,
    pieces,
    cv,
    row_scr,
    ft,
    a_hi,
    a_lo,
    interp,
    src,
    dep,
):
    groups = pk_ref.shape[0]
    each = pk_ref.shape[2] // 9
    capacity = each * 8
    slots = groups * capacity
    blocks = slots // LANES
    count, group = info_ref[0], info_ref[1]

    per_line = each // LANES
    for b in range(blocks):
        q, r = divmod(b, capacity // LANES)
        line, at = divmod(r, per_line)
        at = capacity + at * LANES
        cell_scr[b : b + 1, :] = pk_ref[q, line : line + 1, at : at + LANES]
    cell = cell_scr[...].astype(jnp.int32)
    slot = iota((blocks, LANES), 0) * LANES + iota((blocks, LANES), 1)
    y_of = ((cell >> 7) & 127) - group * 32
    mine = jnp.logical_and(slot < count, jnp.logical_and(y_of >= -1, y_of < 32))
    ones = jnp.where(mine, 1.0, 0.0).astype(BF16)
    before = jnp.where(iota((LANES, LANES), 0) < iota((LANES, LANES), 1), 1.0, 0.0).astype(BF16)
    after = jnp.where(iota((LANES, LANES), 1) < iota((LANES, LANES), 0), 1.0, 0.0).astype(BF16)
    full = jnp.ones((LANES, LANES), BF16)
    within = jnp.dot(ones, before, preferred_element_type=F32)
    row_sum = jnp.dot(ones, full, preferred_element_type=F32).astype(BF16)
    offset = jnp.dot(after, row_sum, preferred_element_type=F32)
    dst = jnp.where(mine, within + offset, -1.0)
    dst_ref[...] = dst
    own_dst_ref[...] = jnp.where(y_of >= 0, dst, -1.0)
    counts = lax.dot_general(jnp.ones((16, LANES), BF16), ones, NT, preferred_element_type=F32)
    counts = counts.astype(BF16)
    starts = jnp.dot(counts, before, preferred_element_type=F32)
    total = jnp.dot(counts, full, preferred_element_type=F32)
    first = iota((8, LANES), 0) == 0
    off_ref[...] = jnp.where(first, starts[0:8], total[0:8]).astype(jnp.int32)
    copy = pltpu.make_async_copy(off_ref, off_smem, sem)
    copy.start()

    def split(q, carry):
        for line in range(8):
            cells = pk_ref[q, line : line + 1, capacity : capacity + each]
            cells = jnp.broadcast_to(cells, (8, each)).astype(jnp.int32)
            row = iota((8, each), 0)
            y_place = ((cells >> 7) & 127) - group * 32
            place = jnp.where(row == 0, cells >> 14, jnp.where(row == 1, y_place, cells & 127))
            values = pk_ref[q, :, line * each : (line + 1) * each]
            high, low = halves(jnp.concatenate([values, place.astype(F32)], axis=0))
            at = pl.ds(pl.multiple_of(q * capacity + line * each, each), each)
            pieces[0:16, at] = high
            pieces[16:32, at] = low
        return carry

    lax.fori_loop(0, groups, split, 0)

    zero = jnp.zeros((256, LANES), F32)
    own = [temp_ref, dens_ref, vel_ref.at[0], vel_ref.at[1], vel_ref.at[2], fuel_ref.at[0]]
    planes = temp_ref.shape[0]
    rows = temp_ref.shape[1]
    for f in range(6):
        row_scr[...] = zero
        for x in range(planes + 2):
            if x == 0:
                block = lo_ref[f, 0]
            elif x == planes + 1:
                block = hi_ref[f, 0]
            else:
                block = own[f][x - 1]
            row_scr[x * YPAD : x * YPAD + rows, :] = block
            row_scr[x * YPAD + rows : x * YPAD + rows + 1, :] = ynext_ref[f, x]
            row_scr[(x + 1) * YPAD - 1 : (x + 1) * YPAD, :] = ylast_ref[f, x]
        high, low = halves(row_scr[...].T)
        at = slice(f * LANES, (f + 1) * LANES)
        ft[at, 0:256] = high
        ft[at, 256:512] = low
        ft[at, 512:768] = high

    cv[...] = jnp.zeros(cv.shape, F32)
    state_ref[...] = jnp.zeros(state_ref.shape, F32)
    dep[...] = jnp.zeros(dep.shape, F32)
    copy.wait()
    live = off_smem[1, 0]

    def compact(i, carry):
        got = []
        for j in range(8):
            b = i * 8 + j
            aligned = (off_smem[0, b] >> 7) << 7
            hot = one_hot(dst_ref[pl.ds(b, 1), :], aligned)
            block = pieces[:, pl.ds(pl.multiple_of(b * LANES, LANES), LANES)]
            got.append((aligned, lax.dot_general(block, hot, NT, preferred_element_type=F32)))
        for aligned, both in got:
            at = pl.ds(pl.multiple_of(aligned, LANES), WINDOW)
            cv[:, at] += both[0:16] + both[16:32]
        return carry

    lax.fori_loop(0, blocks // 8, compact, 0)

    def gather(c, carry):
        at = pl.ds(pl.multiple_of(c * CHUNK, CHUNK), CHUNK)
        valid = c * CHUNK + iota((1, CHUNK), 1) < live
        fx, fy, fz = cv[0:1, at], cv[1:2, at], cv[2:3, at]
        x0, z0 = cv[8:9, at], cv[10:11, at]
        y0 = jnp.where(valid, cv[9:10, at], 1000.0)
        line = iota((YPAD, CHUNK), 0)
        wy = hat(jnp.where(line == YPAD - 1, -1, line).astype(F32), y0, fy)
        parts = [wy * hat(float(x), x0, fx) for x in range(planes + 2)]
        parts.append(jnp.zeros((256 - (planes + 2) * YPAD, CHUNK), F32))
        high, low = halves(jnp.concatenate(parts, axis=0))
        a_hi[c] = high
        a_lo[c] = low
        stacked = jnp.concatenate([high, high, low], axis=0)
        lines = jnp.dot(ft[...], stacked, preferred_element_type=F32)
        wz = hat(iota((LANES, CHUNK), 0).astype(F32), z0, fz)
        for f in range(6):
            interp[f : f + 1, at] = jnp.sum(
                lines[f * LANES : (f + 1) * LANES] * wz, axis=0, keepdims=True
            )
        return carry

    chunks = (live + CHUNK - 1) // CHUNK
    lax.fori_loop(0, chunks, gather, 0)

    def step(c, carry):
        at = pl.ds(pl.multiple_of(c * PHYS, PHYS), PHYS)
        valid = c * PHYS + iota((1, PHYS), 1) < live
        inside = [jnp.where(valid, interp[f : f + 1, at], 0.0) for f in range(6)]
        radius = jnp.where(valid, cv[3:4, at], 1.0)
        velocity = [cv[d : d + 1, at] for d in (5, 6, 7)]
        new, sources = physics(inside, radius, cv[4:5, at], velocity)
        for s in range(5):
            state_ref[s : s + 1, at] = jnp.where(valid, new[s], 0.0)
        for k in range(7):
            src[k : k + 1, at] = jnp.where(valid, sources[k], 0.0)
        return carry

    lax.fori_loop(0, (live + PHYS - 1) // PHYS, step, 0)

    def deposit(c, carry):
        at = pl.ds(pl.multiple_of(c * CHUNK, CHUNK), CHUNK)
        wz = hat(iota((LANES, CHUNK), 0).astype(F32), cv[10:11, at], cv[2:3, at])
        high, low = halves(jnp.concatenate([wz * src[k : k + 1, at] for k in range(7)], axis=0))
        left = jnp.concatenate([high, low, high], axis=1)
        right = jnp.concatenate([a_hi[c], a_hi[c], a_lo[c]], axis=1)
        dep[...] += lax.dot_general(left, right, NT, preferred_element_type=F32)
        return carry

    lax.fori_loop(0, chunks, deposit, 0)

    for k in range(7):
        cells = dep[k * LANES : (k + 1) * LANES, :].T
        for x in range(planes + 2):
            block = cells[x * YPAD : x * YPAD + rows]
            if x == 0:
                dlo_ref[k, 0] = block
            elif x == planes + 1:
                dhi_ref[k, 0] = block
            else:
                main_ref[k, x - 1] = block


def spread_kernel(info_ref, off_ref, dst_ref, state_ref, *outs_and_scratch):
    outs, both_scr = outs_and_scratch[:-1], outs_and_scratch[-1]
    high, low = halves(state_ref[...])
    both_scr[0:16, :] = jnp.concatenate([high, low], axis=0)
    group = info_ref[1]
    each = dst_ref.shape[0] // len(outs)
    for d, out in enumerate(outs):
        owner = lax.rem(group + d, len(outs))

        def spread(i, carry):
            for j in range(8):
                b = owner * each + i * 8 + j
                aligned = (off_ref[0, b] >> 7) << 7
                hot = one_hot(dst_ref[pl.ds(b, 1), :], aligned)
                block = both_scr[:, pl.ds(pl.multiple_of(aligned, LANES), WINDOW)]
                got = jnp.dot(block, hot, preferred_element_type=F32)
                at = pl.ds(pl.multiple_of((i * 8 + j) * LANES, LANES), LANES)
                out[:, at] = got[0:8] + got[8:16]
            return carry

        lax.fori_loop(0, each // 8, spread, 0)


def prepare_kernel(
    cells_ref,
    weights_ref,
    radius_ref,
    temp_ref,
    velocity_ref,
    gas_temp_ref,
    dens_ref,
    vel_ref,
    species_ref,
    packed_ref,
    top_ref,
    bottom_ref,
    up_ref,
    down_ref,
    right_ref,
    left_ref,
):
    planes, rows = species_ref.shape[1:3]
    up_ref[...] = species_ref[:, planes - 2 : planes]
    down_ref[...] = species_ref[:, 0:2]
    right_ref[...] = species_ref[:, :, rows - 2 : rows]
    left_ref[...] = species_ref[:, :, 0:2]

    @pl.when(pl.program_id(0) == 0)
    def _():
        w = [weights_ref[c : c + 1, :] for c in range(8)]
        slots = cells_ref.shape[1]
        each = slots // 8
        packed_ref[0:1, 0:slots] = (w[4] + w[5]) + (w[6] + w[7])
        packed_ref[1:2, 0:slots] = (w[2] + w[3]) + (w[6] + w[7])
        packed_ref[2:3, 0:slots] = (w[1] + w[3]) + (w[5] + w[7])
        packed_ref[3:4, 0:slots] = radius_ref[...].reshape(1, -1)
        packed_ref[4:5, 0:slots] = temp_ref[...].reshape(1, -1)
        packed_ref[5:8, 0:slots] = velocity_ref[...]
        for i in range(8):
            first = cells_ref[0:1, i * each : (i + 1) * each]
            packed_ref[i : i + 1, slots : slots + each] = first.astype(F32)
        own = [gas_temp_ref, dens_ref, vel_ref.at[0], vel_ref.at[1], vel_ref.at[2],
               species_ref.at[0]]
        for f in range(6):
            top_ref[f, 0] = own[f][planes - 1]
            bottom_ref[f, 0] = own[f][0]


def transport_kernel(
    first_part,
    first_block,
    diff_ref,
    y_ref,
    xlo_ref,
    xhi_ref,
    ylo_ref,
    yhi_ref,
    ux_ref,
    dens_ref,
    *rest,
):
    if first_part:
        main_ref, below_ref, above_ref, out_ref, gas_ref, pad = rest

        @pl.when(pl.program_id(0) == 0)
        def _():
            last = main_ref.shape[1] - 1
            for k in range(main_ref.shape[0]):
                for x in range(last + 1):
                    total = main_ref[k, x]
                    if x == 0:
                        total = total + below_ref[k, 0]
                    if x == last:
                        total = total + above_ref[k, 0]
                    gas_ref[k, x] = total

        vap_ref = gas_ref.at[0]
    else:
        vap_ref, _, out_ref, pad = rest
    species, planes, rows, depth = y_ref.shape
    at = iota((rows, depth), 1)
    left1 = jnp.where(at >= 1, 16.0, 0.0)
    left2 = jnp.where(at >= 2, -1.0, 0.0)
    right1 = jnp.where(at < depth - 1, 16.0, 0.0)
    right2 = jnp.where(at < depth - 2, -1.0, 0.0)
    first = (first_block + pl.program_id(0)) * species
    for x in range(planes):
        speed = ux_ref[x] * (courant / 12.0)
        gain = source_coef * vap_ref[x] / dens_ref[x]

        for s in range(species):
            d12 = diff_ref[first + s] * (1.0 / 12.0)

            def plane(i, s=s):
                if i < 0:
                    return xlo_ref[s, i + 2]
                if i >= planes:
                    return xhi_ref[s, i - planes]
                return y_ref[s, i]

            center = plane(x)
            up1, up2, dn1, dn2 = plane(x + 1), plane(x + 2), plane(x - 1), plane(x - 2)
            pad[s, 6:8, :] = ylo_ref[s, x]
            pad[s, 8 : 8 + rows, :] = center
            pad[s, 8 + rows : 10 + rows, :] = yhi_ref[s, x]
            near = up1 + dn1 + pad[s, 7 : 7 + rows, :] + pad[s, 9 : 9 + rows, :]
            far = up2 + dn2 + pad[s, 6 : 6 + rows, :] + pad[s, 10 : 10 + rows, :]
            along = (
                left1 * pltpu.roll(center, 1, 1)
                + right1 * pltpu.roll(center, depth - 1, 1)
                + left2 * pltpu.roll(center, 2, 1)
                + right2 * pltpu.roll(center, depth - 2, 1)
            )
            slope = 8.0 * (up1 - dn1) - (up2 - dn2)
            flag = jnp.where(first + s == 0, 1.0, 0.0)
            laplace = 16.0 * near - far + along - 90.0 * center
            out_ref[s, x] = center + d12 * laplace - speed * slope + gain * (flag - center)


def per_device(
    species,
    diffusion,
    gas_temp,
    gas_density,
    gas_velocity,
    drop_radius,
    drop_temp,
    drop_velocity,
    parcel_cells,
    parcel_weights,
    parcel_counts,
):
    count_s = lax.axis_size("space")
    groups = lax.axis_size("group")
    planes, rows, depth = gas_temp.shape
    kinds = species.shape[0]
    capacity = drop_radius.shape[0]
    slots = capacity * groups
    blocks = slots // LANES
    ahead = [(i, i + 1) for i in range(count_s - 1)]
    back = [(b, a) for a, b in ahead]
    g_ahead = [(i, i + 1) for i in range(groups - 1)]
    g_back = [(b, a) for a, b in g_ahead]
    group = lax.axis_index("group")
    info = jnp.stack([parcel_counts[0], group.astype(jnp.int32)])

    whole = lambda shape: pl.BlockSpec(shape, lambda i, n=len(shape): (0,) * n)
    smem = pl.BlockSpec(memory_space=pltpu.SMEM)
    hbm = pl.BlockSpec(memory_space=pl.ANY)
    shaped = lambda *shape: jax.ShapeDtypeStruct(shape, F32)
    limit = pltpu.CompilerParams(vmem_limit_bytes=62 * 2**20)

    def by_kind(first, *shape):
        return pl.BlockSpec((MANY,) + shape, lambda i: (first + i, 0, 0, 0))

    packed, top, bottom, x_up, x_down, y_right, y_left = pl.pallas_call(
        prepare_kernel,
        grid=(kinds // MANY,),
        in_specs=[
            whole((8, capacity)),
            whole((8, capacity)),
            whole((capacity,)),
            whole((capacity,)),
            whole((3, capacity)),
            whole((planes, rows, depth)),
            whole((planes, rows, depth)),
            whole((3, planes, rows, depth)),
            by_kind(0, planes, rows, depth),
        ],
        out_specs=[
            whole((8, capacity // 8 * 9)),
            whole((6, 1, rows, depth)),
            whole((6, 1, rows, depth)),
            by_kind(0, 2, rows, depth),
            by_kind(0, 2, rows, depth),
            by_kind(0, planes, 2, depth),
            by_kind(0, planes, 2, depth),
        ],
        out_shape=[
            shaped(8, capacity // 8 * 9),
            shaped(6, 1, rows, depth),
            shaped(6, 1, rows, depth),
            shaped(kinds, 2, rows, depth),
            shaped(kinds, 2, rows, depth),
            shaped(kinds, planes, 2, depth),
            shaped(kinds, planes, 2, depth),
        ],
        compiler_params=limit,
        name="prepare",
    )(
        parcel_cells, parcel_weights, drop_radius, drop_temp, drop_velocity,
        gas_temp, gas_density, gas_velocity, species,
    )
    parcels = lax.all_gather(packed, "group", axis=0)
    field_lo = lax.ppermute(top, "space", ahead)
    field_hi = lax.ppermute(bottom, "space", back)

    def line(y):
        at = slice(y, y + 1)
        own = [gas_temp[None, :, at], gas_density[None, :, at], gas_velocity[:, :, at],
               species[0:1, :, at]]
        own = jnp.concatenate(own, axis=0)
        return jnp.concatenate([field_lo[:, :, at], own, field_hi[:, :, at]], axis=1)

    y_next = lax.ppermute(line(0), "group", g_back)
    y_last = lax.ppermute(line(rows - 1), "group", g_ahead)
    x_up, x_down, y_right, y_left, parcels = lax.optimization_barrier(
        (x_up, x_down, y_right, y_left, parcels)
    )
    x_lo = lax.ppermute(x_up, "space", ahead)
    x_hi = lax.ppermute(x_down, "space", back)
    y_lo = lax.ppermute(y_right, "group", g_ahead)
    y_hi = lax.ppermute(y_left, "group", g_back)

    reach = slots + WINDOW
    main, dep_lo, dep_hi, state, dst, off = pl.pallas_call(
        parcel_kernel,
        grid=(1,),
        in_specs=[
            smem,
            whole((groups, 8, capacity // 8 * 9)),
            whole((6, 1, rows, depth)),
            whole((planes, rows, depth)),
            whole((planes, rows, depth)),
            whole((3, planes, rows, depth)),
            whole((1, planes, rows, depth)),
            whole((6, 1, rows, depth)),
            whole((6, planes + 2, 1, depth)),
            whole((6, planes + 2, 1, depth)),
        ],
        out_specs=[
            whole((7, planes, rows, depth)),
            whole((7, 1, rows, depth)),
            whole((7, 1, rows, depth)),
            whole((8, reach)),
            whole((blocks, LANES)),
            whole((8, LANES)),
        ],
        out_shape=[
            shaped(7, planes, rows, depth),
            shaped(7, 1, rows, depth),
            shaped(7, 1, rows, depth),
            shaped(8, reach),
            shaped(blocks, LANES),
            jax.ShapeDtypeStruct((8, LANES), jnp.int32),
        ],
        scratch_shapes=[
            pltpu.VMEM((blocks, LANES), F32),
            pltpu.VMEM((blocks, LANES), F32),
            pltpu.SMEM((8, LANES), jnp.int32),
            pltpu.SemaphoreType.DMA,
            pltpu.VMEM((32, slots), BF16),
            pltpu.VMEM((16, reach), F32),
            pltpu.VMEM((256, LANES), F32),
            pltpu.VMEM((6 * LANES, 768), BF16),
            pltpu.VMEM((slots // CHUNK, 256, CHUNK), BF16),
            pltpu.VMEM((slots // CHUNK, 256, CHUNK), BF16),
            pltpu.VMEM((8, slots), F32),
            pltpu.VMEM((8, slots), F32),
            pltpu.VMEM((7 * LANES, 256), F32),
        ],
        compiler_params=limit,
        name="parcels",
    )(info, parcels, field_lo, gas_temp, gas_density, gas_velocity, species, field_hi, y_next, y_last)

    from_below = lax.ppermute(dep_hi, "space", ahead)
    from_above = lax.ppermute(dep_lo, "space", back)

    from_below, from_above, state = lax.optimization_barrier((from_below, from_above, state))
    spread = pl.pallas_call(
        spread_kernel,
        grid=(1,),
        in_specs=[smem, smem, whole((blocks, LANES)), whole((8, reach))],
        out_specs=[whole((8, capacity))] * groups,
        out_shape=[shaped(8, capacity)] * groups,
        scratch_shapes=[pltpu.VMEM((16, reach), BF16)],
        compiler_params=limit,
        name="spread",
    )(info, off, dst, state)
    new_state = spread[0]
    for d in range(1, groups):
        route = [(i, (i + d) % groups) for i in range(groups)]
        new_state = new_state + lax.ppermute(spread[d], "group", route)
    old_state = jnp.concatenate([drop_radius[None], drop_temp[None], drop_velocity], axis=0)
    slot = group * capacity + jnp.arange(capacity, dtype=jnp.int32)
    live = slot < parcel_counts[0]
    parcel_state = jnp.where(live[None], new_state[0:5], old_state)

    gas = pl.BlockSpec((planes, rows, depth), lambda i: (0, 0, 0))
    row0 = pl.BlockSpec((None, planes, rows, depth), lambda i: (0, 0, 0, 0))
    all_gas = whole((7, planes, rows, depth))
    rim = whole((7, 1, rows, depth))
    species_next = gas_sources = None
    at = 0
    for c, size in enumerate(PARTS):
        first = at // MANY
        at += size
        out_specs = [by_kind(first, planes, rows, depth)]
        out_shape = [shaped(*species.shape)]
        if c == 0:
            extra, extra_specs = (main, from_below, from_above), [all_gas, rim, rim]
            out_specs.append(all_gas)
            out_shape.append(shaped(7, planes, rows, depth))
        else:
            extra, extra_specs = (gas_sources, species_next), [row0, hbm]
        got = pl.pallas_call(
            functools.partial(transport_kernel, c == 0, first),
            grid=(size // MANY,),
            in_specs=[
                smem,
                by_kind(first, planes, rows, depth),
                by_kind(first, 2, rows, depth),
                by_kind(first, 2, rows, depth),
                by_kind(first, planes, 2, depth),
                by_kind(first, planes, 2, depth),
                row0,
                gas,
            ]
            + extra_specs,
            out_specs=out_specs,
            out_shape=out_shape,
            input_output_aliases={} if c == 0 else {9: 0},
            scratch_shapes=[pltpu.VMEM((MANY, rows + 16, depth), F32)],
            compiler_params=limit,
            name="transport",
        )(diffusion, species, x_lo, x_hi, y_lo, y_hi, gas_velocity, gas_density, *extra)
        species_next = got[0]
        if c == 0:
            gas_sources = got[1]
    return (species_next, gas_sources, parcel_state)


def solution(mesh):
    in_specs = (
        P(None, "space", "group", None),
        P(),
        P("space", "group", None),
        P("space", "group", None),
        P(None, "space", "group", None),
        P(("space", "group")),
        P(("space", "group")),
        P(None, ("space", "group")),
        P(None, ("space", "group")),
        P(None, ("space", "group")),
        P("space"),
    )
    out_specs = (
        P(None, "space", "group", None),
        P(None, "space", "group", None),
        P(None, ("space", "group")),
    )
    return jax.shard_map(
        per_device, mesh=mesh, in_specs=in_specs, out_specs=out_specs, check_vma=False
    )
```

```python
import functools

import jax
import jax.numpy as jnp
from jax import lax
from jax.experimental import pallas as pl
from jax.experimental.pallas import tpu as pltpu
from jax.sharding import PartitionSpec as P

time_step = 0.05
evap_coef = 0.5
heat_coef = 0.15
latent_coef = 0.2
enthalpy_coef = 1.3
source_coef = 0.5
courant = 0.3

LANES = 128
PARTS = (54,)
MANY = 18
CHUNK = 512
PHYS = 1024
WINDOW = 256
YPAD = 40
ROWS_WIDTH = 9 * LANES
F32 = jnp.float32
BF16 = jnp.bfloat16
NT = (((1,), (1,)), ((), ()))


def halves(value):
    high = value.astype(BF16)
    return high, (value - high.astype(F32)).astype(BF16)


def hat(index, start, fraction):
    away = index - start
    return jnp.where(away == 0.0, 1.0 - fraction, jnp.where(away == 1.0, fraction, 0.0))


def iota(shape, dim):
    return lax.broadcasted_iota(jnp.int32, shape, dim)


def one_hot(dst_row, aligned):
    rel = dst_row - aligned.astype(F32)
    return jnp.where(iota((WINDOW, LANES), 0).astype(F32) == rel, 1.0, 0.0).astype(BF16)


def cells_of(width):
    return (width - ROWS_WIDTH) // 9 * 8


def physics(interp, radius, drop_temp, velocity):
    heat, density, speed, fuel = interp[0], interp[1], interp[2:5], interp[5]
    slip = [g - v for g, v in zip(speed, velocity)]
    slip_square = slip[0] * slip[0] + slip[1] * slip[1] + slip[2] * slip[2]
    log_flow = jnp.log(1.0 + density * radius * slip_square)
    sherwood = 2.0 + 0.6 * jnp.exp(0.25 * log_flow)
    surface = 0.5 / (1.0 + jnp.exp(-4.0 * (drop_temp - 1.0)))
    evap = evap_coef * radius * density * sherwood * jnp.log((1.0 - fuel) / (1.0 - surface))
    mass = radius * radius * radius
    ratio = 1.0 - time_step * evap / mass
    new_radius = radius * jnp.exp(jnp.log(ratio) * (1.0 / 3.0))
    rate = time_step * (1.0 + 0.15 * jnp.exp(0.35 * log_flow)) / (2.0 * radius * radius)
    change = [rate * s for s in slip]
    new_velocity = [v + c for v, c in zip(velocity, change)]
    heat_rate = heat_coef * sherwood / (radius * radius)
    new_temp = drop_temp + time_step * (
        heat_rate * (heat - drop_temp) - latent_coef * evap / mass
    )
    vapour = time_step * evap
    lost = [mass * (v - n) for v, n in zip(velocity, new_velocity)]
    momentum = [m + vapour * v for m, v in zip(lost, velocity)]
    heat_gain = -time_step * mass * heat_rate * (heat - drop_temp)
    enthalpy = enthalpy_coef * vapour * new_temp
    drag = lost[0] * speed[0] + lost[1] * speed[1] + lost[2] * speed[2]
    return [new_radius, new_temp] + new_velocity, [vapour] + momentum + [heat_gain, enthalpy, drag]


def parcel_kernel(
    info_ref,
    pk_ref,
    lo_ref,
    temp_ref,
    dens_ref,
    vel_ref,
    fuel_ref,
    hi_ref,
    main_ref,
    dlo_ref,
    dhi_ref,
    state_ref,
    own_dst_ref,
    off_ref,
    dst_ref,
    cell_scr,
    off_smem,
    sem,
    pieces,
    cv,
    row_scr,
    ft,
    a_hi,
    a_lo,
    interp,
    src,
    dep,
):
    groups = pk_ref.shape[0]
    each = cells_of(pk_ref.shape[2]) // 8
    capacity = each * 8
    slots = groups * capacity
    blocks = slots // LANES
    count, group = info_ref[0], info_ref[1]

    per_line = each // LANES
    for b in range(blocks):
        q, r = divmod(b, capacity // LANES)
        line, at = divmod(r, per_line)
        at = capacity + at * LANES
        cell_scr[b : b + 1, :] = pk_ref[q, line : line + 1, at : at + LANES]
    cell = cell_scr[...].astype(jnp.int32)
    slot = iota((blocks, LANES), 0) * LANES + iota((blocks, LANES), 1)
    y_of = ((cell >> 7) & 127) - group * 32
    mine = jnp.logical_and(slot < count, jnp.logical_and(y_of >= -1, y_of < 32))
    ones = jnp.where(mine, 1.0, 0.0).astype(BF16)
    before = jnp.where(iota((LANES, LANES), 0) < iota((LANES, LANES), 1), 1.0, 0.0).astype(BF16)
    after = jnp.where(iota((LANES, LANES), 1) < iota((LANES, LANES), 0), 1.0, 0.0).astype(BF16)
    full = jnp.ones((LANES, LANES), BF16)
    within = jnp.dot(ones, before, preferred_element_type=F32)
    row_sum = jnp.dot(ones, full, preferred_element_type=F32).astype(BF16)
    offset = jnp.dot(after, row_sum, preferred_element_type=F32)
    dst = jnp.where(mine, within + offset, -1.0)
    dst_ref[...] = dst
    own_dst_ref[...] = jnp.where(y_of >= 0, dst, -1.0)
    counts = lax.dot_general(jnp.ones((16, LANES), BF16), ones, NT, preferred_element_type=F32)
    counts = counts.astype(BF16)
    starts = jnp.dot(counts, before, preferred_element_type=F32)
    total = jnp.dot(counts, full, preferred_element_type=F32)
    first = iota((8, LANES), 0) == 0
    off_ref[...] = jnp.where(first, starts[0:8], total[0:8]).astype(jnp.int32)
    copy = pltpu.make_async_copy(off_ref, off_smem, sem)
    copy.start()

    def split(q, carry):
        for line in range(8):
            cells = pk_ref[q, line : line + 1, capacity : capacity + each]
            cells = jnp.broadcast_to(cells, (8, each)).astype(jnp.int32)
            row = iota((8, each), 0)
            y_place = ((cells >> 7) & 127) - group * 32
            place = jnp.where(row == 0, cells >> 14, jnp.where(row == 1, y_place, cells & 127))
            values = pk_ref[q, :, line * each : (line + 1) * each]
            high, low = halves(jnp.concatenate([values, place.astype(F32)], axis=0))
            at = pl.ds(pl.multiple_of(q * capacity + line * each, each), each)
            pieces[0:16, at] = high
            pieces[16:32, at] = low
        return carry

    lax.fori_loop(0, groups, split, 0)

    zero = jnp.zeros((256, LANES), F32)
    own = [temp_ref, dens_ref, vel_ref.at[0], vel_ref.at[1], vel_ref.at[2], fuel_ref.at[0]]
    planes = temp_ref.shape[0]
    rows = temp_ref.shape[1]
    row_start = capacity + each
    after_me = jnp.minimum(group + 1, groups - 1)
    before_me = jnp.maximum(group - 1, 0)
    for f in range(6):
        row_scr[...] = zero
        for x in range(planes + 2):
            if x == 0:
                block = lo_ref[f, 0]
            elif x == planes + 1:
                block = hi_ref[f, 0]
            else:
                block = own[f][x - 1]
            row_scr[x * YPAD : x * YPAD + rows, :] = block
            block, line = row_place(planes, f, x, 0)
            at = row_start + block * LANES
            following = pk_ref[after_me, line : line + 1, at : at + LANES]
            row_scr[x * YPAD + rows : x * YPAD + rows + 1, :] = following
            block, line = row_place(planes, f, x, 1)
            at = row_start + block * LANES
            former = pk_ref[before_me, line : line + 1, at : at + LANES]
            row_scr[(x + 1) * YPAD - 1 : (x + 1) * YPAD, :] = former
        high, low = halves(row_scr[...].T)
        at = slice(f * LANES, (f + 1) * LANES)
        ft[at, 0:256] = high
        ft[at, 256:512] = low
        ft[at, 512:768] = high

    cv[...] = jnp.zeros(cv.shape, F32)
    state_ref[...] = jnp.zeros(state_ref.shape, F32)
    dep[...] = jnp.zeros(dep.shape, F32)
    copy.wait()
    live = off_smem[1, 0]

    def compact(i, carry):
        got = []
        for j in range(8):
            b = i * 8 + j
            aligned = (off_smem[0, b] >> 7) << 7
            hot = one_hot(dst_ref[pl.ds(b, 1), :], aligned)
            block = pieces[:, pl.ds(pl.multiple_of(b * LANES, LANES), LANES)]
            got.append((aligned, lax.dot_general(block, hot, NT, preferred_element_type=F32)))
        for aligned, both in got:
            at = pl.ds(pl.multiple_of(aligned, LANES), WINDOW)
            cv[:, at] += both[0:16] + both[16:32]
        return carry

    lax.fori_loop(0, blocks // 8, compact, 0)

    def gather(c, carry):
        at = pl.ds(pl.multiple_of(c * CHUNK, CHUNK), CHUNK)
        valid = c * CHUNK + iota((1, CHUNK), 1) < live
        fx, fy, fz = cv[0:1, at], cv[1:2, at], cv[2:3, at]
        x0, z0 = cv[8:9, at], cv[10:11, at]
        y0 = jnp.where(valid, cv[9:10, at], 1000.0)
        line = iota((YPAD, CHUNK), 0)
        wy = hat(jnp.where(line == YPAD - 1, -1, line).astype(F32), y0, fy)
        parts = [wy * hat(float(x), x0, fx) for x in range(planes + 2)]
        parts.append(jnp.zeros((256 - (planes + 2) * YPAD, CHUNK), F32))
        high, low = halves(jnp.concatenate(parts, axis=0))
        a_hi[c] = high
        a_lo[c] = low
        stacked = jnp.concatenate([high, high, low], axis=0)
        lines = jnp.dot(ft[...], stacked, preferred_element_type=F32)
        wz = hat(iota((LANES, CHUNK), 0).astype(F32), z0, fz)
        for f in range(6):
            interp[f : f + 1, at] = jnp.sum(
                lines[f * LANES : (f + 1) * LANES] * wz, axis=0, keepdims=True
            )
        return carry

    chunks = (live + CHUNK - 1) // CHUNK
    lax.fori_loop(0, chunks, gather, 0)

    def step(c, carry):
        at = pl.ds(pl.multiple_of(c * PHYS, PHYS), PHYS)
        valid = c * PHYS + iota((1, PHYS), 1) < live
        inside = [jnp.where(valid, interp[f : f + 1, at], 0.0) for f in range(6)]
        radius = jnp.where(valid, cv[3:4, at], 1.0)
        velocity = [cv[d : d + 1, at] for d in (5, 6, 7)]
        new, sources = physics(inside, radius, cv[4:5, at], velocity)
        for s in range(5):
            state_ref[s : s + 1, at] = jnp.where(valid, new[s], 0.0)
        for k in range(7):
            src[k : k + 1, at] = jnp.where(valid, sources[k], 0.0)
        return carry

    lax.fori_loop(0, (live + PHYS - 1) // PHYS, step, 0)

    def deposit(c, carry):
        at = pl.ds(pl.multiple_of(c * CHUNK, CHUNK), CHUNK)
        wz = hat(iota((LANES, CHUNK), 0).astype(F32), cv[10:11, at], cv[2:3, at])
        high, low = halves(jnp.concatenate([wz * src[k : k + 1, at] for k in range(7)], axis=0))
        left = jnp.concatenate([high, low, high], axis=1)
        right = jnp.concatenate([a_hi[c], a_hi[c], a_lo[c]], axis=1)
        dep[...] += lax.dot_general(left, right, NT, preferred_element_type=F32)
        return carry

    lax.fori_loop(0, chunks, deposit, 0)

    for k in range(7):
        cells = dep[k * LANES : (k + 1) * LANES, :].T
        for x in range(planes + 2):
            block = cells[x * YPAD : x * YPAD + rows]
            if x == 0:
                dlo_ref[k, 0] = block
            elif x == planes + 1:
                dhi_ref[k, 0] = block
            else:
                main_ref[k, x - 1] = block


def spread_kernel(info_ref, off_ref, dst_ref, state_ref, *outs_and_scratch):
    outs, both_scr = outs_and_scratch[:-1], outs_and_scratch[-1]
    high, low = halves(state_ref[...])
    both_scr[0:16, :] = jnp.concatenate([high, low], axis=0)
    group = info_ref[1]
    each = dst_ref.shape[0] // len(outs)
    for d, out in enumerate(outs):
        owner = lax.rem(group + d, len(outs))

        def spread(i, carry):
            for j in range(8):
                b = owner * each + i * 8 + j
                aligned = (off_ref[0, b] >> 7) << 7
                hot = one_hot(dst_ref[pl.ds(b, 1), :], aligned)
                block = both_scr[:, pl.ds(pl.multiple_of(aligned, LANES), WINDOW)]
                got = jnp.dot(block, hot, preferred_element_type=F32)
                at = pl.ds(pl.multiple_of((i * 8 + j) * LANES, LANES), LANES)
                out[:, at] = got[0:8] + got[8:16]
            return carry

        lax.fori_loop(0, each // 8, spread, 0)


def prepare_kernel(
    cells_ref,
    weights_ref,
    radius_ref,
    temp_ref,
    velocity_ref,
    gas_temp_ref,
    dens_ref,
    vel_ref,
    species_ref,
    packed_ref,
    top_ref,
    bottom_ref,
    up_ref,
    down_ref,
    right_ref,
    left_ref,
):
    planes, rows = species_ref.shape[1:3]
    up_ref[...] = species_ref[:, planes - 2 : planes]
    down_ref[...] = species_ref[:, 0:2]
    right_ref[...] = species_ref[:, :, rows - 2 : rows]
    left_ref[...] = species_ref[:, :, 0:2]

    @pl.when(pl.program_id(0) == 0)
    def _():
        w = [weights_ref[c : c + 1, :] for c in range(8)]
        slots = cells_ref.shape[1]
        each = slots // 8
        packed_ref[0:1, 0:slots] = (w[4] + w[5]) + (w[6] + w[7])
        packed_ref[1:2, 0:slots] = (w[2] + w[3]) + (w[6] + w[7])
        packed_ref[2:3, 0:slots] = (w[1] + w[3]) + (w[5] + w[7])
        packed_ref[3:4, 0:slots] = radius_ref[...].reshape(1, -1)
        packed_ref[4:5, 0:slots] = temp_ref[...].reshape(1, -1)
        packed_ref[5:8, 0:slots] = velocity_ref[...]
        for i in range(8):
            first = cells_ref[0:1, i * each : (i + 1) * each]
            packed_ref[i : i + 1, slots : slots + each] = first.astype(F32)
        own = [gas_temp_ref, dens_ref, vel_ref.at[0], vel_ref.at[1], vel_ref.at[2],
               species_ref.at[0]]
        for f in range(6):
            top_ref[f, 0] = own[f][planes - 1]
            bottom_ref[f, 0] = own[f][0]


def assemble_kernel(packed_ref, lo_ref, temp_ref, dens_ref, vel_ref, fuel_ref, hi_ref, out_ref):
    start = packed_ref.shape[1]
    out_ref[:, 0:start] = packed_ref[...]
    planes, rows = temp_ref.shape[0:2]
    own = [temp_ref, dens_ref, vel_ref.at[0], vel_ref.at[1], vel_ref.at[2], fuel_ref.at[0]]
    for f in range(6):
        for x in range(planes + 2):
            if x == 0:
                plane = lo_ref.at[f, 0]
            elif x == planes + 1:
                plane = hi_ref.at[f, 0]
            else:
                plane = own[f].at[x - 1]
            for side, y in enumerate((0, rows - 1)):
                block, line = row_place(planes, f, x, side)
                at = start + block * LANES
                out_ref[line : line + 1, at : at + LANES] = plane[y : y + 1, :]


def row_place(planes, f, x, side):
    return divmod((f * (planes + 2) + x) * 2 + side, 8)


def transport_kernel(
    first_part,
    first_block,
    diff_ref,
    y_ref,
    xlo_ref,
    xhi_ref,
    ylo_ref,
    yhi_ref,
    ux_ref,
    dens_ref,
    *rest,
):
    if first_part:
        main_ref, below_ref, above_ref, out_ref, gas_ref, pad = rest

        @pl.when(pl.program_id(0) == 0)
        def _():
            last = main_ref.shape[1] - 1
            for k in range(main_ref.shape[0]):
                for x in range(last + 1):
                    total = main_ref[k, x]
                    if x == 0:
                        total = total + below_ref[k, 0]
                    if x == last:
                        total = total + above_ref[k, 0]
                    gas_ref[k, x] = total

        vap_ref = gas_ref.at[0]
    else:
        vap_ref, _, out_ref, pad = rest
    species, planes, rows, depth = y_ref.shape
    at = iota((rows, depth), 1)
    left1 = jnp.where(at >= 1, 16.0, 0.0)
    left2 = jnp.where(at >= 2, -1.0, 0.0)
    right1 = jnp.where(at < depth - 1, 16.0, 0.0)
    right2 = jnp.where(at < depth - 2, -1.0, 0.0)
    first = (first_block + pl.program_id(0)) * species
    for x in range(planes):
        speed = ux_ref[x] * (courant / 12.0)
        gain = source_coef * vap_ref[x] / dens_ref[x]

        for s in range(species):
            d12 = diff_ref[first + s] * (1.0 / 12.0)

            def plane(i, s=s):
                if i < 0:
                    return xlo_ref[s, i + 2]
                if i >= planes:
                    return xhi_ref[s, i - planes]
                return y_ref[s, i]

            center = plane(x)
            up1, up2, dn1, dn2 = plane(x + 1), plane(x + 2), plane(x - 1), plane(x - 2)
            pad[s, 6:8, :] = ylo_ref[s, x]
            pad[s, 8 : 8 + rows, :] = center
            pad[s, 8 + rows : 10 + rows, :] = yhi_ref[s, x]
            near = up1 + dn1 + pad[s, 7 : 7 + rows, :] + pad[s, 9 : 9 + rows, :]
            far = up2 + dn2 + pad[s, 6 : 6 + rows, :] + pad[s, 10 : 10 + rows, :]
            along = (
                left1 * pltpu.roll(center, 1, 1)
                + right1 * pltpu.roll(center, depth - 1, 1)
                + left2 * pltpu.roll(center, 2, 1)
                + right2 * pltpu.roll(center, depth - 2, 1)
            )
            slope = 8.0 * (up1 - dn1) - (up2 - dn2)
            flag = jnp.where(first + s == 0, 1.0, 0.0)
            laplace = 16.0 * near - far + along - 90.0 * center
            out_ref[s, x] = center + d12 * laplace - speed * slope + gain * (flag - center)


def per_device(
    species,
    diffusion,
    gas_temp,
    gas_density,
    gas_velocity,
    drop_radius,
    drop_temp,
    drop_velocity,
    parcel_cells,
    parcel_weights,
    parcel_counts,
):
    count_s = lax.axis_size("space")
    groups = lax.axis_size("group")
    planes, rows, depth = gas_temp.shape
    kinds = species.shape[0]
    capacity = drop_radius.shape[0]
    slots = capacity * groups
    blocks = slots // LANES
    ahead = [(i, i + 1) for i in range(count_s - 1)]
    back = [(b, a) for a, b in ahead]
    g_ahead = [(i, i + 1) for i in range(groups - 1)]
    g_back = [(b, a) for a, b in g_ahead]
    group = lax.axis_index("group")
    info = jnp.stack([parcel_counts[0], group.astype(jnp.int32)])

    whole = lambda shape: pl.BlockSpec(shape, lambda i, n=len(shape): (0,) * n)
    smem = pl.BlockSpec(memory_space=pltpu.SMEM)
    hbm = pl.BlockSpec(memory_space=pl.ANY)
    shaped = lambda *shape: jax.ShapeDtypeStruct(shape, F32)
    limit = pltpu.CompilerParams(vmem_limit_bytes=62 * 2**20)

    def by_kind(first, *shape):
        return pl.BlockSpec((MANY,) + shape, lambda i: (first + i, 0, 0, 0))

    packed, top, bottom, x_up, x_down, y_right, y_left = pl.pallas_call(
        prepare_kernel,
        grid=(kinds // MANY,),
        in_specs=[
            whole((8, capacity)),
            whole((8, capacity)),
            whole((capacity,)),
            whole((capacity,)),
            whole((3, capacity)),
            whole((planes, rows, depth)),
            whole((planes, rows, depth)),
            whole((3, planes, rows, depth)),
            by_kind(0, planes, rows, depth),
        ],
        out_specs=[
            whole((8, capacity // 8 * 9)),
            whole((6, 1, rows, depth)),
            whole((6, 1, rows, depth)),
            by_kind(0, 2, rows, depth),
            by_kind(0, 2, rows, depth),
            by_kind(0, planes, 2, depth),
            by_kind(0, planes, 2, depth),
        ],
        out_shape=[
            shaped(8, capacity // 8 * 9),
            shaped(6, 1, rows, depth),
            shaped(6, 1, rows, depth),
            shaped(kinds, 2, rows, depth),
            shaped(kinds, 2, rows, depth),
            shaped(kinds, planes, 2, depth),
            shaped(kinds, planes, 2, depth),
        ],
        compiler_params=limit,
        name="prepare",
    )(
        parcel_cells, parcel_weights, drop_radius, drop_temp, drop_velocity,
        gas_temp, gas_density, gas_velocity, species,
    )
    field_lo = lax.ppermute(top, "space", ahead)
    field_hi = lax.ppermute(bottom, "space", back)
    width = capacity // 8 * 9 + ROWS_WIDTH
    sent = pl.pallas_call(
        assemble_kernel,
        grid=(1,),
        in_specs=[
            whole((8, capacity // 8 * 9)),
            whole((6, 1, rows, depth)),
            whole((planes, rows, depth)),
            whole((planes, rows, depth)),
            whole((3, planes, rows, depth)),
            whole((1, planes, rows, depth)),
            whole((6, 1, rows, depth)),
        ],
        out_specs=whole((8, width)),
        out_shape=shaped(8, width),
        compiler_params=limit,
        name="assemble",
    )(packed, field_lo, gas_temp, gas_density, gas_velocity, species, field_hi)
    parcels = lax.all_gather(sent, "group", axis=0)

    x_up, x_down, y_right, y_left, parcels = lax.optimization_barrier(
        (x_up, x_down, y_right, y_left, parcels)
    )
    x_lo = lax.ppermute(x_up, "space", ahead)
    x_hi = lax.ppermute(x_down, "space", back)
    y_lo = lax.ppermute(y_right, "group", g_ahead)
    y_hi = lax.ppermute(y_left, "group", g_back)

    reach = slots + WINDOW
    main, dep_lo, dep_hi, state, dst, off = pl.pallas_call(
        parcel_kernel,
        grid=(1,),
        in_specs=[
            smem,
            whole((groups, 8, width)),
            whole((6, 1, rows, depth)),
            whole((planes, rows, depth)),
            whole((planes, rows, depth)),
            whole((3, planes, rows, depth)),
            whole((1, planes, rows, depth)),
            whole((6, 1, rows, depth)),
        ],
        out_specs=[
            whole((7, planes, rows, depth)),
            whole((7, 1, rows, depth)),
            whole((7, 1, rows, depth)),
            whole((8, reach)),
            whole((blocks, LANES)),
            whole((8, LANES)),
        ],
        out_shape=[
            shaped(7, planes, rows, depth),
            shaped(7, 1, rows, depth),
            shaped(7, 1, rows, depth),
            shaped(8, reach),
            shaped(blocks, LANES),
            jax.ShapeDtypeStruct((8, LANES), jnp.int32),
        ],
        scratch_shapes=[
            pltpu.VMEM((blocks, LANES), F32),
            pltpu.VMEM((blocks, LANES), F32),
            pltpu.SMEM((8, LANES), jnp.int32),
            pltpu.SemaphoreType.DMA,
            pltpu.VMEM((32, slots), BF16),
            pltpu.VMEM((16, reach), F32),
            pltpu.VMEM((256, LANES), F32),
            pltpu.VMEM((6 * LANES, 768), BF16),
            pltpu.VMEM((slots // CHUNK, 256, CHUNK), BF16),
            pltpu.VMEM((slots // CHUNK, 256, CHUNK), BF16),
            pltpu.VMEM((8, slots), F32),
            pltpu.VMEM((8, slots), F32),
            pltpu.VMEM((7 * LANES, 256), F32),
        ],
        compiler_params=limit,
        name="parcels",
    )(info, parcels, field_lo, gas_temp, gas_density, gas_velocity, species, field_hi)

    from_below = lax.ppermute(dep_hi, "space", ahead)
    from_above = lax.ppermute(dep_lo, "space", back)

    from_below, from_above, state = lax.optimization_barrier((from_below, from_above, state))
    spread = pl.pallas_call(
        spread_kernel,
        grid=(1,),
        in_specs=[smem, smem, whole((blocks, LANES)), whole((8, reach))],
        out_specs=[whole((8, capacity))] * groups,
        out_shape=[shaped(8, capacity)] * groups,
        scratch_shapes=[pltpu.VMEM((16, reach), BF16)],
        compiler_params=limit,
        name="spread",
    )(info, off, dst, state)
    new_state = spread[0]
    for d in range(1, groups):
        route = [(i, (i + d) % groups) for i in range(groups)]
        new_state = new_state + lax.ppermute(spread[d], "group", route)
    old_state = jnp.concatenate([drop_radius[None], drop_temp[None], drop_velocity], axis=0)
    slot = group * capacity + jnp.arange(capacity, dtype=jnp.int32)
    live = slot < parcel_counts[0]
    parcel_state = jnp.where(live[None], new_state[0:5], old_state)

    gas = pl.BlockSpec((planes, rows, depth), lambda i: (0, 0, 0))
    row0 = pl.BlockSpec((None, planes, rows, depth), lambda i: (0, 0, 0, 0))
    all_gas = whole((7, planes, rows, depth))
    rim = whole((7, 1, rows, depth))
    species_next = gas_sources = None
    at = 0
    for c, size in enumerate(PARTS):
        first = at // MANY
        at += size
        out_specs = [by_kind(first, planes, rows, depth)]
        out_shape = [shaped(*species.shape)]
        if c == 0:
            extra, extra_specs = (main, from_below, from_above), [all_gas, rim, rim]
            out_specs.append(all_gas)
            out_shape.append(shaped(7, planes, rows, depth))
        else:
            extra, extra_specs = (gas_sources, species_next), [row0, hbm]
        got = pl.pallas_call(
            functools.partial(transport_kernel, c == 0, first),
            grid=(size // MANY,),
            in_specs=[
                smem,
                by_kind(first, planes, rows, depth),
                by_kind(first, 2, rows, depth),
                by_kind(first, 2, rows, depth),
                by_kind(first, planes, 2, depth),
                by_kind(first, planes, 2, depth),
                row0,
                gas,
            ]
            + extra_specs,
            out_specs=out_specs,
            out_shape=out_shape,
            input_output_aliases={} if c == 0 else {9: 0},
            scratch_shapes=[pltpu.VMEM((MANY, rows + 16, depth), F32)],
            compiler_params=limit,
            name="transport",
        )(diffusion, species, x_lo, x_hi, y_lo, y_hi, gas_velocity, gas_density, *extra)
        species_next = got[0]
        if c == 0:
            gas_sources = got[1]
    return (species_next, gas_sources, parcel_state)


def solution(mesh):
    in_specs = (
        P(None, "space", "group", None),
        P(),
        P("space", "group", None),
        P("space", "group", None),
        P(None, "space", "group", None),
        P(("space", "group")),
        P(("space", "group")),
        P(None, ("space", "group")),
        P(None, ("space", "group")),
        P(None, ("space", "group")),
        P("space"),
    )
    out_specs = (
        P(None, "space", "group", None),
        P(None, "space", "group", None),
        P(None, ("space", "group")),
    )
    return jax.shard_map(
        per_device, mesh=mesh, in_specs=in_specs, out_specs=out_specs, check_vma=False
    )
```

```python
import functools

import jax
import jax.numpy as jnp
from jax import lax
from jax.experimental import pallas as pl
from jax.experimental.pallas import tpu as pltpu
from jax.sharding import PartitionSpec as P

time_step = 0.05
evap_coef = 0.5
heat_coef = 0.15
latent_coef = 0.2
enthalpy_coef = 1.3
source_coef = 0.5
courant = 0.3

LANES = 128
PARTS = (54,)
MANY = 18
CHUNK = 1024
PHYS = 1024
WINDOW = 256
YPAD = 40
ROWS_WIDTH = 9 * LANES
F32 = jnp.float32
BF16 = jnp.bfloat16
NT = (((1,), (1,)), ((), ()))


def halves(value):
    high = value.astype(BF16)
    return high, (value - high.astype(F32)).astype(BF16)


def hat(index, start, fraction):
    away = index - start
    return jnp.where(away == 0.0, 1.0 - fraction, jnp.where(away == 1.0, fraction, 0.0))


def iota(shape, dim):
    return lax.broadcasted_iota(jnp.int32, shape, dim)


def one_hot(dst_row, aligned):
    rel = dst_row - aligned.astype(F32)
    return jnp.where(iota((WINDOW, LANES), 0).astype(F32) == rel, 1.0, 0.0).astype(BF16)


def cells_of(width):
    return (width - ROWS_WIDTH) // 9 * 8


def physics(interp, radius, drop_temp, velocity):
    heat, density, speed, fuel = interp[0], interp[1], interp[2:5], interp[5]
    slip = [g - v for g, v in zip(speed, velocity)]
    slip_square = slip[0] * slip[0] + slip[1] * slip[1] + slip[2] * slip[2]
    log_flow = jnp.log(1.0 + density * radius * slip_square)
    sherwood = 2.0 + 0.6 * jnp.exp(0.25 * log_flow)
    surface = 0.5 / (1.0 + jnp.exp(-4.0 * (drop_temp - 1.0)))
    evap = evap_coef * radius * density * sherwood * jnp.log((1.0 - fuel) / (1.0 - surface))
    mass = radius * radius * radius
    ratio = 1.0 - time_step * evap / mass
    new_radius = radius * jnp.exp(jnp.log(ratio) * (1.0 / 3.0))
    rate = time_step * (1.0 + 0.15 * jnp.exp(0.35 * log_flow)) / (2.0 * radius * radius)
    change = [rate * s for s in slip]
    new_velocity = [v + c for v, c in zip(velocity, change)]
    heat_rate = heat_coef * sherwood / (radius * radius)
    new_temp = drop_temp + time_step * (
        heat_rate * (heat - drop_temp) - latent_coef * evap / mass
    )
    vapour = time_step * evap
    lost = [mass * (v - n) for v, n in zip(velocity, new_velocity)]
    momentum = [m + vapour * v for m, v in zip(lost, velocity)]
    heat_gain = -time_step * mass * heat_rate * (heat - drop_temp)
    enthalpy = enthalpy_coef * vapour * new_temp
    drag = lost[0] * speed[0] + lost[1] * speed[1] + lost[2] * speed[2]
    return [new_radius, new_temp] + new_velocity, [vapour] + momentum + [heat_gain, enthalpy, drag]


def parcel_kernel(
    info_ref,
    pk_ref,
    lo_ref,
    temp_ref,
    dens_ref,
    vel_ref,
    fuel_ref,
    hi_ref,
    main_ref,
    dlo_ref,
    dhi_ref,
    state_ref,
    own_dst_ref,
    off_ref,
    dst_ref,
    cell_scr,
    off_smem,
    sem,
    pieces,
    cv,
    row_scr,
    ft,
    a_hi,
    a_lo,
    interp,
    src,
    dep,
):
    groups = pk_ref.shape[0]
    each = cells_of(pk_ref.shape[2]) // 8
    capacity = each * 8
    slots = groups * capacity
    blocks = slots // LANES
    count, group = info_ref[0], info_ref[1]

    per_line = each // LANES
    for b in range(blocks):
        q, r = divmod(b, capacity // LANES)
        line, at = divmod(r, per_line)
        at = capacity + at * LANES
        cell_scr[b : b + 1, :] = pk_ref[q, line : line + 1, at : at + LANES]
    cell = cell_scr[...].astype(jnp.int32)
    slot = iota((blocks, LANES), 0) * LANES + iota((blocks, LANES), 1)
    y_of = ((cell >> 7) & 127) - group * 32
    mine = jnp.logical_and(slot < count, jnp.logical_and(y_of >= -1, y_of < 32))
    ones = jnp.where(mine, 1.0, 0.0).astype(BF16)
    before = jnp.where(iota((LANES, LANES), 0) < iota((LANES, LANES), 1), 1.0, 0.0).astype(BF16)
    after = jnp.where(iota((LANES, LANES), 1) < iota((LANES, LANES), 0), 1.0, 0.0).astype(BF16)
    full = jnp.ones((LANES, LANES), BF16)
    within = jnp.dot(ones, before, preferred_element_type=F32)
    row_sum = jnp.dot(ones, full, preferred_element_type=F32).astype(BF16)
    offset = jnp.dot(after, row_sum, preferred_element_type=F32)
    dst = jnp.where(mine, within + offset, -1.0)
    dst_ref[...] = dst
    own_dst_ref[...] = jnp.where(y_of >= 0, dst, -1.0)
    counts = lax.dot_general(jnp.ones((16, LANES), BF16), ones, NT, preferred_element_type=F32)
    counts = counts.astype(BF16)
    starts = jnp.dot(counts, before, preferred_element_type=F32)
    total = jnp.dot(counts, full, preferred_element_type=F32)
    first = iota((8, LANES), 0) == 0
    off_ref[...] = jnp.where(first, starts[0:8], total[0:8]).astype(jnp.int32)
    copy = pltpu.make_async_copy(off_ref, off_smem, sem)
    copy.start()

    def split(q, carry):
        for line in range(8):
            cells = pk_ref[q, line : line + 1, capacity : capacity + each]
            cells = jnp.broadcast_to(cells, (8, each)).astype(jnp.int32)
            row = iota((8, each), 0)
            y_place = ((cells >> 7) & 127) - group * 32
            place = jnp.where(row == 0, cells >> 14, jnp.where(row == 1, y_place, cells & 127))
            values = pk_ref[q, :, line * each : (line + 1) * each]
            high, low = halves(jnp.concatenate([values, place.astype(F32)], axis=0))
            at = pl.ds(pl.multiple_of(q * capacity + line * each, each), each)
            pieces[0:16, at] = high
            pieces[16:32, at] = low
        return carry

    lax.fori_loop(0, groups, split, 0)

    zero = jnp.zeros((256, LANES), F32)
    own = [temp_ref, dens_ref, vel_ref.at[0], vel_ref.at[1], vel_ref.at[2], fuel_ref.at[0]]
    planes = temp_ref.shape[0]
    rows = temp_ref.shape[1]
    row_start = capacity + each
    after_me = jnp.minimum(group + 1, groups - 1)
    before_me = jnp.maximum(group - 1, 0)
    for f in range(6):
        row_scr[...] = zero
        for x in range(planes + 2):
            if x == 0:
                block = lo_ref[f, 0]
            elif x == planes + 1:
                block = hi_ref[f, 0]
            else:
                block = own[f][x - 1]
            row_scr[x * YPAD : x * YPAD + rows, :] = block
            block, line = row_place(planes, f, x, 0)
            at = row_start + block * LANES
            following = pk_ref[after_me, line : line + 1, at : at + LANES]
            row_scr[x * YPAD + rows : x * YPAD + rows + 1, :] = following
            block, line = row_place(planes, f, x, 1)
            at = row_start + block * LANES
            former = pk_ref[before_me, line : line + 1, at : at + LANES]
            row_scr[(x + 1) * YPAD - 1 : (x + 1) * YPAD, :] = former
        high, low = halves(row_scr[...].T)
        at = slice(f * LANES, (f + 1) * LANES)
        ft[at, 0:256] = high
        ft[at, 256:512] = low
        ft[at, 512:768] = high

    cv[...] = jnp.zeros(cv.shape, F32)
    state_ref[...] = jnp.zeros(state_ref.shape, F32)
    dep[...] = jnp.zeros(dep.shape, F32)
    copy.wait()
    live = off_smem[1, 0]

    def compact(i, carry):
        got = []
        for j in range(8):
            b = i * 8 + j
            aligned = (off_smem[0, b] >> 7) << 7
            hot = one_hot(dst_ref[pl.ds(b, 1), :], aligned)
            block = pieces[:, pl.ds(pl.multiple_of(b * LANES, LANES), LANES)]
            got.append((aligned, lax.dot_general(block, hot, NT, preferred_element_type=F32)))
        for aligned, both in got:
            at = pl.ds(pl.multiple_of(aligned, LANES), WINDOW)
            cv[:, at] += both[0:16] + both[16:32]
        return carry

    lax.fori_loop(0, blocks // 8, compact, 0)

    def gather(c, carry):
        at = pl.ds(pl.multiple_of(c * CHUNK, CHUNK), CHUNK)
        valid = c * CHUNK + iota((1, CHUNK), 1) < live
        fx, fy, fz = cv[0:1, at], cv[1:2, at], cv[2:3, at]
        x0, z0 = cv[8:9, at], cv[10:11, at]
        y0 = jnp.where(valid, cv[9:10, at], 1000.0)
        line = iota((YPAD, CHUNK), 0)
        wy = hat(jnp.where(line == YPAD - 1, -1, line).astype(F32), y0, fy)
        parts = [wy * hat(float(x), x0, fx) for x in range(planes + 2)]
        parts.append(jnp.zeros((256 - (planes + 2) * YPAD, CHUNK), F32))
        high, low = halves(jnp.concatenate(parts, axis=0))
        a_hi[c] = high
        a_lo[c] = low
        stacked = jnp.concatenate([high, high, low], axis=0)
        lines = jnp.dot(ft[...], stacked, preferred_element_type=F32)
        wz = hat(iota((LANES, CHUNK), 0).astype(F32), z0, fz)
        for f in range(6):
            interp[f : f + 1, at] = jnp.sum(
                lines[f * LANES : (f + 1) * LANES] * wz, axis=0, keepdims=True
            )
        return carry

    chunks = (live + CHUNK - 1) // CHUNK
    lax.fori_loop(0, chunks, gather, 0)

    def step(c, carry):
        at = pl.ds(pl.multiple_of(c * PHYS, PHYS), PHYS)
        valid = c * PHYS + iota((1, PHYS), 1) < live
        inside = [jnp.where(valid, interp[f : f + 1, at], 0.0) for f in range(6)]
        radius = jnp.where(valid, cv[3:4, at], 1.0)
        velocity = [cv[d : d + 1, at] for d in (5, 6, 7)]
        new, sources = physics(inside, radius, cv[4:5, at], velocity)
        for s in range(5):
            state_ref[s : s + 1, at] = jnp.where(valid, new[s], 0.0)
        for k in range(7):
            src[k : k + 1, at] = jnp.where(valid, sources[k], 0.0)
        return carry

    lax.fori_loop(0, (live + PHYS - 1) // PHYS, step, 0)

    def deposit(c, carry):
        at = pl.ds(pl.multiple_of(c * CHUNK, CHUNK), CHUNK)
        wz = hat(iota((LANES, CHUNK), 0).astype(F32), cv[10:11, at], cv[2:3, at])
        high, low = halves(jnp.concatenate([wz * src[k : k + 1, at] for k in range(7)], axis=0))
        left = jnp.concatenate([high, low, high], axis=1)
        right = jnp.concatenate([a_hi[c], a_hi[c], a_lo[c]], axis=1)
        dep[...] += lax.dot_general(left, right, NT, preferred_element_type=F32)
        return carry

    lax.fori_loop(0, chunks, deposit, 0)

    for k in range(7):
        cells = dep[k * LANES : (k + 1) * LANES, :].T
        for x in range(planes + 2):
            block = cells[x * YPAD : x * YPAD + rows]
            if x == 0:
                dlo_ref[k, 0] = block
            elif x == planes + 1:
                dhi_ref[k, 0] = block
            else:
                main_ref[k, x - 1] = block


def spread_kernel(info_ref, off_ref, dst_ref, state_ref, *outs_and_scratch):
    outs, both_scr = outs_and_scratch[:-1], outs_and_scratch[-1]
    high, low = halves(state_ref[...])
    both_scr[0:16, :] = jnp.concatenate([high, low], axis=0)
    group = info_ref[1]
    each = dst_ref.shape[0] // len(outs)
    for d, out in enumerate(outs):
        owner = lax.rem(group + d, len(outs))

        def spread(i, carry):
            for j in range(8):
                b = owner * each + i * 8 + j
                aligned = (off_ref[0, b] >> 7) << 7
                hot = one_hot(dst_ref[pl.ds(b, 1), :], aligned)
                block = both_scr[:, pl.ds(pl.multiple_of(aligned, LANES), WINDOW)]
                got = jnp.dot(block, hot, preferred_element_type=F32)
                at = pl.ds(pl.multiple_of((i * 8 + j) * LANES, LANES), LANES)
                out[:, at] = got[0:8] + got[8:16]
            return carry

        lax.fori_loop(0, each // 8, spread, 0)


def prepare_kernel(
    cells_ref,
    weights_ref,
    radius_ref,
    temp_ref,
    velocity_ref,
    gas_temp_ref,
    dens_ref,
    vel_ref,
    species_ref,
    packed_ref,
    top_ref,
    bottom_ref,
    up_ref,
    down_ref,
    right_ref,
    left_ref,
):
    planes, rows = species_ref.shape[1:3]
    up_ref[...] = species_ref[:, planes - 2 : planes]
    down_ref[...] = species_ref[:, 0:2]
    right_ref[...] = species_ref[:, :, rows - 2 : rows]
    left_ref[...] = species_ref[:, :, 0:2]

    @pl.when(pl.program_id(0) == 0)
    def _():
        w = [weights_ref[c : c + 1, :] for c in range(8)]
        slots = cells_ref.shape[1]
        each = slots // 8
        packed_ref[0:1, 0:slots] = (w[4] + w[5]) + (w[6] + w[7])
        packed_ref[1:2, 0:slots] = (w[2] + w[3]) + (w[6] + w[7])
        packed_ref[2:3, 0:slots] = (w[1] + w[3]) + (w[5] + w[7])
        packed_ref[3:4, 0:slots] = radius_ref[...].reshape(1, -1)
        packed_ref[4:5, 0:slots] = temp_ref[...].reshape(1, -1)
        packed_ref[5:8, 0:slots] = velocity_ref[...]
        for i in range(8):
            first = cells_ref[0:1, i * each : (i + 1) * each]
            packed_ref[i : i + 1, slots : slots + each] = first.astype(F32)
        own = [gas_temp_ref, dens_ref, vel_ref.at[0], vel_ref.at[1], vel_ref.at[2],
               species_ref.at[0]]
        for f in range(6):
            top_ref[f, 0] = own[f][planes - 1]
            bottom_ref[f, 0] = own[f][0]


def assemble_kernel(packed_ref, lo_ref, temp_ref, dens_ref, vel_ref, fuel_ref, hi_ref, out_ref):
    start = packed_ref.shape[1]
    out_ref[:, 0:start] = packed_ref[...]
    planes, rows = temp_ref.shape[0:2]
    own = [temp_ref, dens_ref, vel_ref.at[0], vel_ref.at[1], vel_ref.at[2], fuel_ref.at[0]]
    for f in range(6):
        for x in range(planes + 2):
            if x == 0:
                plane = lo_ref.at[f, 0]
            elif x == planes + 1:
                plane = hi_ref.at[f, 0]
            else:
                plane = own[f].at[x - 1]
            for side, y in enumerate((0, rows - 1)):
                block, line = row_place(planes, f, x, side)
                at = start + block * LANES
                out_ref[line : line + 1, at : at + LANES] = plane[y : y + 1, :]


def row_place(planes, f, x, side):
    return divmod((f * (planes + 2) + x) * 2 + side, 8)


def transport_kernel(
    first_part,
    first_block,
    diff_ref,
    y_ref,
    xlo_ref,
    xhi_ref,
    ylo_ref,
    yhi_ref,
    ux_ref,
    dens_ref,
    *rest,
):
    if first_part:
        main_ref, below_ref, above_ref, out_ref, gas_ref, pad = rest

        @pl.when(pl.program_id(0) == 0)
        def _():
            last = main_ref.shape[1] - 1
            for k in range(main_ref.shape[0]):
                for x in range(last + 1):
                    total = main_ref[k, x]
                    if x == 0:
                        total = total + below_ref[k, 0]
                    if x == last:
                        total = total + above_ref[k, 0]
                    gas_ref[k, x] = total

        vap_ref = gas_ref.at[0]
    else:
        vap_ref, _, out_ref, pad = rest
    species, planes, rows, depth = y_ref.shape
    at = iota((rows, depth), 1)
    left1 = jnp.where(at >= 1, 16.0, 0.0)
    left2 = jnp.where(at >= 2, -1.0, 0.0)
    right1 = jnp.where(at < depth - 1, 16.0, 0.0)
    right2 = jnp.where(at < depth - 2, -1.0, 0.0)
    first = (first_block + pl.program_id(0)) * species
    for x in range(planes):
        speed = ux_ref[x] * (courant / 12.0)
        gain = source_coef * vap_ref[x] / dens_ref[x]

        for s in range(species):
            d12 = diff_ref[first + s] * (1.0 / 12.0)

            def plane(i, s=s):
                if i < 0:
                    return xlo_ref[s, i + 2]
                if i >= planes:
                    return xhi_ref[s, i - planes]
                return y_ref[s, i]

            center = plane(x)
            up1, up2, dn1, dn2 = plane(x + 1), plane(x + 2), plane(x - 1), plane(x - 2)
            pad[s, 6:8, :] = ylo_ref[s, x]
            pad[s, 8 : 8 + rows, :] = center
            pad[s, 8 + rows : 10 + rows, :] = yhi_ref[s, x]
            near = up1 + dn1 + pad[s, 7 : 7 + rows, :] + pad[s, 9 : 9 + rows, :]
            far = up2 + dn2 + pad[s, 6 : 6 + rows, :] + pad[s, 10 : 10 + rows, :]
            along = (
                left1 * pltpu.roll(center, 1, 1)
                + right1 * pltpu.roll(center, depth - 1, 1)
                + left2 * pltpu.roll(center, 2, 1)
                + right2 * pltpu.roll(center, depth - 2, 1)
            )
            slope = 8.0 * (up1 - dn1) - (up2 - dn2)
            flag = jnp.where(first + s == 0, 1.0, 0.0)
            laplace = 16.0 * near - far + along - 90.0 * center
            out_ref[s, x] = center + d12 * laplace - speed * slope + gain * (flag - center)


def per_device(
    species,
    diffusion,
    gas_temp,
    gas_density,
    gas_velocity,
    drop_radius,
    drop_temp,
    drop_velocity,
    parcel_cells,
    parcel_weights,
    parcel_counts,
):
    count_s = lax.axis_size("space")
    groups = lax.axis_size("group")
    planes, rows, depth = gas_temp.shape
    kinds = species.shape[0]
    capacity = drop_radius.shape[0]
    slots = capacity * groups
    blocks = slots // LANES
    ahead = [(i, i + 1) for i in range(count_s - 1)]
    back = [(b, a) for a, b in ahead]
    g_ahead = [(i, i + 1) for i in range(groups - 1)]
    g_back = [(b, a) for a, b in g_ahead]
    group = lax.axis_index("group")
    info = jnp.stack([parcel_counts[0], group.astype(jnp.int32)])

    whole = lambda shape: pl.BlockSpec(shape, lambda i, n=len(shape): (0,) * n)
    smem = pl.BlockSpec(memory_space=pltpu.SMEM)
    hbm = pl.BlockSpec(memory_space=pl.ANY)
    shaped = lambda *shape: jax.ShapeDtypeStruct(shape, F32)
    limit = pltpu.CompilerParams(vmem_limit_bytes=62 * 2**20)

    def by_kind(first, *shape):
        return pl.BlockSpec((MANY,) + shape, lambda i: (first + i, 0, 0, 0))

    packed, top, bottom, x_up, x_down, y_right, y_left = pl.pallas_call(
        prepare_kernel,
        grid=(kinds // MANY,),
        in_specs=[
            whole((8, capacity)),
            whole((8, capacity)),
            whole((capacity,)),
            whole((capacity,)),
            whole((3, capacity)),
            whole((planes, rows, depth)),
            whole((planes, rows, depth)),
            whole((3, planes, rows, depth)),
            by_kind(0, planes, rows, depth),
        ],
        out_specs=[
            whole((8, capacity // 8 * 9)),
            whole((6, 1, rows, depth)),
            whole((6, 1, rows, depth)),
            by_kind(0, 2, rows, depth),
            by_kind(0, 2, rows, depth),
            by_kind(0, planes, 2, depth),
            by_kind(0, planes, 2, depth),
        ],
        out_shape=[
            shaped(8, capacity // 8 * 9),
            shaped(6, 1, rows, depth),
            shaped(6, 1, rows, depth),
            shaped(kinds, 2, rows, depth),
            shaped(kinds, 2, rows, depth),
            shaped(kinds, planes, 2, depth),
            shaped(kinds, planes, 2, depth),
        ],
        compiler_params=limit,
        name="prepare",
    )(
        parcel_cells, parcel_weights, drop_radius, drop_temp, drop_velocity,
        gas_temp, gas_density, gas_velocity, species,
    )
    field_lo = lax.ppermute(top, "space", ahead)
    field_hi = lax.ppermute(bottom, "space", back)
    width = capacity // 8 * 9 + ROWS_WIDTH
    sent = pl.pallas_call(
        assemble_kernel,
        grid=(1,),
        in_specs=[
            whole((8, capacity // 8 * 9)),
            whole((6, 1, rows, depth)),
            whole((planes, rows, depth)),
            whole((planes, rows, depth)),
            whole((3, planes, rows, depth)),
            whole((1, planes, rows, depth)),
            whole((6, 1, rows, depth)),
        ],
        out_specs=whole((8, width)),
        out_shape=shaped(8, width),
        compiler_params=limit,
        name="assemble",
    )(packed, field_lo, gas_temp, gas_density, gas_velocity, species, field_hi)
    parcels = lax.all_gather(sent, "group", axis=0)

    x_up, x_down, y_right, y_left, parcels = lax.optimization_barrier(
        (x_up, x_down, y_right, y_left, parcels)
    )
    x_lo = lax.ppermute(x_up, "space", ahead)
    x_hi = lax.ppermute(x_down, "space", back)
    y_lo = lax.ppermute(y_right, "group", g_ahead)

    reach = slots + WINDOW
    main, dep_lo, dep_hi, state, dst, off = pl.pallas_call(
        parcel_kernel,
        grid=(1,),
        in_specs=[
            smem,
            whole((groups, 8, width)),
            whole((6, 1, rows, depth)),
            whole((planes, rows, depth)),
            whole((planes, rows, depth)),
            whole((3, planes, rows, depth)),
            whole((1, planes, rows, depth)),
            whole((6, 1, rows, depth)),
        ],
        out_specs=[
            whole((7, planes, rows, depth)),
            whole((7, 1, rows, depth)),
            whole((7, 1, rows, depth)),
            whole((8, reach)),
            whole((blocks, LANES)),
            whole((8, LANES)),
        ],
        out_shape=[
            shaped(7, planes, rows, depth),
            shaped(7, 1, rows, depth),
            shaped(7, 1, rows, depth),
            shaped(8, reach),
            shaped(blocks, LANES),
            jax.ShapeDtypeStruct((8, LANES), jnp.int32),
        ],
        scratch_shapes=[
            pltpu.VMEM((blocks, LANES), F32),
            pltpu.VMEM((blocks, LANES), F32),
            pltpu.SMEM((8, LANES), jnp.int32),
            pltpu.SemaphoreType.DMA,
            pltpu.VMEM((32, slots), BF16),
            pltpu.VMEM((16, reach), F32),
            pltpu.VMEM((256, LANES), F32),
            pltpu.VMEM((6 * LANES, 768), BF16),
            pltpu.VMEM((slots // CHUNK, 256, CHUNK), BF16),
            pltpu.VMEM((slots // CHUNK, 256, CHUNK), BF16),
            pltpu.VMEM((8, slots), F32),
            pltpu.VMEM((8, slots), F32),
            pltpu.VMEM((7 * LANES, 256), F32),
        ],
        compiler_params=limit,
        name="parcels",
    )(info, parcels, field_lo, gas_temp, gas_density, gas_velocity, species, field_hi)

    from_below = lax.ppermute(dep_hi, "space", ahead)
    from_above = lax.ppermute(dep_lo, "space", back)

    spread = pl.pallas_call(
        spread_kernel,
        grid=(1,),
        in_specs=[smem, smem, whole((blocks, LANES)), whole((8, reach))],
        out_specs=[whole((8, capacity))] * groups,
        out_shape=[shaped(8, capacity)] * groups,
        scratch_shapes=[pltpu.VMEM((16, reach), BF16)],
        compiler_params=limit,
        name="spread",
    )(info, off, dst, state)
    y_lo, y_left, spread = lax.optimization_barrier((y_lo, y_left, spread))
    y_hi = lax.ppermute(y_left, "group", g_back)
    y_lo, y_hi, from_below, from_above, spread = lax.optimization_barrier(
        (y_lo, y_hi, from_below, from_above, spread)
    )
    returned = [spread[0]]
    for d in range(1, groups):
        route = [(i, (i + d) % groups) for i in range(groups)]
        returned.append(lax.ppermute(spread[d], "group", route))
    gas = pl.BlockSpec((planes, rows, depth), lambda i: (0, 0, 0))
    row0 = pl.BlockSpec((None, planes, rows, depth), lambda i: (0, 0, 0, 0))
    all_gas = whole((7, planes, rows, depth))
    rim = whole((7, 1, rows, depth))
    species_next = gas_sources = None
    at = 0
    for c, size in enumerate(PARTS):
        first = at // MANY
        at += size
        out_specs = [by_kind(first, planes, rows, depth)]
        out_shape = [shaped(*species.shape)]
        if c == 0:
            extra, extra_specs = (main, from_below, from_above), [all_gas, rim, rim]
            out_specs.append(all_gas)
            out_shape.append(shaped(7, planes, rows, depth))
        else:
            extra, extra_specs = (gas_sources, species_next), [row0, hbm]
        got = pl.pallas_call(
            functools.partial(transport_kernel, c == 0, first),
            grid=(size // MANY,),
            in_specs=[
                smem,
                by_kind(first, planes, rows, depth),
                by_kind(first, 2, rows, depth),
                by_kind(first, 2, rows, depth),
                by_kind(first, planes, 2, depth),
                by_kind(first, planes, 2, depth),
                row0,
                gas,
            ]
            + extra_specs,
            out_specs=out_specs,
            out_shape=out_shape,
            input_output_aliases={} if c == 0 else {9: 0},
            scratch_shapes=[pltpu.VMEM((MANY, rows + 16, depth), F32)],
            compiler_params=limit,
            name="transport",
        )(diffusion, species, x_lo, x_hi, y_lo, y_hi, gas_velocity, gas_density, *extra)
        species_next = got[0]
        if c == 0:
            gas_sources = got[1]
    species_next, returned = lax.optimization_barrier((species_next, returned))
    new_state = sum(returned[1:], returned[0])
    old_state = jnp.concatenate([drop_radius[None], drop_temp[None], drop_velocity], axis=0)
    slot = group * capacity + jnp.arange(capacity, dtype=jnp.int32)
    live = slot < parcel_counts[0]
    parcel_state = jnp.where(live[None], new_state[0:5], old_state)
    return (species_next, gas_sources, parcel_state)


def solution(mesh):
    in_specs = (
        P(None, "space", "group", None),
        P(),
        P("space", "group", None),
        P("space", "group", None),
        P(None, "space", "group", None),
        P(("space", "group")),
        P(("space", "group")),
        P(None, ("space", "group")),
        P(None, ("space", "group")),
        P(None, ("space", "group")),
        P("space"),
    )
    out_specs = (
        P(None, "space", "group", None),
        P(None, "space", "group", None),
        P(None, ("space", "group")),
    )
    return jax.shard_map(
        per_device, mesh=mesh, in_specs=in_specs, out_specs=out_specs, check_vma=False
    )
```

```python
import functools

import jax
import jax.numpy as jnp
from jax import lax
from jax.experimental import pallas as pl
from jax.experimental.pallas import tpu as pltpu
from jax.sharding import PartitionSpec as P

time_step = 0.05
evap_coef = 0.5
heat_coef = 0.15
latent_coef = 0.2
enthalpy_coef = 1.3
source_coef = 0.5
courant = 0.3

LANES = 128
PARTS = (54,)
MANY = 18
CHUNK = 1536
WINDOW = 256
YPAD = 40
ROWS_WIDTH = 9 * LANES
F32 = jnp.float32
BF16 = jnp.bfloat16
NT = (((1,), (1,)), ((), ()))


def halves(value):
    high = value.astype(BF16)
    return high, (value - high.astype(F32)).astype(BF16)


def hat(index, start, fraction):
    away = index - start
    return jnp.where(away == 0.0, 1.0 - fraction, jnp.where(away == 1.0, fraction, 0.0))


def iota(shape, dim):
    return lax.broadcasted_iota(jnp.int32, shape, dim)


def one_hot(dst_row, aligned):
    rel = dst_row - aligned.astype(F32)
    return jnp.where(iota((WINDOW, LANES), 0).astype(F32) == rel, 1.0, 0.0).astype(BF16)


def cells_of(width):
    return (width - ROWS_WIDTH) // 9 * 8


def physics(interp, radius, drop_temp, velocity):
    heat, density, speed, fuel = interp[0], interp[1], interp[2:5], interp[5]
    slip = [g - v for g, v in zip(speed, velocity)]
    slip_square = slip[0] * slip[0] + slip[1] * slip[1] + slip[2] * slip[2]
    log_flow = jnp.log(1.0 + density * radius * slip_square)
    sherwood = 2.0 + 0.6 * jnp.exp(0.25 * log_flow)
    surface = 0.5 / (1.0 + jnp.exp(-4.0 * (drop_temp - 1.0)))
    evap = evap_coef * radius * density * sherwood * jnp.log((1.0 - fuel) / (1.0 - surface))
    mass = radius * radius * radius
    ratio = 1.0 - time_step * evap / mass
    new_radius = radius * jnp.exp(jnp.log(ratio) * (1.0 / 3.0))
    rate = time_step * (1.0 + 0.15 * jnp.exp(0.35 * log_flow)) / (2.0 * radius * radius)
    change = [rate * s for s in slip]
    new_velocity = [v + c for v, c in zip(velocity, change)]
    heat_rate = heat_coef * sherwood / (radius * radius)
    new_temp = drop_temp + time_step * (
        heat_rate * (heat - drop_temp) - latent_coef * evap / mass
    )
    vapour = time_step * evap
    lost = [mass * (v - n) for v, n in zip(velocity, new_velocity)]
    momentum = [m + vapour * v for m, v in zip(lost, velocity)]
    heat_gain = -time_step * mass * heat_rate * (heat - drop_temp)
    enthalpy = enthalpy_coef * vapour * new_temp
    drag = lost[0] * speed[0] + lost[1] * speed[1] + lost[2] * speed[2]
    return [new_radius, new_temp] + new_velocity, [vapour] + momentum + [heat_gain, enthalpy, drag]


def parcel_kernel(
    info_ref,
    pk_ref,
    lo_ref,
    temp_ref,
    dens_ref,
    vel_ref,
    fuel_ref,
    hi_ref,
    main_ref,
    dlo_ref,
    dhi_ref,
    state_ref,
    own_dst_ref,
    off_ref,
    dst_ref,
    cell_scr,
    off_smem,
    sem,
    pieces,
    cv,
    row_scr,
    ft,
    a_hi,
    a_lo,
    interp,
    src,
    dep,
):
    groups = pk_ref.shape[0]
    each = cells_of(pk_ref.shape[2]) // 8
    capacity = each * 8
    slots = groups * capacity
    blocks = slots // LANES
    count, group = info_ref[0], info_ref[1]

    per_line = each // LANES
    for b in range(blocks):
        q, r = divmod(b, capacity // LANES)
        line, at = divmod(r, per_line)
        at = capacity + at * LANES
        cell_scr[b : b + 1, :] = pk_ref[q, line : line + 1, at : at + LANES]
    cell = cell_scr[...].astype(jnp.int32)
    slot = iota((blocks, LANES), 0) * LANES + iota((blocks, LANES), 1)
    y_of = ((cell >> 7) & 127) - group * 32
    mine = jnp.logical_and(slot < count, jnp.logical_and(y_of >= -1, y_of < 32))
    ones = jnp.where(mine, 1.0, 0.0).astype(BF16)
    before = jnp.where(iota((LANES, LANES), 0) < iota((LANES, LANES), 1), 1.0, 0.0).astype(BF16)
    after = jnp.where(iota((LANES, LANES), 1) < iota((LANES, LANES), 0), 1.0, 0.0).astype(BF16)
    full = jnp.ones((LANES, LANES), BF16)
    within = jnp.dot(ones, before, preferred_element_type=F32)
    row_sum = jnp.dot(ones, full, preferred_element_type=F32).astype(BF16)
    offset = jnp.dot(after, row_sum, preferred_element_type=F32)
    dst = jnp.where(mine, within + offset, -1.0)
    dst_ref[...] = dst
    own_dst_ref[...] = jnp.where(y_of >= 0, dst, -1.0)
    counts = lax.dot_general(jnp.ones((16, LANES), BF16), ones, NT, preferred_element_type=F32)
    counts = counts.astype(BF16)
    starts = jnp.dot(counts, before, preferred_element_type=F32)
    total = jnp.dot(counts, full, preferred_element_type=F32)
    first = iota((8, LANES), 0) == 0
    off_ref[...] = jnp.where(first, starts[0:8], total[0:8]).astype(jnp.int32)
    copy = pltpu.make_async_copy(off_ref, off_smem, sem)
    copy.start()

    def split(q, carry):
        for line in range(8):
            cells = pk_ref[q, line : line + 1, capacity : capacity + each]
            cells = jnp.broadcast_to(cells, (8, each)).astype(jnp.int32)
            row = iota((8, each), 0)
            y_place = ((cells >> 7) & 127) - group * 32
            place = jnp.where(row == 0, cells >> 14, jnp.where(row == 1, y_place, cells & 127))
            values = pk_ref[q, :, line * each : (line + 1) * each]
            high, low = halves(jnp.concatenate([values, place.astype(F32)], axis=0))
            at = pl.ds(pl.multiple_of(q * capacity + line * each, each), each)
            pieces[0:16, at] = high
            pieces[16:32, at] = low
        return carry

    lax.fori_loop(0, groups, split, 0)

    zero = jnp.zeros((256, LANES), F32)
    own = [temp_ref, dens_ref, vel_ref.at[0], vel_ref.at[1], vel_ref.at[2], fuel_ref.at[0]]
    planes = temp_ref.shape[0]
    rows = temp_ref.shape[1]
    row_start = capacity + each
    after_me = jnp.minimum(group + 1, groups - 1)
    before_me = jnp.maximum(group - 1, 0)
    for f in range(6):
        row_scr[...] = zero
        for x in range(planes + 2):
            if x == 0:
                block = lo_ref[f, 0]
            elif x == planes + 1:
                block = hi_ref[f, 0]
            else:
                block = own[f][x - 1]
            row_scr[x * YPAD : x * YPAD + rows, :] = block
            block, line = row_place(planes, f, x, 0)
            at = row_start + block * LANES
            following = pk_ref[after_me, line : line + 1, at : at + LANES]
            row_scr[x * YPAD + rows : x * YPAD + rows + 1, :] = following
            block, line = row_place(planes, f, x, 1)
            at = row_start + block * LANES
            former = pk_ref[before_me, line : line + 1, at : at + LANES]
            row_scr[(x + 1) * YPAD - 1 : (x + 1) * YPAD, :] = former
        high, low = halves(row_scr[...].T)
        at = slice(f * LANES, (f + 1) * LANES)
        ft[at, 0:256] = high
        ft[at, 256:512] = low
        ft[at, 512:768] = high

    cv[...] = jnp.zeros(cv.shape, F32)
    state_ref[...] = jnp.zeros(state_ref.shape, F32)
    dep[...] = jnp.zeros(dep.shape, F32)
    copy.wait()
    live = off_smem[1, 0]

    def compact(i, carry):
        got = []
        for j in range(8):
            b = i * 8 + j
            aligned = (off_smem[0, b] >> 7) << 7
            hot = one_hot(dst_ref[pl.ds(b, 1), :], aligned)
            block = pieces[:, pl.ds(pl.multiple_of(b * LANES, LANES), LANES)]
            got.append((aligned, lax.dot_general(block, hot, NT, preferred_element_type=F32)))
        for aligned, both in got:
            at = pl.ds(pl.multiple_of(aligned, LANES), WINDOW)
            cv[:, at] += both[0:16] + both[16:32]
        return carry

    lax.fori_loop(0, blocks // 8, compact, 0)

    def gather(c, carry):
        at = pl.ds(pl.multiple_of(c * CHUNK, CHUNK), CHUNK)
        valid = c * CHUNK + iota((1, CHUNK), 1) < live
        fx, fy, fz = cv[0:1, at], cv[1:2, at], cv[2:3, at]
        x0, z0 = cv[8:9, at], cv[10:11, at]
        y0 = jnp.where(valid, cv[9:10, at], 1000.0)
        line = iota((YPAD, CHUNK), 0)
        wy = hat(jnp.where(line == YPAD - 1, -1, line).astype(F32), y0, fy)
        parts = [wy * hat(float(x), x0, fx) for x in range(planes + 2)]
        parts.append(jnp.zeros((256 - (planes + 2) * YPAD, CHUNK), F32))
        high, low = halves(jnp.concatenate(parts, axis=0))
        a_hi[c] = high
        a_lo[c] = low
        stacked = jnp.concatenate([high, high, low], axis=0)
        lines = jnp.dot(ft[...], stacked, preferred_element_type=F32)
        wz = hat(iota((LANES, CHUNK), 0).astype(F32), z0, fz)
        for f in range(6):
            interp[f : f + 1, at] = jnp.sum(
                lines[f * LANES : (f + 1) * LANES] * wz, axis=0, keepdims=True
            )
        return carry

    chunks = (live + CHUNK - 1) // CHUNK
    lax.fori_loop(0, chunks, gather, 0)

    def step(c, carry):
        at = pl.ds(pl.multiple_of(c * CHUNK, CHUNK), CHUNK)
        valid = c * CHUNK + iota((1, CHUNK), 1) < live
        inside = [jnp.where(valid, interp[f : f + 1, at], 0.0) for f in range(6)]
        radius = jnp.where(valid, cv[3:4, at], 1.0)
        velocity = [cv[d : d + 1, at] for d in (5, 6, 7)]
        new, sources = physics(inside, radius, cv[4:5, at], velocity)
        for s in range(5):
            state_ref[s : s + 1, at] = jnp.where(valid, new[s], 0.0)
        for k in range(7):
            src[k : k + 1, at] = jnp.where(valid, sources[k], 0.0)
        return carry

    lax.fori_loop(0, (live + CHUNK - 1) // CHUNK, step, 0)

    def deposit(c, carry):
        at = pl.ds(pl.multiple_of(c * CHUNK, CHUNK), CHUNK)
        wz = hat(iota((LANES, CHUNK), 0).astype(F32), cv[10:11, at], cv[2:3, at])
        high, low = halves(jnp.concatenate([wz * src[k : k + 1, at] for k in range(7)], axis=0))
        left = jnp.concatenate([high, low, high], axis=1)
        right = jnp.concatenate([a_hi[c], a_hi[c], a_lo[c]], axis=1)
        dep[...] += lax.dot_general(left, right, NT, preferred_element_type=F32)
        return carry

    lax.fori_loop(0, chunks, deposit, 0)

    for k in range(7):
        cells = dep[k * LANES : (k + 1) * LANES, :].T
        for x in range(planes + 2):
            block = cells[x * YPAD : x * YPAD + rows]
            if x == 0:
                dlo_ref[k, 0] = block
            elif x == planes + 1:
                dhi_ref[k, 0] = block
            else:
                main_ref[k, x - 1] = block


def spread_kernel(off_ref, dst_ref, state_ref, out_ref, both_scr):
    high, low = halves(state_ref[...])
    both_scr[0:16, :] = jnp.concatenate([high, low], axis=0)
    each = dst_ref.shape[0] // out_ref.shape[0]
    for owner in range(out_ref.shape[0]):

        def spread(i, carry, owner=owner):
            for j in range(8):
                b = owner * each + i * 8 + j
                aligned = (off_ref[0, b] >> 7) << 7
                hot = one_hot(dst_ref[pl.ds(b, 1), :], aligned)
                block = both_scr[:, pl.ds(pl.multiple_of(aligned, LANES), WINDOW)]
                got = jnp.dot(block, hot, preferred_element_type=F32)
                at = pl.ds(pl.multiple_of((i * 8 + j) * LANES, LANES), LANES)
                out_ref[owner, :, at] = got[0:8] + got[8:16]
            return carry

        lax.fori_loop(0, each // 8, spread, 0)


def state_kernel(info_ref, returned_ref, radius_ref, temp_ref, velocity_ref, out_ref):
    slots = velocity_ref.shape[1]
    new = returned_ref[0] + returned_ref[1]
    for owner in range(2, returned_ref.shape[0]):
        new = new + returned_ref[owner]
    live = info_ref[1] * slots + iota((1, slots), 1) < info_ref[0]
    out_ref[0:1, :] = jnp.where(live, new[0:1], radius_ref[...].reshape(1, -1))
    out_ref[1:2, :] = jnp.where(live, new[1:2], temp_ref[...].reshape(1, -1))
    out_ref[2:5, :] = jnp.where(live, new[2:5], velocity_ref[...])


def pack_kernel(
    cells_ref,
    weights_ref,
    radius_ref,
    temp_ref,
    velocity_ref,
    gas_temp_ref,
    dens_ref,
    vel_ref,
    fuel_ref,
    packed_ref,
    top_ref,
    bottom_ref,
):
    planes = gas_temp_ref.shape[0]
    own = [gas_temp_ref, dens_ref, vel_ref.at[0], vel_ref.at[1], vel_ref.at[2], fuel_ref.at[0]]
    for f in range(6):
        top_ref[f, 0] = own[f][planes - 1]
        bottom_ref[f, 0] = own[f][0]
    w = [weights_ref[c : c + 1, :] for c in range(8)]
    slots = cells_ref.shape[1]
    each = slots // 8
    packed_ref[0:1, 0:slots] = (w[4] + w[5]) + (w[6] + w[7])
    packed_ref[1:2, 0:slots] = (w[2] + w[3]) + (w[6] + w[7])
    packed_ref[2:3, 0:slots] = (w[1] + w[3]) + (w[5] + w[7])
    packed_ref[3:4, 0:slots] = radius_ref[...].reshape(1, -1)
    packed_ref[4:5, 0:slots] = temp_ref[...].reshape(1, -1)
    packed_ref[5:8, 0:slots] = velocity_ref[...]
    for i in range(8):
        first = cells_ref[0:1, i * each : (i + 1) * each]
        packed_ref[i : i + 1, slots : slots + each] = first.astype(F32)


def rims_kernel(species_ref, up_ref, down_ref, right_ref, left_ref):
    planes, rows = species_ref.shape[1:3]
    up_ref[...] = species_ref[:, planes - 2 : planes]
    down_ref[...] = species_ref[:, 0:2]
    right_ref[...] = species_ref[:, :, rows - 2 : rows]
    left_ref[...] = species_ref[:, :, 0:2]


def assemble_kernel(packed_ref, lo_ref, temp_ref, dens_ref, vel_ref, fuel_ref, hi_ref, out_ref):
    start = packed_ref.shape[1]
    out_ref[:, 0:start] = packed_ref[...]
    planes, rows = temp_ref.shape[0:2]
    own = [temp_ref, dens_ref, vel_ref.at[0], vel_ref.at[1], vel_ref.at[2], fuel_ref.at[0]]
    for f in range(6):
        for x in range(planes + 2):
            if x == 0:
                plane = lo_ref.at[f, 0]
            elif x == planes + 1:
                plane = hi_ref.at[f, 0]
            else:
                plane = own[f].at[x - 1]
            for side, y in enumerate((0, rows - 1)):
                block, line = row_place(planes, f, x, side)
                at = start + block * LANES
                out_ref[line : line + 1, at : at + LANES] = plane[y : y + 1, :]


def row_place(planes, f, x, side):
    return divmod((f * (planes + 2) + x) * 2 + side, 8)


def transport_kernel(
    first_part,
    first_block,
    diff_ref,
    y_ref,
    xlo_ref,
    xhi_ref,
    ylo_ref,
    yhi_ref,
    ux_ref,
    dens_ref,
    *rest,
):
    if first_part:
        main_ref, below_ref, above_ref, out_ref, gas_ref, pad = rest

        @pl.when(pl.program_id(0) == 0)
        def _():
            last = main_ref.shape[1] - 1
            for k in range(main_ref.shape[0]):
                for x in range(last + 1):
                    total = main_ref[k, x]
                    if x == 0:
                        total = total + below_ref[k, 0]
                    if x == last:
                        total = total + above_ref[k, 0]
                    gas_ref[k, x] = total

        vap_ref = gas_ref.at[0]
    else:
        vap_ref, _, out_ref, pad = rest
    species, planes, rows, depth = y_ref.shape
    at = iota((rows, depth), 1)
    left1 = jnp.where(at >= 1, 16.0, 0.0)
    left2 = jnp.where(at >= 2, -1.0, 0.0)
    right1 = jnp.where(at < depth - 1, 16.0, 0.0)
    right2 = jnp.where(at < depth - 2, -1.0, 0.0)
    first = (first_block + pl.program_id(0)) * species
    for x in range(planes):
        speed = ux_ref[x] * (courant / 12.0)
        gain = source_coef * vap_ref[x] / dens_ref[x]

        for s in range(species):
            d12 = diff_ref[first + s] * (1.0 / 12.0)

            def plane(i, s=s):
                if i < 0:
                    return xlo_ref[s, i + 2]
                if i >= planes:
                    return xhi_ref[s, i - planes]
                return y_ref[s, i]

            center = plane(x)
            up1, up2, dn1, dn2 = plane(x + 1), plane(x + 2), plane(x - 1), plane(x - 2)
            pad[s, 6:8, :] = ylo_ref[s, x]
            pad[s, 8 : 8 + rows, :] = center
            pad[s, 8 + rows : 10 + rows, :] = yhi_ref[s, x]
            near = up1 + dn1 + pad[s, 7 : 7 + rows, :] + pad[s, 9 : 9 + rows, :]
            far = up2 + dn2 + pad[s, 6 : 6 + rows, :] + pad[s, 10 : 10 + rows, :]
            along = (
                left1 * pltpu.roll(center, 1, 1)
                + right1 * pltpu.roll(center, depth - 1, 1)
                + left2 * pltpu.roll(center, 2, 1)
                + right2 * pltpu.roll(center, depth - 2, 1)
            )
            slope = 8.0 * (up1 - dn1) - (up2 - dn2)
            flag = jnp.where(first + s == 0, 1.0, 0.0)
            laplace = 16.0 * near - far + along - 90.0 * center
            out_ref[s, x] = center + d12 * laplace - speed * slope + gain * (flag - center)


def per_device(
    species,
    diffusion,
    gas_temp,
    gas_density,
    gas_velocity,
    drop_radius,
    drop_temp,
    drop_velocity,
    parcel_cells,
    parcel_weights,
    parcel_counts,
):
    count_s = lax.axis_size("space")
    groups = lax.axis_size("group")
    planes, rows, depth = gas_temp.shape
    kinds = species.shape[0]
    capacity = drop_radius.shape[0]
    slots = capacity * groups
    blocks = slots // LANES
    ahead = [(i, i + 1) for i in range(count_s - 1)]
    back = [(b, a) for a, b in ahead]
    g_ahead = [(i, i + 1) for i in range(groups - 1)]
    g_back = [(b, a) for a, b in g_ahead]
    group = lax.axis_index("group")
    info = jnp.stack([parcel_counts[0], group.astype(jnp.int32)])

    whole = lambda shape: pl.BlockSpec(shape, lambda i, n=len(shape): (0,) * n)
    smem = pl.BlockSpec(memory_space=pltpu.SMEM)
    hbm = pl.BlockSpec(memory_space=pl.ANY)
    shaped = lambda *shape: jax.ShapeDtypeStruct(shape, F32)
    limit = pltpu.CompilerParams(vmem_limit_bytes=62 * 2**20)

    def by_kind(first, *shape):
        return pl.BlockSpec((MANY,) + shape, lambda i: (first + i, 0, 0, 0))

    packed, top, bottom = pl.pallas_call(
        pack_kernel,
        grid=(1,),
        in_specs=[
            whole((8, capacity)),
            whole((8, capacity)),
            whole((capacity,)),
            whole((capacity,)),
            whole((3, capacity)),
            whole((planes, rows, depth)),
            whole((planes, rows, depth)),
            whole((3, planes, rows, depth)),
            whole((1, planes, rows, depth)),
        ],
        out_specs=[
            whole((8, capacity // 8 * 9)),
            whole((6, 1, rows, depth)),
            whole((6, 1, rows, depth)),
        ],
        out_shape=[
            shaped(8, capacity // 8 * 9),
            shaped(6, 1, rows, depth),
            shaped(6, 1, rows, depth),
        ],
        compiler_params=limit,
        name="pack",
    )(
        parcel_cells, parcel_weights, drop_radius, drop_temp, drop_velocity,
        gas_temp, gas_density, gas_velocity, species,
    )
    species_cut, packed = lax.optimization_barrier((species, packed))
    x_up, x_down, y_right, y_left = pl.pallas_call(
        rims_kernel,
        grid=(kinds // MANY,),
        in_specs=[by_kind(0, planes, rows, depth)],
        out_specs=[
            by_kind(0, 2, rows, depth),
            by_kind(0, 2, rows, depth),
            by_kind(0, planes, 2, depth),
            by_kind(0, planes, 2, depth),
        ],
        out_shape=[
            shaped(kinds, 2, rows, depth),
            shaped(kinds, 2, rows, depth),
            shaped(kinds, planes, 2, depth),
            shaped(kinds, planes, 2, depth),
        ],
        compiler_params=limit,
        name="rims",
    )(species_cut)
    field_lo = lax.ppermute(top, "space", ahead)
    field_hi = lax.ppermute(bottom, "space", back)
    width = capacity // 8 * 9 + ROWS_WIDTH
    sent = pl.pallas_call(
        assemble_kernel,
        grid=(1,),
        in_specs=[
            whole((8, capacity // 8 * 9)),
            whole((6, 1, rows, depth)),
            whole((planes, rows, depth)),
            whole((planes, rows, depth)),
            whole((3, planes, rows, depth)),
            whole((1, planes, rows, depth)),
            whole((6, 1, rows, depth)),
        ],
        out_specs=whole((8, width)),
        out_shape=shaped(8, width),
        compiler_params=limit,
        name="assemble",
    )(packed, field_lo, gas_temp, gas_density, gas_velocity, species, field_hi)
    sent, x_up, x_down, y_right, y_left = lax.optimization_barrier(
        (sent, x_up, x_down, y_right, y_left)
    )
    parcels = lax.all_gather(sent, "group", axis=0)

    x_up, x_down, y_right, y_left, parcels = lax.optimization_barrier(
        (x_up, x_down, y_right, y_left, parcels)
    )
    x_lo = lax.ppermute(x_up, "space", ahead)
    x_hi = lax.ppermute(x_down, "space", back)
    y_lo = lax.ppermute(y_right, "group", g_ahead)

    chunks = pl.cdiv(slots, CHUNK)
    reach = max(chunks * CHUNK, slots + WINDOW)
    main, dep_lo, dep_hi, state, dst, off = pl.pallas_call(
        parcel_kernel,
        grid=(1,),
        in_specs=[
            smem,
            whole((groups, 8, width)),
            whole((6, 1, rows, depth)),
            whole((planes, rows, depth)),
            whole((planes, rows, depth)),
            whole((3, planes, rows, depth)),
            whole((1, planes, rows, depth)),
            whole((6, 1, rows, depth)),
        ],
        out_specs=[
            whole((7, planes, rows, depth)),
            whole((7, 1, rows, depth)),
            whole((7, 1, rows, depth)),
            whole((8, reach)),
            whole((blocks, LANES)),
            whole((8, LANES)),
        ],
        out_shape=[
            shaped(7, planes, rows, depth),
            shaped(7, 1, rows, depth),
            shaped(7, 1, rows, depth),
            shaped(8, reach),
            shaped(blocks, LANES),
            jax.ShapeDtypeStruct((8, LANES), jnp.int32),
        ],
        scratch_shapes=[
            pltpu.VMEM((blocks, LANES), F32),
            pltpu.VMEM((blocks, LANES), F32),
            pltpu.SMEM((8, LANES), jnp.int32),
            pltpu.SemaphoreType.DMA,
            pltpu.VMEM((32, slots), BF16),
            pltpu.VMEM((16, reach), F32),
            pltpu.VMEM((256, LANES), F32),
            pltpu.VMEM((6 * LANES, 768), BF16),
            pltpu.VMEM((chunks, 256, CHUNK), BF16),
            pltpu.VMEM((chunks, 256, CHUNK), BF16),
            pltpu.VMEM((8, reach), F32),
            pltpu.VMEM((8, reach), F32),
            pltpu.VMEM((7 * LANES, 256), F32),
        ],
        compiler_params=limit,
        name="parcels",
    )(info, parcels, field_lo, gas_temp, gas_density, gas_velocity, species, field_hi)

    y_lo, y_left, state = lax.optimization_barrier((y_lo, y_left, state))
    y_hi = lax.ppermute(y_left, "group", g_back)

    from_below = lax.ppermute(dep_hi, "space", ahead)
    from_above = lax.ppermute(dep_lo, "space", back)

    spread = pl.pallas_call(
        spread_kernel,
        grid=(1,),
        in_specs=[smem, whole((blocks, LANES)), whole((8, reach))],
        out_specs=whole((groups, 8, capacity)),
        out_shape=shaped(groups, 8, capacity),
        scratch_shapes=[pltpu.VMEM((16, reach), BF16)],
        compiler_params=limit,
        name="spread",
    )(off, dst, state)
    y_lo, y_hi, from_below, from_above, spread = lax.optimization_barrier(
        (y_lo, y_hi, from_below, from_above, spread)
    )
    returned = lax.all_to_all(spread, "group", 0, 0)
    gas = pl.BlockSpec((planes, rows, depth), lambda i: (0, 0, 0))
    row0 = pl.BlockSpec((None, planes, rows, depth), lambda i: (0, 0, 0, 0))
    all_gas = whole((7, planes, rows, depth))
    rim = whole((7, 1, rows, depth))
    species_next = gas_sources = None
    at = 0
    for c, size in enumerate(PARTS):
        first = at // MANY
        at += size
        out_specs = [by_kind(first, planes, rows, depth)]
        out_shape = [shaped(*species.shape)]
        if c == 0:
            extra, extra_specs = (main, from_below, from_above), [all_gas, rim, rim]
            out_specs.append(all_gas)
            out_shape.append(shaped(7, planes, rows, depth))
        else:
            extra, extra_specs = (gas_sources, species_next), [row0, hbm]
        got = pl.pallas_call(
            functools.partial(transport_kernel, c == 0, first),
            grid=(size // MANY,),
            in_specs=[
                smem,
                by_kind(first, planes, rows, depth),
                by_kind(first, 2, rows, depth),
                by_kind(first, 2, rows, depth),
                by_kind(first, planes, 2, depth),
                by_kind(first, planes, 2, depth),
                row0,
                gas,
            ]
            + extra_specs,
            out_specs=out_specs,
            out_shape=out_shape,
            input_output_aliases={} if c == 0 else {9: 0},
            scratch_shapes=[pltpu.VMEM((MANY, rows + 16, depth), F32)],
            compiler_params=limit,
            name="transport",
        )(diffusion, species, x_lo, x_hi, y_lo, y_hi, gas_velocity, gas_density, *extra)
        species_next = got[0]
        if c == 0:
            gas_sources = got[1]
    species_next, returned = lax.optimization_barrier((species_next, returned))
    parcel_state = pl.pallas_call(
        state_kernel,
        grid=(1,),
        in_specs=[
            smem,
            whole((groups, 8, capacity)),
            whole((capacity,)),
            whole((capacity,)),
            whole((3, capacity)),
        ],
        out_specs=whole((5, capacity)),
        out_shape=shaped(5, capacity),
        compiler_params=limit,
        name="state",
    )(info, returned, drop_radius, drop_temp, drop_velocity)
    return (species_next, gas_sources, parcel_state)


def solution(mesh):
    in_specs = (
        P(None, "space", "group", None),
        P(),
        P("space", "group", None),
        P("space", "group", None),
        P(None, "space", "group", None),
        P(("space", "group")),
        P(("space", "group")),
        P(None, ("space", "group")),
        P(None, ("space", "group")),
        P(None, ("space", "group")),
        P("space"),
    )
    out_specs = (
        P(None, "space", "group", None),
        P(None, "space", "group", None),
        P(None, ("space", "group")),
    )
    return jax.shard_map(
        per_device, mesh=mesh, in_specs=in_specs, out_specs=out_specs, check_vma=False
    )
```

```python
import functools

import jax
import jax.numpy as jnp
from jax import lax
from jax.experimental import pallas as pl
from jax.experimental.pallas import tpu as pltpu
from jax.sharding import PartitionSpec as P

time_step = 0.05
evap_coef = 0.5
heat_coef = 0.15
latent_coef = 0.2
enthalpy_coef = 1.3
source_coef = 0.5
courant = 0.3

LANES = 128
PARTS = (54,)
MANY = 18
CHUNK = 1536
WINDOW = 256
YPAD = 40
OWN_ROWS = 48
RIM_ROWS = 24
ROWS_WIDTH = (OWN_ROWS + RIM_ROWS) // 8 * LANES
F32 = jnp.float32
BF16 = jnp.bfloat16
NT = (((1,), (1,)), ((), ()))


def halves(value):
    high = value.astype(BF16)
    return high, (value - high.astype(F32)).astype(BF16)


def hat(index, start, fraction):
    away = index - start
    return jnp.where(away == 0.0, 1.0 - fraction, jnp.where(away == 1.0, fraction, 0.0))


def iota(shape, dim):
    return lax.broadcasted_iota(jnp.int32, shape, dim)


def one_hot(dst_row, aligned):
    rel = jnp.broadcast_to(dst_row - aligned.astype(F32), (16, LANES)).astype(BF16)
    rel = jnp.concatenate([rel] * (WINDOW // 16), axis=0)
    places = iota((WINDOW, LANES), 0).astype(F32).astype(BF16)
    return jnp.where(places == rel, jnp.ones_like(rel), jnp.zeros_like(rel))


def cells_of(width):
    return (width - ROWS_WIDTH) // 9 * 8


def physics(interp, radius, drop_temp, velocity):
    heat, density, speed, fuel = interp[0], interp[1], interp[2:5], interp[5]
    slip = [g - v for g, v in zip(speed, velocity)]
    slip_square = slip[0] * slip[0] + slip[1] * slip[1] + slip[2] * slip[2]
    log_flow = jnp.log(1.0 + density * radius * slip_square)
    sherwood = 2.0 + 0.6 * jnp.exp(0.25 * log_flow)
    surface = 0.5 / (1.0 + jnp.exp(-4.0 * (drop_temp - 1.0)))
    evap = evap_coef * radius * density * sherwood * jnp.log((1.0 - fuel) / (1.0 - surface))
    mass = radius * radius * radius
    ratio = 1.0 - time_step * evap / mass
    new_radius = radius * jnp.exp(jnp.log(ratio) * (1.0 / 3.0))
    rate = time_step * (1.0 + 0.15 * jnp.exp(0.35 * log_flow)) / (2.0 * radius * radius)
    change = [rate * s for s in slip]
    new_velocity = [v + c for v, c in zip(velocity, change)]
    heat_rate = heat_coef * sherwood / (radius * radius)
    new_temp = drop_temp + time_step * (
        heat_rate * (heat - drop_temp) - latent_coef * evap / mass
    )
    vapour = time_step * evap
    lost = [mass * (v - n) for v, n in zip(velocity, new_velocity)]
    momentum = [m + vapour * v for m, v in zip(lost, velocity)]
    heat_gain = -time_step * mass * heat_rate * (heat - drop_temp)
    enthalpy = enthalpy_coef * vapour * new_temp
    drag = lost[0] * speed[0] + lost[1] * speed[1] + lost[2] * speed[2]
    return [new_radius, new_temp] + new_velocity, [vapour] + momentum + [heat_gain, enthalpy, drag]


def parcel_kernel(
    count_ref,
    pk_ref,
    lo_ref,
    temp_ref,
    dens_ref,
    vel_ref,
    fuel_ref,
    hi_ref,
    main_ref,
    dlo_ref,
    dhi_ref,
    state_ref,
    own_dst_ref,
    off_ref,
    dst_ref,
    cell_scr,
    off_smem,
    sem,
    pieces,
    cv,
    row_scr,
    ft,
    a_hi,
    a_lo,
    interp,
    src,
    dep,
):
    groups = pk_ref.shape[0]
    each = cells_of(pk_ref.shape[2]) // 8
    capacity = each * 8
    slots = groups * capacity
    blocks = slots // LANES
    count, group = count_ref[0], lax.axis_index("group")

    per_line = each // LANES
    for b in range(blocks):
        q, r = divmod(b, capacity // LANES)
        line, at = divmod(r, per_line)
        at = capacity + at * LANES
        cell_scr[b : b + 1, :] = pk_ref[q, line : line + 1, at : at + LANES]
    cell = cell_scr[...].astype(jnp.int32)
    slot = iota((blocks, LANES), 0) * LANES + iota((blocks, LANES), 1)
    y_of = ((cell >> 7) & 127) - group * 32
    mine = jnp.logical_and(slot < count, jnp.logical_and(y_of >= -1, y_of < 32))
    ones = jnp.where(mine, 1.0, 0.0).astype(BF16)
    before = jnp.where(iota((LANES, LANES), 0) < iota((LANES, LANES), 1), 1.0, 0.0).astype(BF16)
    after = jnp.where(iota((LANES, LANES), 1) < iota((LANES, LANES), 0), 1.0, 0.0).astype(BF16)
    full = jnp.ones((LANES, LANES), BF16)
    within = jnp.dot(ones, before, preferred_element_type=F32)
    row_sum = jnp.dot(ones, full, preferred_element_type=F32).astype(BF16)
    offset = jnp.dot(after, row_sum, preferred_element_type=F32)
    dst = jnp.where(mine, within + offset, -1.0)
    dst_ref[...] = dst
    own_dst_ref[...] = jnp.where(y_of >= 0, dst, -1.0)
    counts = lax.dot_general(jnp.ones((16, LANES), BF16), ones, NT, preferred_element_type=F32)
    counts = counts.astype(BF16)
    starts = jnp.dot(counts, before, preferred_element_type=F32)
    total = jnp.dot(counts, full, preferred_element_type=F32)
    first = iota((8, LANES), 0) == 0
    off_ref[...] = jnp.where(first, starts[0:8], total[0:8]).astype(jnp.int32)
    copy = pltpu.make_async_copy(off_ref, off_smem, sem)
    copy.start()

    def split(q, carry):
        for line in range(8):
            cells = pk_ref[q, line : line + 1, capacity : capacity + each]
            cells = jnp.broadcast_to(cells, (8, each)).astype(jnp.int32)
            row = iota((8, each), 0)
            y_place = ((cells >> 7) & 127) - group * 32
            place = jnp.where(row == 0, cells >> 14, jnp.where(row == 1, y_place, cells & 127))
            values = pk_ref[q, :, line * each : (line + 1) * each]
            high, low = halves(jnp.concatenate([values, place.astype(F32)], axis=0))
            at = pl.ds(pl.multiple_of(q * capacity + line * each, each), each)
            pieces[0:16, at] = high
            pieces[16:32, at] = low
        return carry

    lax.fori_loop(0, groups, split, 0)

    zero = jnp.zeros((256, LANES), F32)
    own = [temp_ref, dens_ref, vel_ref.at[0], vel_ref.at[1], vel_ref.at[2], fuel_ref.at[0]]
    planes = temp_ref.shape[0]
    rows = temp_ref.shape[1]
    row_start = capacity + each
    after_me = jnp.minimum(group + 1, groups - 1)
    before_me = jnp.maximum(group - 1, 0)
    for f in range(6):
        row_scr[...] = zero
        for x in range(planes + 2):
            if x == 0:
                block = lo_ref[f, 0]
            elif x == planes + 1:
                block = hi_ref[f, 0]
            else:
                block = own[f][x - 1]
            row_scr[x * YPAD : x * YPAD + rows, :] = block
            block, line = row_place(planes, f, x, 0)
            at = row_start + block * LANES
            following = pk_ref[after_me, line : line + 1, at : at + LANES]
            row_scr[x * YPAD + rows : x * YPAD + rows + 1, :] = following
            block, line = row_place(planes, f, x, 1)
            at = row_start + block * LANES
            former = pk_ref[before_me, line : line + 1, at : at + LANES]
            row_scr[(x + 1) * YPAD - 1 : (x + 1) * YPAD, :] = former
        high, low = halves(row_scr[...].T)
        at = slice(f * LANES, (f + 1) * LANES)
        ft[at, 0:256] = high
        ft[at, 256:512] = low
        ft[at, 512:768] = high

    cv[...] = jnp.zeros(cv.shape, F32)
    state_ref[...] = jnp.zeros(state_ref.shape, F32)
    dep[...] = jnp.zeros(dep.shape, F32)
    copy.wait()
    live = off_smem[1, 0]

    def compact(i, carry):
        got = []
        for j in range(8):
            b = i * 8 + j
            aligned = (off_smem[0, b] >> 7) << 7
            hot = one_hot(dst_ref[pl.ds(b, 1), :], aligned)
            block = pieces[:, pl.ds(pl.multiple_of(b * LANES, LANES), LANES)]
            got.append((aligned, lax.dot_general(block, hot, NT, preferred_element_type=F32)))
        for aligned, both in got:
            at = pl.ds(pl.multiple_of(aligned, LANES), WINDOW)
            cv[:, at] += both[0:16] + both[16:32]
        return carry

    lax.fori_loop(0, blocks // 8, compact, 0)

    def gather(c, carry):
        at = pl.ds(pl.multiple_of(c * CHUNK, CHUNK), CHUNK)
        valid = c * CHUNK + iota((1, CHUNK), 1) < live
        fx, fy, fz = cv[0:1, at], cv[1:2, at], cv[2:3, at]
        x0, z0 = cv[8:9, at], cv[10:11, at]
        y0 = jnp.where(valid, cv[9:10, at], 1000.0)
        line = iota((YPAD, CHUNK), 0)
        wy = hat(jnp.where(line == YPAD - 1, -1, line).astype(F32), y0, fy)
        parts = [wy * hat(float(x), x0, fx) for x in range(planes + 2)]
        parts.append(jnp.zeros((256 - (planes + 2) * YPAD, CHUNK), F32))
        high, low = halves(jnp.concatenate(parts, axis=0))
        a_hi[c] = high
        a_lo[c] = low
        stacked = jnp.concatenate([high, high, low], axis=0)
        lines = jnp.dot(ft[...], stacked, preferred_element_type=F32)
        wz = hat(iota((LANES, CHUNK), 0).astype(F32), z0, fz)
        for f in range(6):
            interp[f : f + 1, at] = jnp.sum(
                lines[f * LANES : (f + 1) * LANES] * wz, axis=0, keepdims=True
            )
        return carry

    chunks = (live + CHUNK - 1) // CHUNK
    lax.fori_loop(0, chunks, gather, 0)

    def step(c, carry):
        at = pl.ds(pl.multiple_of(c * CHUNK, CHUNK), CHUNK)
        valid = c * CHUNK + iota((1, CHUNK), 1) < live
        inside = [jnp.where(valid, interp[f : f + 1, at], 0.0) for f in range(6)]
        radius = jnp.where(valid, cv[3:4, at], 1.0)
        velocity = [cv[d : d + 1, at] for d in (5, 6, 7)]
        new, sources = physics(inside, radius, cv[4:5, at], velocity)
        for s in range(5):
            state_ref[s : s + 1, at] = jnp.where(valid, new[s], 0.0)
        for k in range(7):
            src[k : k + 1, at] = jnp.where(valid, sources[k], 0.0)
        return carry

    lax.fori_loop(0, (live + CHUNK - 1) // CHUNK, step, 0)

    def deposit(c, carry):
        at = pl.ds(pl.multiple_of(c * CHUNK, CHUNK), CHUNK)
        wz = hat(iota((LANES, CHUNK), 0).astype(F32), cv[10:11, at], cv[2:3, at])
        high, low = halves(jnp.concatenate([wz * src[k : k + 1, at] for k in range(7)], axis=0))
        left = jnp.concatenate([high, low, high], axis=1)
        right = jnp.concatenate([a_hi[c], a_hi[c], a_lo[c]], axis=1)
        dep[...] += lax.dot_general(left, right, NT, preferred_element_type=F32)
        return carry

    lax.fori_loop(0, chunks, deposit, 0)

    for k in range(7):
        cells = dep[k * LANES : (k + 1) * LANES, :].T
        for x in range(planes + 2):
            block = cells[x * YPAD : x * YPAD + rows]
            if x == 0:
                dlo_ref[k, 0] = block
            elif x == planes + 1:
                dhi_ref[k, 0] = block
            else:
                main_ref[k, x - 1] = block


def spread_kernel(off_ref, dst_ref, state_ref, *outs_and_scratch):
    both_scr = outs_and_scratch[-1]
    high, low = halves(state_ref[...])
    both_scr[0:16, :] = jnp.concatenate([high, low], axis=0)
    outs = outs_and_scratch[:-1]
    group = lax.axis_index("group")
    each = dst_ref.shape[0] // len(outs)
    for d, out in enumerate(outs):
        owner = lax.rem(group + d, len(outs))

        def spread(i, carry, owner=owner, out=out):
            for j in range(8):
                b = owner * each + i * 8 + j
                aligned = (off_ref[0, b] >> 7) << 7
                hot = one_hot(dst_ref[pl.ds(b, 1), :], aligned)
                block = both_scr[:, pl.ds(pl.multiple_of(aligned, LANES), WINDOW)]
                got = jnp.dot(block, hot, preferred_element_type=F32)
                at = pl.ds(pl.multiple_of((i * 8 + j) * LANES, LANES), LANES)
                out[:, at] = got[0:8] + got[8:16]
            return carry

        lax.fori_loop(0, each // 8, spread, 0)


def pack_kernel(
    cells_ref,
    weights_ref,
    radius_ref,
    temp_ref,
    velocity_ref,
    gas_temp_ref,
    dens_ref,
    vel_ref,
    fuel_ref,
    packed_ref,
    top_ref,
    bottom_ref,
):
    planes = gas_temp_ref.shape[0]
    own = [gas_temp_ref, dens_ref, vel_ref.at[0], vel_ref.at[1], vel_ref.at[2], fuel_ref.at[0]]
    for f in range(6):
        top_ref[f, 0] = own[f][planes - 1]
        bottom_ref[f, 0] = own[f][0]
    w = [weights_ref[c : c + 1, :] for c in range(8)]
    slots = cells_ref.shape[1]
    each = slots // 8
    packed_ref[0:1, 0:slots] = (w[4] + w[5]) + (w[6] + w[7])
    packed_ref[1:2, 0:slots] = (w[2] + w[3]) + (w[6] + w[7])
    packed_ref[2:3, 0:slots] = (w[1] + w[3]) + (w[5] + w[7])
    packed_ref[3:4, 0:slots] = radius_ref[...].reshape(1, -1)
    packed_ref[4:5, 0:slots] = temp_ref[...].reshape(1, -1)
    packed_ref[5:8, 0:slots] = velocity_ref[...]
    for i in range(8):
        first = cells_ref[0:1, i * each : (i + 1) * each]
        packed_ref[i : i + 1, slots : slots + each] = first.astype(F32)
    rows = gas_temp_ref.shape[1]
    for f in range(6):
        for x in range(planes):
            for side, y in enumerate((0, rows - 1)):
                block, line = row_place(planes, f, x + 1, side)
                at = slots + each + block * LANES
                packed_ref[line : line + 1, at : at + LANES] = own[f][x, y : y + 1, :]


def rims_kernel(species_ref, up_ref, down_ref, right_ref, left_ref):
    planes, rows = species_ref.shape[1:3]
    up_ref[...] = species_ref[:, planes - 2 : planes]
    down_ref[...] = species_ref[:, 0:2]
    right_ref[...] = species_ref[:, :, rows - 2 : rows]
    left_ref[...] = species_ref[:, :, 0:2]


def assemble_kernel(packed_ref, lo_ref, hi_ref, out_ref):
    planes = OWN_ROWS // 12
    rows = lo_ref.shape[2]
    for f in range(6):
        for x, plane in ((0, lo_ref.at[f, 0]), (planes + 1, hi_ref.at[f, 0])):
            for side, y in enumerate((0, rows - 1)):
                block, line = row_place(planes, f, x, side)
                at = (block - OWN_ROWS // 8) * LANES
                out_ref[line : line + 1, at : at + LANES] = plane[y : y + 1, :]


def row_place(planes, f, x, side):
    if 0 < x <= planes:
        return divmod((f * planes + x - 1) * 2 + side, 8)
    return divmod(planes * 12 + (f * 2 + (x > 0)) * 2 + side, 8)


def transport_kernel(
    first_part,
    first_block,
    diff_ref,
    y_ref,
    xlo_ref,
    xhi_ref,
    ylo_ref,
    yhi_ref,
    ux_ref,
    dens_ref,
    *rest,
):
    if first_part:
        main_ref, below_ref, above_ref, out_ref, gas_ref, pad = rest

        @pl.when(pl.program_id(0) == 0)
        def _():
            last = main_ref.shape[1] - 1
            for k in range(main_ref.shape[0]):
                for x in range(last + 1):
                    total = main_ref[k, x]
                    if x == 0:
                        total = total + below_ref[k, 0]
                    if x == last:
                        total = total + above_ref[k, 0]
                    gas_ref[k, x] = total

        vap_ref = gas_ref.at[0]
    else:
        vap_ref, _, out_ref, pad = rest
    species, planes, rows, depth = y_ref.shape
    at = iota((rows, depth), 1)
    left1 = jnp.where(at >= 1, 16.0, 0.0)
    left2 = jnp.where(at >= 2, -1.0, 0.0)
    right1 = jnp.where(at < depth - 1, 16.0, 0.0)
    right2 = jnp.where(at < depth - 2, -1.0, 0.0)
    first = (first_block + pl.program_id(0)) * species
    for x in range(planes):
        speed = ux_ref[x] * (courant / 12.0)
        gain = source_coef * vap_ref[x] / dens_ref[x]

        for s in range(species):
            d12 = diff_ref[first + s] * (1.0 / 12.0)

            def plane(i, s=s):
                if i < 0:
                    return xlo_ref[s, i + 2]
                if i >= planes:
                    return xhi_ref[s, i - planes]
                return y_ref[s, i]

            center = plane(x)
            up1, up2, dn1, dn2 = plane(x + 1), plane(x + 2), plane(x - 1), plane(x - 2)
            pad[s, 6:8, :] = ylo_ref[s, x]
            pad[s, 8 : 8 + rows, :] = center
            pad[s, 8 + rows : 10 + rows, :] = yhi_ref[s, x]
            near = up1 + dn1 + pad[s, 7 : 7 + rows, :] + pad[s, 9 : 9 + rows, :]
            far = up2 + dn2 + pad[s, 6 : 6 + rows, :] + pad[s, 10 : 10 + rows, :]
            along = (
                left1 * pltpu.roll(center, 1, 1)
                + right1 * pltpu.roll(center, depth - 1, 1)
                + left2 * pltpu.roll(center, 2, 1)
                + right2 * pltpu.roll(center, depth - 2, 1)
            )
            slope = 8.0 * (up1 - dn1) - (up2 - dn2)
            flag = jnp.where(first + s == 0, 1.0, 0.0)
            laplace = 16.0 * near - far + along - 90.0 * center
            out_ref[s, x] = center + d12 * laplace - speed * slope + gain * (flag - center)


def per_device(
    species,
    diffusion,
    gas_temp,
    gas_density,
    gas_velocity,
    drop_radius,
    drop_temp,
    drop_velocity,
    parcel_cells,
    parcel_weights,
    parcel_counts,
):
    count_s = lax.axis_size("space")
    groups = lax.axis_size("group")
    planes, rows, depth = gas_temp.shape
    kinds = species.shape[0]
    capacity = drop_radius.shape[0]
    slots = capacity * groups
    blocks = slots // LANES
    ahead = [(i, i + 1) for i in range(count_s - 1)]
    back = [(b, a) for a, b in ahead]
    g_ahead = [(i, i + 1) for i in range(groups - 1)]
    g_back = [(b, a) for a, b in g_ahead]

    whole = lambda shape: pl.BlockSpec(shape, lambda i, n=len(shape): (0,) * n)
    smem = pl.BlockSpec(memory_space=pltpu.SMEM)
    hbm = pl.BlockSpec(memory_space=pl.ANY)
    shaped = lambda *shape: jax.ShapeDtypeStruct(shape, F32)
    limit = pltpu.CompilerParams(vmem_limit_bytes=62 * 2**20)

    def by_kind(first, *shape):
        return pl.BlockSpec((MANY,) + shape, lambda i: (first + i, 0, 0, 0))

    width = capacity // 8 * 9 + ROWS_WIDTH
    packed, top, bottom = pl.pallas_call(
        pack_kernel,
        grid=(1,),
        in_specs=[
            whole((8, capacity)),
            whole((8, capacity)),
            whole((capacity,)),
            whole((capacity,)),
            whole((3, capacity)),
            whole((planes, rows, depth)),
            whole((planes, rows, depth)),
            whole((3, planes, rows, depth)),
            whole((1, planes, rows, depth)),
        ],
        out_specs=[
            whole((8, width)),
            whole((6, 1, rows, depth)),
            whole((6, 1, rows, depth)),
        ],
        out_shape=[
            shaped(8, width),
            shaped(6, 1, rows, depth),
            shaped(6, 1, rows, depth),
        ],
        compiler_params=limit,
        name="pack",
    )(
        parcel_cells, parcel_weights, drop_radius, drop_temp, drop_velocity,
        gas_temp, gas_density, gas_velocity, species,
    )
    species_cut, packed = lax.optimization_barrier((species, packed))
    x_up, x_down, y_right, y_left = pl.pallas_call(
        rims_kernel,
        grid=(kinds // MANY,),
        in_specs=[by_kind(0, planes, rows, depth)],
        out_specs=[
            by_kind(0, 2, rows, depth),
            by_kind(0, 2, rows, depth),
            by_kind(0, planes, 2, depth),
            by_kind(0, planes, 2, depth),
        ],
        out_shape=[
            shaped(kinds, 2, rows, depth),
            shaped(kinds, 2, rows, depth),
            shaped(kinds, planes, 2, depth),
            shaped(kinds, planes, 2, depth),
        ],
        compiler_params=limit,
        name="rims",
    )(species_cut)
    field_lo = lax.ppermute(top, "space", ahead)
    field_hi = lax.ppermute(bottom, "space", back)
    tail = RIM_ROWS // 8 * LANES
    sent = pl.pallas_call(
        assemble_kernel,
        grid=(1,),
        in_specs=[hbm, whole((6, 1, rows, depth)), whole((6, 1, rows, depth))],
        out_specs=pl.BlockSpec((8, tail), lambda i: (0, width // tail - 1)),
        out_shape=shaped(8, width),
        input_output_aliases={0: 0},
        compiler_params=limit,
        name="assemble",
    )(packed, field_lo, field_hi)
    sent, x_up, x_down, y_right, y_left = lax.optimization_barrier(
        (sent, x_up, x_down, y_right, y_left)
    )
    parcels = lax.all_gather(sent, "group", axis=0)

    x_up, x_down, y_right, y_left, parcels = lax.optimization_barrier(
        (x_up, x_down, y_right, y_left, parcels)
    )
    x_lo = lax.ppermute(x_up, "space", ahead)
    x_hi = lax.ppermute(x_down, "space", back)
    y_lo = lax.ppermute(y_right, "group", g_ahead)

    chunks = pl.cdiv(slots, CHUNK)
    reach = max(chunks * CHUNK, slots + WINDOW)
    main, dep_lo, dep_hi, state, dst, off = pl.pallas_call(
        parcel_kernel,
        grid=(1,),
        in_specs=[
            smem,
            whole((groups, 8, width)),
            whole((6, 1, rows, depth)),
            whole((planes, rows, depth)),
            whole((planes, rows, depth)),
            whole((3, planes, rows, depth)),
            whole((1, planes, rows, depth)),
            whole((6, 1, rows, depth)),
        ],
        out_specs=[
            whole((7, planes, rows, depth)),
            whole((7, 1, rows, depth)),
            whole((7, 1, rows, depth)),
            whole((8, reach)),
            whole((blocks, LANES)),
            whole((8, LANES)),
        ],
        out_shape=[
            shaped(7, planes, rows, depth),
            shaped(7, 1, rows, depth),
            shaped(7, 1, rows, depth),
            shaped(8, reach),
            shaped(blocks, LANES),
            jax.ShapeDtypeStruct((8, LANES), jnp.int32),
        ],
        scratch_shapes=[
            pltpu.VMEM((blocks, LANES), F32),
            pltpu.VMEM((blocks, LANES), F32),
            pltpu.SMEM((8, LANES), jnp.int32),
            pltpu.SemaphoreType.DMA,
            pltpu.VMEM((32, slots), BF16),
            pltpu.VMEM((16, reach), F32),
            pltpu.VMEM((256, LANES), F32),
            pltpu.VMEM((6 * LANES, 768), BF16),
            pltpu.VMEM((chunks, 256, CHUNK), BF16),
            pltpu.VMEM((chunks, 256, CHUNK), BF16),
            pltpu.VMEM((8, reach), F32),
            pltpu.VMEM((8, reach), F32),
            pltpu.VMEM((7 * LANES, 256), F32),
        ],
        compiler_params=limit,
        name="parcels",
    )(parcel_counts, parcels, field_lo, gas_temp, gas_density, gas_velocity, species, field_hi)

    y_lo, y_left, state = lax.optimization_barrier((y_lo, y_left, state))
    y_hi = lax.ppermute(y_left, "group", g_back)

    from_below = lax.ppermute(dep_hi, "space", ahead)
    from_above = lax.ppermute(dep_lo, "space", back)

    spread = pl.pallas_call(
        spread_kernel,
        grid=(1,),
        in_specs=[smem, whole((blocks, LANES)), whole((8, reach))],
        out_specs=[whole((8, capacity))] * groups,
        out_shape=[shaped(8, capacity)] * groups,
        scratch_shapes=[pltpu.VMEM((16, reach), BF16)],
        compiler_params=limit,
        name="spread",
    )(off, dst, state)
    y_lo, y_hi, from_below, from_above, spread = lax.optimization_barrier(
        (y_lo, y_hi, from_below, from_above, spread)
    )
    returned = [spread[0]]
    for d in range(1, groups):
        route = [(i, (i + d) % groups) for i in range(groups)]
        returned.append(lax.ppermute(spread[d], "group", route))
    gas = pl.BlockSpec((planes, rows, depth), lambda i: (0, 0, 0))
    row0 = pl.BlockSpec((None, planes, rows, depth), lambda i: (0, 0, 0, 0))
    all_gas = whole((7, planes, rows, depth))
    rim = whole((7, 1, rows, depth))
    species_next = gas_sources = None
    at = 0
    for c, size in enumerate(PARTS):
        first = at // MANY
        at += size
        out_specs = [by_kind(first, planes, rows, depth)]
        out_shape = [shaped(*species.shape)]
        if c == 0:
            extra, extra_specs = (main, from_below, from_above), [all_gas, rim, rim]
            out_specs.append(all_gas)
            out_shape.append(shaped(7, planes, rows, depth))
        else:
            extra, extra_specs = (gas_sources, species_next), [row0, hbm]
        got = pl.pallas_call(
            functools.partial(transport_kernel, c == 0, first),
            grid=(size // MANY,),
            in_specs=[
                smem,
                by_kind(first, planes, rows, depth),
                by_kind(first, 2, rows, depth),
                by_kind(first, 2, rows, depth),
                by_kind(first, planes, 2, depth),
                by_kind(first, planes, 2, depth),
                row0,
                gas,
            ]
            + extra_specs,
            out_specs=out_specs,
            out_shape=out_shape,
            input_output_aliases={} if c == 0 else {9: 0},
            scratch_shapes=[pltpu.VMEM((MANY, rows + 16, depth), F32)],
            compiler_params=limit,
            name="transport",
        )(diffusion, species, x_lo, x_hi, y_lo, y_hi, gas_velocity, gas_density, *extra)
        species_next = got[0]
        if c == 0:
            gas_sources = got[1]
    species_next, returned = lax.optimization_barrier((species_next, returned))
    new_state = sum(returned[1:], returned[0])
    old_state = jnp.concatenate([drop_radius[None], drop_temp[None], drop_velocity], axis=0)
    slot = lax.axis_index("group") * capacity + jnp.arange(capacity, dtype=jnp.int32)
    live = slot < parcel_counts[0]
    parcel_state = jnp.where(live[None], new_state[0:5], old_state)
    return (species_next, gas_sources, parcel_state)


def solution(mesh):
    in_specs = (
        P(None, "space", "group", None),
        P(),
        P("space", "group", None),
        P("space", "group", None),
        P(None, "space", "group", None),
        P(("space", "group")),
        P(("space", "group")),
        P(None, ("space", "group")),
        P(None, ("space", "group")),
        P(None, ("space", "group")),
        P("space"),
    )
    out_specs = (
        P(None, "space", "group", None),
        P(None, "space", "group", None),
        P(None, ("space", "group")),
    )
    return jax.shard_map(
        per_device, mesh=mesh, in_specs=in_specs, out_specs=out_specs, check_vma=False
    )
```

```python
import functools

import jax
import jax.numpy as jnp
from jax import lax
from jax.experimental import pallas as pl
from jax.experimental.pallas import tpu as pltpu
from jax.sharding import PartitionSpec as P

time_step = 0.05
evap_coef = 0.5
heat_coef = 0.15
latent_coef = 0.2
enthalpy_coef = 1.3
source_coef = 0.5
courant = 0.3

LANES = 128
PARTS = (54,)
MANY = 18
CHUNK = 1536
WINDOW = 256
YPAD = 40
OWN_ROWS = 48
RIM_ROWS = 24
ROWS_WIDTH = (OWN_ROWS + RIM_ROWS) // 8 * LANES
F32 = jnp.float32
BF16 = jnp.bfloat16
NT = (((1,), (1,)), ((), ()))


def halves(value):
    high = value.astype(BF16)
    return high, (value - high.astype(F32)).astype(BF16)


def hat(index, start, fraction):
    away = index - start
    return jnp.where(away == 0.0, 1.0 - fraction, jnp.where(away == 1.0, fraction, 0.0))


def iota(shape, dim):
    return lax.broadcasted_iota(jnp.int32, shape, dim)


def one_hot(dst_row, aligned):
    rel = jnp.broadcast_to(dst_row - aligned.astype(F32), (16, LANES)).astype(BF16)
    rel = jnp.concatenate([rel] * (WINDOW // 16), axis=0)
    places = iota((WINDOW, LANES), 0).astype(F32).astype(BF16)
    return jnp.where(places == rel, jnp.ones_like(rel), jnp.zeros_like(rel))


def cells_of(width):
    return (width - ROWS_WIDTH) // 9 * 8


def physics(interp, radius, drop_temp, velocity):
    heat, density, speed, fuel = interp[0], interp[1], interp[2:5], interp[5]
    slip = [g - v for g, v in zip(speed, velocity)]
    slip_square = slip[0] * slip[0] + slip[1] * slip[1] + slip[2] * slip[2]
    log_flow = jnp.log(1.0 + density * radius * slip_square)
    sherwood = 2.0 + 0.6 * jnp.exp(0.25 * log_flow)
    surface = 0.5 / (1.0 + jnp.exp(-4.0 * (drop_temp - 1.0)))
    evap = evap_coef * radius * density * sherwood * jnp.log((1.0 - fuel) / (1.0 - surface))
    mass = radius * radius * radius
    ratio = 1.0 - time_step * evap / mass
    new_radius = radius * jnp.exp(jnp.log(ratio) * (1.0 / 3.0))
    rate = time_step * (1.0 + 0.15 * jnp.exp(0.35 * log_flow)) / (2.0 * radius * radius)
    change = [rate * s for s in slip]
    new_velocity = [v + c for v, c in zip(velocity, change)]
    heat_rate = heat_coef * sherwood / (radius * radius)
    new_temp = drop_temp + time_step * (
        heat_rate * (heat - drop_temp) - latent_coef * evap / mass
    )
    vapour = time_step * evap
    lost = [mass * (v - n) for v, n in zip(velocity, new_velocity)]
    momentum = [m + vapour * v for m, v in zip(lost, velocity)]
    heat_gain = -time_step * mass * heat_rate * (heat - drop_temp)
    enthalpy = enthalpy_coef * vapour * new_temp
    drag = lost[0] * speed[0] + lost[1] * speed[1] + lost[2] * speed[2]
    return [new_radius, new_temp] + new_velocity, [vapour] + momentum + [heat_gain, enthalpy, drag]


def parcel_kernel(
    count_ref,
    pk_ref,
    lo_ref,
    temp_ref,
    dens_ref,
    vel_ref,
    fuel_ref,
    hi_ref,
    main_ref,
    dlo_ref,
    dhi_ref,
    state_ref,
    own_dst_ref,
    off_ref,
    dst_ref,
    cell_scr,
    off_smem,
    sem,
    pieces,
    cv,
    row_scr,
    ft,
    a_hi,
    a_lo,
    interp,
    src,
    dep,
):
    groups = pk_ref.shape[0]
    each = cells_of(pk_ref.shape[2]) // 8
    capacity = each * 8
    slots = groups * capacity
    blocks = slots // LANES
    count, group = count_ref[0], lax.axis_index("group")

    per_line = each // LANES
    for b in range(blocks):
        q, r = divmod(b, capacity // LANES)
        line, at = divmod(r, per_line)
        at = capacity + at * LANES
        cell_scr[b : b + 1, :] = pk_ref[q, line : line + 1, at : at + LANES]
    cell = cell_scr[...].astype(jnp.int32)
    slot = iota((blocks, LANES), 0) * LANES + iota((blocks, LANES), 1)
    y_of = ((cell >> 7) & 127) - group * 32
    mine = jnp.logical_and(slot < count, jnp.logical_and(y_of >= -1, y_of < 32))
    ones = jnp.where(mine, 1.0, 0.0).astype(BF16)
    before = jnp.where(iota((LANES, LANES), 0) < iota((LANES, LANES), 1), 1.0, 0.0).astype(BF16)
    after = jnp.where(iota((LANES, LANES), 1) < iota((LANES, LANES), 0), 1.0, 0.0).astype(BF16)
    full = jnp.ones((LANES, LANES), BF16)
    within = jnp.dot(ones, before, preferred_element_type=F32)
    row_sum = jnp.dot(ones, full, preferred_element_type=F32).astype(BF16)
    offset = jnp.dot(after, row_sum, preferred_element_type=F32)
    dst = jnp.where(mine, within + offset, -1.0)
    dst_ref[...] = dst
    own_dst_ref[...] = jnp.where(y_of >= 0, dst, -1.0)
    counts = lax.dot_general(jnp.ones((16, LANES), BF16), ones, NT, preferred_element_type=F32)
    counts = counts.astype(BF16)
    starts = jnp.dot(counts, before, preferred_element_type=F32)
    total = jnp.dot(counts, full, preferred_element_type=F32)
    first = iota((8, LANES), 0) == 0
    off_ref[...] = jnp.where(first, starts[0:8], total[0:8]).astype(jnp.int32)
    copy = pltpu.make_async_copy(off_ref, off_smem, sem)
    copy.start()

    def split(q, carry):
        for line in range(8):
            cells = pk_ref[q, line : line + 1, capacity : capacity + each]
            cells = jnp.broadcast_to(cells, (8, each)).astype(jnp.int32)
            row = iota((8, each), 0)
            y_place = ((cells >> 7) & 127) - group * 32
            place = jnp.where(row == 0, cells >> 14, jnp.where(row == 1, y_place, cells & 127))
            values = pk_ref[q, :, line * each : (line + 1) * each]
            high, low = halves(jnp.concatenate([values, place.astype(F32)], axis=0))
            at = pl.ds(pl.multiple_of(q * capacity + line * each, each), each)
            pieces[0:16, at] = high
            pieces[16:32, at] = low
        return carry

    lax.fori_loop(0, groups, split, 0)

    zero = jnp.zeros((256, LANES), F32)
    own = [temp_ref, dens_ref, vel_ref.at[0], vel_ref.at[1], vel_ref.at[2], fuel_ref.at[0]]
    planes = temp_ref.shape[0]
    rows = temp_ref.shape[1]
    row_start = capacity + each
    after_me = jnp.minimum(group + 1, groups - 1)
    before_me = jnp.maximum(group - 1, 0)
    for f in range(6):
        row_scr[...] = zero
        for x in range(planes + 2):
            if x == 0:
                block = lo_ref[f, 0]
            elif x == planes + 1:
                block = hi_ref[f, 0]
            else:
                block = own[f][x - 1]
            row_scr[x * YPAD : x * YPAD + rows, :] = block
            block, line = row_place(planes, f, x, 0)
            at = row_start + block * LANES
            following = pk_ref[after_me, line : line + 1, at : at + LANES]
            row_scr[x * YPAD + rows : x * YPAD + rows + 1, :] = following
            block, line = row_place(planes, f, x, 1)
            at = row_start + block * LANES
            former = pk_ref[before_me, line : line + 1, at : at + LANES]
            row_scr[(x + 1) * YPAD - 1 : (x + 1) * YPAD, :] = former
        high, low = halves(row_scr[...].T)
        at = slice(f * LANES, (f + 1) * LANES)
        ft[at, 0:256] = high
        ft[at, 256:512] = low
        ft[at, 512:768] = high

    cv[...] = jnp.zeros(cv.shape, F32)
    state_ref[...] = jnp.zeros(state_ref.shape, F32)
    dep[...] = jnp.zeros(dep.shape, F32)
    copy.wait()
    live = off_smem[1, 0]

    def compact(i, carry):
        got = []
        for j in range(8):
            b = i * 8 + j
            aligned = (off_smem[0, b] >> 7) << 7
            hot = one_hot(dst_ref[pl.ds(b, 1), :], aligned)
            block = pieces[:, pl.ds(pl.multiple_of(b * LANES, LANES), LANES)]
            got.append((aligned, lax.dot_general(block, hot, NT, preferred_element_type=F32)))
        for aligned, both in got:
            at = pl.ds(pl.multiple_of(aligned, LANES), WINDOW)
            cv[:, at] += both[0:16] + both[16:32]
        return carry

    lax.fori_loop(0, blocks // 8, compact, 0)

    def gather(c, carry):
        at = pl.ds(pl.multiple_of(c * CHUNK, CHUNK), CHUNK)
        valid = c * CHUNK + iota((1, CHUNK), 1) < live
        fx, fy, fz = cv[0:1, at], cv[1:2, at], cv[2:3, at]
        x0, z0 = cv[8:9, at], cv[10:11, at]
        y0 = jnp.where(valid, cv[9:10, at], 1000.0)
        line = iota((YPAD, CHUNK), 0)
        wy = hat(jnp.where(line == YPAD - 1, -1, line).astype(F32), y0, fy)
        parts = [wy * hat(float(x), x0, fx) for x in range(planes + 2)]
        parts.append(jnp.zeros((256 - (planes + 2) * YPAD, CHUNK), F32))
        high, low = halves(jnp.concatenate(parts, axis=0))
        a_hi[c] = high
        a_lo[c] = low
        stacked = jnp.concatenate([high, high, low], axis=0)
        lines = jnp.dot(ft[...], stacked, preferred_element_type=F32)
        wz = hat(iota((LANES, CHUNK), 0).astype(F32), z0, fz)
        for f in range(6):
            interp[f : f + 1, at] = jnp.sum(
                lines[f * LANES : (f + 1) * LANES] * wz, axis=0, keepdims=True
            )
        return carry

    chunks = (live + CHUNK - 1) // CHUNK
    lax.fori_loop(0, chunks, gather, 0)

    def step(c, carry):
        at = pl.ds(pl.multiple_of(c * CHUNK, CHUNK), CHUNK)
        valid = c * CHUNK + iota((1, CHUNK), 1) < live
        inside = [jnp.where(valid, interp[f : f + 1, at], 0.0) for f in range(6)]
        radius = jnp.where(valid, cv[3:4, at], 1.0)
        velocity = [cv[d : d + 1, at] for d in (5, 6, 7)]
        new, sources = physics(inside, radius, cv[4:5, at], velocity)
        for s in range(5):
            state_ref[s : s + 1, at] = jnp.where(valid, new[s], 0.0)
        for k in range(7):
            src[k : k + 1, at] = jnp.where(valid, sources[k], 0.0)
        return carry

    lax.fori_loop(0, (live + CHUNK - 1) // CHUNK, step, 0)

    def deposit(c, carry):
        at = pl.ds(pl.multiple_of(c * CHUNK, CHUNK), CHUNK)
        wz = hat(iota((LANES, CHUNK), 0).astype(F32), cv[10:11, at], cv[2:3, at])
        high, low = halves(jnp.concatenate([wz * src[k : k + 1, at] for k in range(7)], axis=0))
        left = jnp.concatenate([high, low, high], axis=1)
        right = jnp.concatenate([a_hi[c], a_hi[c], a_lo[c]], axis=1)
        dep[...] += lax.dot_general(left, right, NT, preferred_element_type=F32)
        return carry

    lax.fori_loop(0, chunks, deposit, 0)

    for k in range(7):
        cells = dep[k * LANES : (k + 1) * LANES, :].T
        for x in range(planes + 2):
            block = cells[x * YPAD : x * YPAD + rows]
            if x == 0:
                dlo_ref[k, 0] = block
            elif x == planes + 1:
                dhi_ref[k, 0] = block
            else:
                main_ref[k, x - 1] = block


def spread_kernel(off_ref, dst_ref, state_ref, *outs_and_scratch):
    both_scr = outs_and_scratch[-1]
    high, low = halves(state_ref[...])
    both_scr[0:16, :] = jnp.concatenate([high, low], axis=0)
    outs = outs_and_scratch[:-1]
    group = lax.axis_index("group")
    each = dst_ref.shape[0] // len(outs)
    for d, out in enumerate(outs):
        owner = lax.rem(group + d, len(outs))

        def spread(i, carry, owner=owner, out=out):
            for j in range(8):
                b = owner * each + i * 8 + j
                aligned = (off_ref[0, b] >> 7) << 7
                hot = one_hot(dst_ref[pl.ds(b, 1), :], aligned)
                block = both_scr[:, pl.ds(pl.multiple_of(aligned, LANES), WINDOW)]
                got = jnp.dot(block, hot, preferred_element_type=F32)
                at = pl.ds(pl.multiple_of((i * 8 + j) * LANES, LANES), LANES)
                out[:, at] = got[0:8] + got[8:16]
            return carry

        lax.fori_loop(0, each // 8, spread, 0)


def pack_kernel(
    cells_ref,
    weights_ref,
    radius_ref,
    temp_ref,
    velocity_ref,
    gas_temp_ref,
    dens_ref,
    vel_ref,
    fuel_ref,
    packed_ref,
    top_ref,
    bottom_ref,
):
    planes = gas_temp_ref.shape[0]
    own = [gas_temp_ref, dens_ref, vel_ref.at[0], vel_ref.at[1], vel_ref.at[2], fuel_ref.at[0]]
    for f in range(6):
        top_ref[f, 0] = own[f][planes - 1]
        bottom_ref[f, 0] = own[f][0]
    w = [weights_ref[c : c + 1, :] for c in range(8)]
    slots = cells_ref.shape[1]
    each = slots // 8
    packed_ref[0:1, 0:slots] = (w[4] + w[5]) + (w[6] + w[7])
    packed_ref[1:2, 0:slots] = (w[2] + w[3]) + (w[6] + w[7])
    packed_ref[2:3, 0:slots] = (w[1] + w[3]) + (w[5] + w[7])
    packed_ref[3:4, 0:slots] = radius_ref[...].reshape(1, -1)
    packed_ref[4:5, 0:slots] = temp_ref[...].reshape(1, -1)
    packed_ref[5:8, 0:slots] = velocity_ref[...]
    for i in range(8):
        first = cells_ref[0:1, i * each : (i + 1) * each]
        packed_ref[i : i + 1, slots : slots + each] = first.astype(F32)
    rows = gas_temp_ref.shape[1]
    for f in range(6):
        for x in range(planes):
            for side, y in enumerate((0, rows - 1)):
                block, line = row_place(planes, f, x + 1, side)
                at = slots + each + block * LANES
                packed_ref[line : line + 1, at : at + LANES] = own[f][x, y : y + 1, :]


def rims_kernel(species_ref, up_ref, down_ref, right_ref, left_ref):
    planes, rows = species_ref.shape[1:3]
    up_ref[...] = species_ref[:, planes - 2 : planes]
    down_ref[...] = species_ref[:, 0:2]
    right_ref[...] = species_ref[:, :, rows - 2 : rows]
    left_ref[...] = species_ref[:, :, 0:2]


def assemble_kernel(packed_ref, lo_ref, hi_ref, out_ref):
    planes = OWN_ROWS // 12
    rows = lo_ref.shape[2]
    for f in range(6):
        for x, plane in ((0, lo_ref.at[f, 0]), (planes + 1, hi_ref.at[f, 0])):
            for side, y in enumerate((0, rows - 1)):
                block, line = row_place(planes, f, x, side)
                at = (block - OWN_ROWS // 8) * LANES
                out_ref[line : line + 1, at : at + LANES] = plane[y : y + 1, :]


def row_place(planes, f, x, side):
    if 0 < x <= planes:
        return divmod((f * planes + x - 1) * 2 + side, 8)
    return divmod(planes * 12 + (f * 2 + (x > 0)) * 2 + side, 8)


def transport_kernel(
    first_part,
    first_block,
    diff_ref,
    y_ref,
    xlo_ref,
    xhi_ref,
    ylo_ref,
    yhi_ref,
    ux_ref,
    dens_ref,
    *rest,
):
    if first_part:
        main_ref, below_ref, above_ref, out_ref, gas_ref, pad = rest

        @pl.when(pl.program_id(0) == 0)
        def _():
            last = main_ref.shape[1] - 1
            for k in range(main_ref.shape[0]):
                for x in range(last + 1):
                    total = main_ref[k, x]
                    if x == 0:
                        total = total + below_ref[k, 0]
                    if x == last:
                        total = total + above_ref[k, 0]
                    gas_ref[k, x] = total

        vap_ref = gas_ref.at[0]
    else:
        vap_ref, _, out_ref, pad = rest
    species, planes, rows, depth = y_ref.shape
    at = iota((rows, depth), 1)
    left1 = jnp.where(at >= 1, 16.0, 0.0)
    left2 = jnp.where(at >= 2, -1.0, 0.0)
    right1 = jnp.where(at < depth - 1, 16.0, 0.0)
    right2 = jnp.where(at < depth - 2, -1.0, 0.0)
    first = (first_block + pl.program_id(0)) * species
    for x in range(planes):
        speed = ux_ref[x] * (courant / 12.0)
        gain = source_coef * vap_ref[x] / dens_ref[x]

        for s in range(species):
            d12 = diff_ref[first + s] * (1.0 / 12.0)

            def plane(i, s=s):
                if i < 0:
                    return xlo_ref[s, i + 2]
                if i >= planes:
                    return xhi_ref[s, i - planes]
                return y_ref[s, i]

            center = plane(x)
            up1, up2, dn1, dn2 = plane(x + 1), plane(x + 2), plane(x - 1), plane(x - 2)
            pad[s, 6:8, :] = ylo_ref[s, x]
            pad[s, 8 : 8 + rows, :] = center
            pad[s, 8 + rows : 10 + rows, :] = yhi_ref[s, x]
            near = up1 + dn1 + pad[s, 7 : 7 + rows, :] + pad[s, 9 : 9 + rows, :]
            far = up2 + dn2 + pad[s, 6 : 6 + rows, :] + pad[s, 10 : 10 + rows, :]
            along = (
                left1 * pltpu.roll(center, 1, 1)
                + right1 * pltpu.roll(center, depth - 1, 1)
                + left2 * pltpu.roll(center, 2, 1)
                + right2 * pltpu.roll(center, depth - 2, 1)
            )
            slope = 8.0 * (up1 - dn1) - (up2 - dn2)
            flag = jnp.where(first + s == 0, 1.0, 0.0)
            laplace = 16.0 * near - far + along - 90.0 * center
            out_ref[s, x] = center + d12 * laplace - speed * slope + gain * (flag - center)


def per_device(
    species,
    diffusion,
    gas_temp,
    gas_density,
    gas_velocity,
    drop_radius,
    drop_temp,
    drop_velocity,
    parcel_cells,
    parcel_weights,
    parcel_counts,
):
    count_s = lax.axis_size("space")
    groups = lax.axis_size("group")
    planes, rows, depth = gas_temp.shape
    kinds = species.shape[0]
    capacity = drop_radius.shape[0]
    slots = capacity * groups
    blocks = slots // LANES
    ahead = [(i, i + 1) for i in range(count_s - 1)]
    back = [(b, a) for a, b in ahead]
    g_ahead = [(i, i + 1) for i in range(groups - 1)]
    g_back = [(b, a) for a, b in g_ahead]

    whole = lambda shape: pl.BlockSpec(shape, lambda i, n=len(shape): (0,) * n)
    smem = pl.BlockSpec(memory_space=pltpu.SMEM)
    hbm = pl.BlockSpec(memory_space=pl.ANY)
    shaped = lambda *shape: jax.ShapeDtypeStruct(shape, F32)
    limit = pltpu.CompilerParams(vmem_limit_bytes=63 * 2**20)
    little = pltpu.CompilerParams(vmem_limit_bytes=2 * 2**20)

    def by_kind(first, *shape):
        return pl.BlockSpec((MANY,) + shape, lambda i: (first + i, 0, 0, 0))

    width = capacity // 8 * 9 + ROWS_WIDTH
    packed, top, bottom = pl.pallas_call(
        pack_kernel,
        grid=(1,),
        in_specs=[
            whole((8, capacity)),
            whole((8, capacity)),
            whole((capacity,)),
            whole((capacity,)),
            whole((3, capacity)),
            whole((planes, rows, depth)),
            whole((planes, rows, depth)),
            whole((3, planes, rows, depth)),
            whole((1, planes, rows, depth)),
        ],
        out_specs=[
            whole((8, width)),
            whole((6, 1, rows, depth)),
            whole((6, 1, rows, depth)),
        ],
        out_shape=[
            shaped(8, width),
            shaped(6, 1, rows, depth),
            shaped(6, 1, rows, depth),
        ],
        compiler_params=limit,
        name="pack",
    )(
        parcel_cells, parcel_weights, drop_radius, drop_temp, drop_velocity,
        gas_temp, gas_density, gas_velocity, species,
    )
    species_cut, packed = lax.optimization_barrier((species, packed))
    x_up, x_down, y_right, y_left = pl.pallas_call(
        rims_kernel,
        grid=(kinds // MANY,),
        in_specs=[by_kind(0, planes, rows, depth)],
        out_specs=[
            by_kind(0, 2, rows, depth),
            by_kind(0, 2, rows, depth),
            by_kind(0, planes, 2, depth),
            by_kind(0, planes, 2, depth),
        ],
        out_shape=[
            shaped(kinds, 2, rows, depth),
            shaped(kinds, 2, rows, depth),
            shaped(kinds, planes, 2, depth),
            shaped(kinds, planes, 2, depth),
        ],
        compiler_params=limit,
        name="rims",
    )(species_cut)
    field_lo = lax.ppermute(top, "space", ahead)
    field_hi = lax.ppermute(bottom, "space", back)
    tail = RIM_ROWS // 8 * LANES
    sent = pl.pallas_call(
        assemble_kernel,
        grid=(1,),
        in_specs=[hbm, whole((6, 1, rows, depth)), whole((6, 1, rows, depth))],
        out_specs=pl.BlockSpec((8, tail), lambda i: (0, width // tail - 1)),
        out_shape=shaped(8, width),
        input_output_aliases={0: 0},
        compiler_params=little,
        name="assemble",
    )(packed, field_lo, field_hi)
    sent, x_up, x_down, y_right, y_left = lax.optimization_barrier(
        (sent, x_up, x_down, y_right, y_left)
    )
    parcels = lax.all_gather(sent, "group", axis=0)

    x_up, x_down, y_right, y_left, parcels = lax.optimization_barrier(
        (x_up, x_down, y_right, y_left, parcels)
    )
    y_lo = lax.ppermute(y_right, "group", g_ahead)
    y_hi = lax.ppermute(y_left, "group", g_back)
    x_up, x_down, y_lo, y_hi = lax.optimization_barrier((x_up, x_down, y_lo, y_hi))
    x_lo = lax.ppermute(x_up, "space", ahead)
    x_hi = lax.ppermute(x_down, "space", back)

    chunks = pl.cdiv(slots, CHUNK)
    reach = max(chunks * CHUNK, slots + WINDOW)
    main, dep_lo, dep_hi, state, dst, off = pl.pallas_call(
        parcel_kernel,
        grid=(1,),
        in_specs=[
            smem,
            whole((groups, 8, width)),
            whole((6, 1, rows, depth)),
            whole((planes, rows, depth)),
            whole((planes, rows, depth)),
            whole((3, planes, rows, depth)),
            whole((1, planes, rows, depth)),
            whole((6, 1, rows, depth)),
        ],
        out_specs=[
            whole((7, planes, rows, depth)),
            whole((7, 1, rows, depth)),
            whole((7, 1, rows, depth)),
            whole((8, reach)),
            whole((blocks, LANES)),
            whole((8, LANES)),
        ],
        out_shape=[
            shaped(7, planes, rows, depth),
            shaped(7, 1, rows, depth),
            shaped(7, 1, rows, depth),
            shaped(8, reach),
            shaped(blocks, LANES),
            jax.ShapeDtypeStruct((8, LANES), jnp.int32),
        ],
        scratch_shapes=[
            pltpu.VMEM((blocks, LANES), F32),
            pltpu.VMEM((blocks, LANES), F32),
            pltpu.SMEM((8, LANES), jnp.int32),
            pltpu.SemaphoreType.DMA,
            pltpu.VMEM((32, slots), BF16),
            pltpu.VMEM((16, reach), F32),
            pltpu.VMEM((256, LANES), F32),
            pltpu.VMEM((6 * LANES, 768), BF16),
            pltpu.VMEM((chunks, 256, CHUNK), BF16),
            pltpu.VMEM((chunks, 256, CHUNK), BF16),
            pltpu.VMEM((8, reach), F32),
            pltpu.VMEM((8, reach), F32),
            pltpu.VMEM((7 * LANES, 256), F32),
        ],
        compiler_params=limit,
        name="parcels",
    )(parcel_counts, parcels, field_lo, gas_temp, gas_density, gas_velocity, species, field_hi)

    from_below = lax.ppermute(dep_hi, "space", ahead)
    from_above = lax.ppermute(dep_lo, "space", back)

    spread = pl.pallas_call(
        spread_kernel,
        grid=(1,),
        in_specs=[smem, whole((blocks, LANES)), whole((8, reach))],
        out_specs=[whole((8, capacity))] * groups,
        out_shape=[shaped(8, capacity)] * groups,
        scratch_shapes=[pltpu.VMEM((16, reach), BF16)],
        compiler_params=limit,
        name="spread",
    )(off, dst, state)
    gas = pl.BlockSpec((planes, rows, depth), lambda i: (0, 0, 0))
    row0 = pl.BlockSpec((None, planes, rows, depth), lambda i: (0, 0, 0, 0))
    all_gas = whole((7, planes, rows, depth))
    rim = whole((7, 1, rows, depth))
    species_next = gas_sources = None
    at = 0
    for c, size in enumerate(PARTS):
        first = at // MANY
        at += size
        out_specs = [by_kind(first, planes, rows, depth)]
        out_shape = [shaped(*species.shape)]
        if c == 0:
            extra, extra_specs = (main, from_below, from_above), [all_gas, rim, rim]
            out_specs.append(all_gas)
            out_shape.append(shaped(7, planes, rows, depth))
        else:
            extra, extra_specs = (gas_sources, species_next), [row0, hbm]
        got = pl.pallas_call(
            functools.partial(transport_kernel, c == 0, first),
            grid=(size // MANY,),
            in_specs=[
                smem,
                by_kind(first, planes, rows, depth),
                by_kind(first, 2, rows, depth),
                by_kind(first, 2, rows, depth),
                by_kind(first, planes, 2, depth),
                by_kind(first, planes, 2, depth),
                row0,
                gas,
            ]
            + extra_specs,
            out_specs=out_specs,
            out_shape=out_shape,
            input_output_aliases={} if c == 0 else {9: 0},
            scratch_shapes=[pltpu.VMEM((MANY, rows + 16, depth), F32)],
            compiler_params=limit,
            name="transport",
        )(diffusion, species, x_lo, x_hi, y_lo, y_hi, gas_velocity, gas_density, *extra)
        species_next = got[0]
        if c == 0:
            gas_sources = got[1]
    species_next, spread = lax.optimization_barrier((species_next, spread))
    returned = [spread[0]]
    for d in range(1, groups):
        route = [(i, (i + d) % groups) for i in range(groups)]
        returned.append(lax.ppermute(spread[d], "group", route))
    new_state = sum(returned[1:], returned[0])
    old_state = jnp.concatenate([drop_radius[None], drop_temp[None], drop_velocity], axis=0)
    slot = lax.axis_index("group") * capacity + jnp.arange(capacity, dtype=jnp.int32)
    live = slot < parcel_counts[0]
    parcel_state = jnp.where(live[None], new_state[0:5], old_state)
    return (species_next, gas_sources, parcel_state)


def solution(mesh):
    in_specs = (
        P(None, "space", "group", None),
        P(),
        P("space", "group", None),
        P("space", "group", None),
        P(None, "space", "group", None),
        P(("space", "group")),
        P(("space", "group")),
        P(None, ("space", "group")),
        P(None, ("space", "group")),
        P(None, ("space", "group")),
        P("space"),
    )
    out_specs = (
        P(None, "space", "group", None),
        P(None, "space", "group", None),
        P(None, ("space", "group")),
    )
    return jax.shard_map(
        per_device, mesh=mesh, in_specs=in_specs, out_specs=out_specs, check_vma=False
    )
```

```python
import functools

import jax
import jax.numpy as jnp
from jax import lax
from jax.experimental import pallas as pl
from jax.experimental.pallas import tpu as pltpu
from jax.sharding import PartitionSpec as P

time_step = 0.05
evap_coef = 0.5
heat_coef = 0.15
latent_coef = 0.2
enthalpy_coef = 1.3
source_coef = 0.5
courant = 0.3

LANES = 128
PARTS = (54,)
MANY = 18
CHUNK = 1536
WINDOW = 256
YPAD = 40
OWN_ROWS = 48
RIM_ROWS = 24
ROWS_WIDTH = (OWN_ROWS + RIM_ROWS) // 8 * LANES
F32 = jnp.float32
BF16 = jnp.bfloat16
NT = (((1,), (1,)), ((), ()))


def halves(value):
    high = value.astype(BF16)
    return high, (value - high.astype(F32)).astype(BF16)


def hat(index, start, fraction):
    away = index - start
    return jnp.where(away == 0.0, 1.0 - fraction, jnp.where(away == 1.0, fraction, 0.0))


def iota(shape, dim):
    return lax.broadcasted_iota(jnp.int32, shape, dim)


def one_hot(dst_row, aligned):
    rel = jnp.broadcast_to(dst_row - aligned.astype(F32), (16, LANES)).astype(BF16)
    rel = jnp.concatenate([rel] * (WINDOW // 16), axis=0)
    places = iota((WINDOW, LANES), 0).astype(F32).astype(BF16)
    return jnp.where(places == rel, jnp.ones_like(rel), jnp.zeros_like(rel))


def cells_of(width):
    return (width - ROWS_WIDTH) // 9 * 8


def physics(interp, radius, drop_temp, velocity):
    heat, density, speed, fuel = interp[0], interp[1], interp[2:5], interp[5]
    slip = [g - v for g, v in zip(speed, velocity)]
    slip_square = slip[0] * slip[0] + slip[1] * slip[1] + slip[2] * slip[2]
    log_flow = jnp.log(1.0 + density * radius * slip_square)
    sherwood = 2.0 + 0.6 * jnp.exp(0.25 * log_flow)
    surface = 0.5 / (1.0 + jnp.exp(-4.0 * (drop_temp - 1.0)))
    evap = evap_coef * radius * density * sherwood * jnp.log((1.0 - fuel) / (1.0 - surface))
    mass = radius * radius * radius
    ratio = 1.0 - time_step * evap / mass
    new_radius = radius * jnp.exp(jnp.log(ratio) * (1.0 / 3.0))
    rate = time_step * (1.0 + 0.15 * jnp.exp(0.35 * log_flow)) / (2.0 * radius * radius)
    change = [rate * s for s in slip]
    new_velocity = [v + c for v, c in zip(velocity, change)]
    heat_rate = heat_coef * sherwood / (radius * radius)
    new_temp = drop_temp + time_step * (
        heat_rate * (heat - drop_temp) - latent_coef * evap / mass
    )
    vapour = time_step * evap
    lost = [mass * (v - n) for v, n in zip(velocity, new_velocity)]
    momentum = [m + vapour * v for m, v in zip(lost, velocity)]
    heat_gain = -time_step * mass * heat_rate * (heat - drop_temp)
    enthalpy = enthalpy_coef * vapour * new_temp
    drag = lost[0] * speed[0] + lost[1] * speed[1] + lost[2] * speed[2]
    return [new_radius, new_temp] + new_velocity, [vapour] + momentum + [heat_gain, enthalpy, drag]


def parcel_kernel(
    count_ref,
    pk_ref,
    lo_ref,
    temp_ref,
    dens_ref,
    vel_ref,
    fuel_ref,
    hi_ref,
    main_ref,
    dlo_ref,
    dhi_ref,
    state_ref,
    own_dst_ref,
    off_ref,
    dst_ref,
    cell_scr,
    off_smem,
    sem,
    pieces,
    cv,
    row_scr,
    ft,
    a_hi,
    a_lo,
    interp,
    src,
    dep,
):
    groups = pk_ref.shape[0]
    each = cells_of(pk_ref.shape[2]) // 8
    capacity = each * 8
    slots = groups * capacity
    blocks = slots // LANES
    count, group = count_ref[0], lax.axis_index("group")

    per_line = each // LANES
    for b in range(blocks):
        q, r = divmod(b, capacity // LANES)
        line, at = divmod(r, per_line)
        at = capacity + at * LANES
        cell_scr[b : b + 1, :] = pk_ref[q, line : line + 1, at : at + LANES]
    cell = cell_scr[...].astype(jnp.int32)
    slot = iota((blocks, LANES), 0) * LANES + iota((blocks, LANES), 1)
    y_of = ((cell >> 7) & 127) - group * 32
    mine = jnp.logical_and(slot < count, jnp.logical_and(y_of >= -1, y_of < 32))
    ones = jnp.where(mine, 1.0, 0.0).astype(BF16)
    before = jnp.where(iota((LANES, LANES), 0) < iota((LANES, LANES), 1), 1.0, 0.0).astype(BF16)
    after = jnp.where(iota((LANES, LANES), 1) < iota((LANES, LANES), 0), 1.0, 0.0).astype(BF16)
    full = jnp.ones((LANES, LANES), BF16)
    within = jnp.dot(ones, before, preferred_element_type=F32)
    row_sum = jnp.dot(ones, full, preferred_element_type=F32).astype(BF16)
    offset = jnp.dot(after, row_sum, preferred_element_type=F32)
    dst = jnp.where(mine, within + offset, -1.0)
    dst_ref[...] = dst
    own_dst_ref[...] = jnp.where(y_of >= 0, dst, -1.0)
    counts = lax.dot_general(jnp.ones((16, LANES), BF16), ones, NT, preferred_element_type=F32)
    counts = counts.astype(BF16)
    starts = jnp.dot(counts, before, preferred_element_type=F32)
    total = jnp.dot(counts, full, preferred_element_type=F32)
    first = iota((8, LANES), 0) == 0
    off_ref[...] = jnp.where(first, starts[0:8], total[0:8]).astype(jnp.int32)
    copy = pltpu.make_async_copy(off_ref, off_smem, sem)
    copy.start()

    def split(q, carry):
        for line in range(8):
            cells = pk_ref[q, line : line + 1, capacity : capacity + each]
            cells = jnp.broadcast_to(cells, (8, each)).astype(jnp.int32)
            row = iota((8, each), 0)
            y_place = ((cells >> 7) & 127) - group * 32
            place = jnp.where(row == 0, cells >> 14, jnp.where(row == 1, y_place, cells & 127))
            values = pk_ref[q, :, line * each : (line + 1) * each]
            high, low = halves(jnp.concatenate([values, place.astype(F32)], axis=0))
            at = pl.ds(pl.multiple_of(q * capacity + line * each, each), each)
            pieces[0:16, at] = high
            pieces[16:32, at] = low
        return carry

    lax.fori_loop(0, groups, split, 0)

    zero = jnp.zeros((256, LANES), F32)
    own = [temp_ref, dens_ref, vel_ref.at[0], vel_ref.at[1], vel_ref.at[2], fuel_ref.at[0]]
    planes = temp_ref.shape[0]
    rows = temp_ref.shape[1]
    row_start = capacity + each
    after_me = jnp.minimum(group + 1, groups - 1)
    before_me = jnp.maximum(group - 1, 0)
    for f in range(6):
        row_scr[...] = zero
        for x in range(planes + 2):
            if x == 0:
                block = lo_ref[f, 0]
            elif x == planes + 1:
                block = hi_ref[f, 0]
            else:
                block = own[f][x - 1]
            row_scr[x * YPAD : x * YPAD + rows, :] = block
            block, line = row_place(planes, f, x, 0)
            at = row_start + block * LANES
            following = pk_ref[after_me, line : line + 1, at : at + LANES]
            row_scr[x * YPAD + rows : x * YPAD + rows + 1, :] = following
            block, line = row_place(planes, f, x, 1)
            at = row_start + block * LANES
            former = pk_ref[before_me, line : line + 1, at : at + LANES]
            row_scr[(x + 1) * YPAD - 1 : (x + 1) * YPAD, :] = former
        high, low = halves(row_scr[...].T)
        at = slice(f * LANES, (f + 1) * LANES)
        ft[at, 0:256] = high
        ft[at, 256:512] = low
        ft[at, 512:768] = high

    cv[...] = jnp.zeros(cv.shape, F32)
    state_ref[...] = jnp.zeros(state_ref.shape, F32)
    dep[...] = jnp.zeros(dep.shape, F32)
    copy.wait()
    live = off_smem[1, 0]

    def compact(i, carry):
        got = []
        for j in range(8):
            b = i * 8 + j
            aligned = (off_smem[0, b] >> 7) << 7
            hot = one_hot(dst_ref[pl.ds(b, 1), :], aligned)
            block = pieces[:, pl.ds(pl.multiple_of(b * LANES, LANES), LANES)]
            got.append((aligned, lax.dot_general(block, hot, NT, preferred_element_type=F32)))
        for aligned, both in got:
            at = pl.ds(pl.multiple_of(aligned, LANES), WINDOW)
            cv[:, at] += both[0:16] + both[16:32]
        return carry

    lax.fori_loop(0, blocks // 8, compact, 0)

    def gather(c, carry):
        at = pl.ds(pl.multiple_of(c * CHUNK, CHUNK), CHUNK)
        valid = c * CHUNK + iota((1, CHUNK), 1) < live
        fx, fy, fz = cv[0:1, at], cv[1:2, at], cv[2:3, at]
        x0, z0 = cv[8:9, at], cv[10:11, at]
        y0 = jnp.where(valid, cv[9:10, at], 1000.0)
        line = iota((YPAD, CHUNK), 0)
        wy = hat(jnp.where(line == YPAD - 1, -1, line).astype(F32), y0, fy)
        parts = [wy * hat(float(x), x0, fx) for x in range(planes + 2)]
        parts.append(jnp.zeros((256 - (planes + 2) * YPAD, CHUNK), F32))
        high, low = halves(jnp.concatenate(parts, axis=0))
        a_hi[c] = high
        a_lo[c] = low
        stacked = jnp.concatenate([high, high, low], axis=0)
        lines = jnp.dot(ft[...], stacked, preferred_element_type=F32)
        wz = hat(iota((LANES, CHUNK), 0).astype(F32), z0, fz)
        for f in range(6):
            interp[f : f + 1, at] = jnp.sum(
                lines[f * LANES : (f + 1) * LANES] * wz, axis=0, keepdims=True
            )
        return carry

    chunks = (live + CHUNK - 1) // CHUNK
    lax.fori_loop(0, chunks, gather, 0)

    def step(c, carry):
        at = pl.ds(pl.multiple_of(c * CHUNK, CHUNK), CHUNK)
        valid = c * CHUNK + iota((1, CHUNK), 1) < live
        inside = [jnp.where(valid, interp[f : f + 1, at], 0.0) for f in range(6)]
        radius = jnp.where(valid, cv[3:4, at], 1.0)
        velocity = [cv[d : d + 1, at] for d in (5, 6, 7)]
        new, sources = physics(inside, radius, cv[4:5, at], velocity)
        for s in range(5):
            state_ref[s : s + 1, at] = jnp.where(valid, new[s], 0.0)
        for k in range(7):
            src[k : k + 1, at] = jnp.where(valid, sources[k], 0.0)
        return carry

    lax.fori_loop(0, (live + CHUNK - 1) // CHUNK, step, 0)

    def deposit(c, carry):
        at = pl.ds(pl.multiple_of(c * CHUNK, CHUNK), CHUNK)
        wz = hat(iota((LANES, CHUNK), 0).astype(F32), cv[10:11, at], cv[2:3, at])
        high, low = halves(jnp.concatenate([wz * src[k : k + 1, at] for k in range(7)], axis=0))
        left = jnp.concatenate([high, low, high], axis=1)
        right = jnp.concatenate([a_hi[c], a_hi[c], a_lo[c]], axis=1)
        dep[...] += lax.dot_general(left, right, NT, preferred_element_type=F32)
        return carry

    lax.fori_loop(0, chunks, deposit, 0)

    for k in range(7):
        cells = dep[k * LANES : (k + 1) * LANES, :].T
        for x in range(planes + 2):
            block = cells[x * YPAD : x * YPAD + rows]
            if x == 0:
                dlo_ref[k, 0] = block
            elif x == planes + 1:
                dhi_ref[k, 0] = block
            else:
                main_ref[k, x - 1] = block


def spread_kernel(off_ref, dst_ref, state_ref, *outs_and_scratch):
    both_scr = outs_and_scratch[-1]
    high, low = halves(state_ref[...])
    both_scr[0:16, :] = jnp.concatenate([high, low], axis=0)
    outs = outs_and_scratch[:-1]
    group = lax.axis_index("group")
    each = dst_ref.shape[0] // len(outs)
    for d, out in enumerate(outs):
        owner = lax.rem(group + d, len(outs))

        def spread(i, carry, owner=owner, out=out):
            for j in range(8):
                b = owner * each + i * 8 + j
                aligned = (off_ref[0, b] >> 7) << 7
                hot = one_hot(dst_ref[pl.ds(b, 1), :], aligned)
                block = both_scr[:, pl.ds(pl.multiple_of(aligned, LANES), WINDOW)]
                got = jnp.dot(block, hot, preferred_element_type=F32)
                at = pl.ds(pl.multiple_of((i * 8 + j) * LANES, LANES), LANES)
                out[:, at] = got[0:8] + got[8:16]
            return carry

        lax.fori_loop(0, each // 8, spread, 0)


def pack_kernel(
    cells_ref,
    weights_ref,
    radius_ref,
    temp_ref,
    velocity_ref,
    gas_temp_ref,
    dens_ref,
    vel_ref,
    fuel_ref,
    packed_ref,
    top_ref,
    bottom_ref,
):
    planes = gas_temp_ref.shape[0]
    own = [gas_temp_ref, dens_ref, vel_ref.at[0], vel_ref.at[1], vel_ref.at[2], fuel_ref.at[0]]
    for f in range(6):
        top_ref[f, 0] = own[f][planes - 1]
        bottom_ref[f, 0] = own[f][0]
    w = [weights_ref[c : c + 1, :] for c in range(8)]
    slots = cells_ref.shape[1]
    each = slots // 8
    packed_ref[0:1, 0:slots] = (w[4] + w[5]) + (w[6] + w[7])
    packed_ref[1:2, 0:slots] = (w[2] + w[3]) + (w[6] + w[7])
    packed_ref[2:3, 0:slots] = (w[1] + w[3]) + (w[5] + w[7])
    packed_ref[3:4, 0:slots] = radius_ref[...].reshape(1, -1)
    packed_ref[4:5, 0:slots] = temp_ref[...].reshape(1, -1)
    packed_ref[5:8, 0:slots] = velocity_ref[...]
    for i in range(8):
        first = cells_ref[0:1, i * each : (i + 1) * each]
        packed_ref[i : i + 1, slots : slots + each] = first.astype(F32)
    rows = gas_temp_ref.shape[1]
    for f in range(6):
        for x in range(planes):
            for side, y in enumerate((0, rows - 1)):
                block, line = row_place(planes, f, x + 1, side)
                at = slots + each + block * LANES
                packed_ref[line : line + 1, at : at + LANES] = own[f][x, y : y + 1, :]


def rims_kernel(species_ref, up_ref, down_ref, right_ref, left_ref):
    planes, rows = species_ref.shape[1:3]
    up_ref[...] = species_ref[:, planes - 2 : planes]
    down_ref[...] = species_ref[:, 0:2]
    right_ref[...] = species_ref[:, :, rows - 2 : rows]
    left_ref[...] = species_ref[:, :, 0:2]


def assemble_kernel(packed_ref, lo_ref, hi_ref, out_ref):
    planes = OWN_ROWS // 12
    rows = lo_ref.shape[2]
    for f in range(6):
        for x, plane in ((0, lo_ref.at[f, 0]), (planes + 1, hi_ref.at[f, 0])):
            for side, y in enumerate((0, rows - 1)):
                block, line = row_place(planes, f, x, side)
                at = (block - OWN_ROWS // 8) * LANES
                out_ref[line : line + 1, at : at + LANES] = plane[y : y + 1, :]


def row_place(planes, f, x, side):
    if 0 < x <= planes:
        return divmod((f * planes + x - 1) * 2 + side, 8)
    return divmod(planes * 12 + (f * 2 + (x > 0)) * 2 + side, 8)


def transport_kernel(
    first_part,
    first_block,
    diff_ref,
    y_ref,
    xlo_ref,
    xhi_ref,
    ylo_ref,
    yhi_ref,
    ux_ref,
    dens_ref,
    *rest,
):
    if first_part:
        main_ref, below_ref, above_ref, out_ref, gas_ref, pad = rest

        @pl.when(pl.program_id(0) == 0)
        def _():
            last = main_ref.shape[1] - 1
            for k in range(main_ref.shape[0]):
                for x in range(last + 1):
                    total = main_ref[k, x]
                    if x == 0:
                        total = total + below_ref[k, 0]
                    if x == last:
                        total = total + above_ref[k, 0]
                    gas_ref[k, x] = total

        vap_ref = gas_ref.at[0]
    else:
        vap_ref, _, out_ref, pad = rest
    species, planes, rows, depth = y_ref.shape
    at = iota((rows, depth), 1)
    left1 = jnp.where(at >= 1, 16.0, 0.0)
    left2 = jnp.where(at >= 2, -1.0, 0.0)
    right1 = jnp.where(at < depth - 1, 16.0, 0.0)
    right2 = jnp.where(at < depth - 2, -1.0, 0.0)
    first = (first_block + pl.program_id(0)) * species
    for x in range(planes):
        speed = ux_ref[x] * (courant / 12.0)
        gain = source_coef * vap_ref[x] / dens_ref[x]

        for s in range(species):
            d12 = diff_ref[first + s] * (1.0 / 12.0)

            def plane(i, s=s):
                if i < 0:
                    return xlo_ref[s, i + 2]
                if i >= planes:
                    return xhi_ref[s, i - planes]
                return y_ref[s, i]

            center = plane(x)
            up1, up2, dn1, dn2 = plane(x + 1), plane(x + 2), plane(x - 1), plane(x - 2)
            pad[s, 6:8, :] = ylo_ref[s, x]
            pad[s, 8 : 8 + rows, :] = center
            pad[s, 8 + rows : 10 + rows, :] = yhi_ref[s, x]
            near = up1 + dn1 + pad[s, 7 : 7 + rows, :] + pad[s, 9 : 9 + rows, :]
            far = up2 + dn2 + pad[s, 6 : 6 + rows, :] + pad[s, 10 : 10 + rows, :]
            along = (
                left1 * pltpu.roll(center, 1, 1)
                + right1 * pltpu.roll(center, depth - 1, 1)
                + left2 * pltpu.roll(center, 2, 1)
                + right2 * pltpu.roll(center, depth - 2, 1)
            )
            slope = 8.0 * (up1 - dn1) - (up2 - dn2)
            flag = jnp.where(first + s == 0, 1.0, 0.0)
            laplace = 16.0 * near - far + along - 90.0 * center
            out_ref[s, x] = center + d12 * laplace - speed * slope + gain * (flag - center)


def per_device(
    species,
    diffusion,
    gas_temp,
    gas_density,
    gas_velocity,
    drop_radius,
    drop_temp,
    drop_velocity,
    parcel_cells,
    parcel_weights,
    parcel_counts,
):
    count_s = lax.axis_size("space")
    groups = lax.axis_size("group")
    planes, rows, depth = gas_temp.shape
    kinds = species.shape[0]
    capacity = drop_radius.shape[0]
    slots = capacity * groups
    blocks = slots // LANES
    ahead = [(i, i + 1) for i in range(count_s - 1)]
    back = [(b, a) for a, b in ahead]
    g_ahead = [(i, i + 1) for i in range(groups - 1)]
    g_back = [(b, a) for a, b in g_ahead]

    whole = lambda shape: pl.BlockSpec(shape, lambda i, n=len(shape): (0,) * n)
    smem = pl.BlockSpec(memory_space=pltpu.SMEM)
    hbm = pl.BlockSpec(memory_space=pl.ANY)
    shaped = lambda *shape: jax.ShapeDtypeStruct(shape, F32)
    limit = pltpu.CompilerParams(vmem_limit_bytes=63 * 2**20)
    little = pltpu.CompilerParams(vmem_limit_bytes=2 * 2**20)

    def by_kind(first, *shape):
        return pl.BlockSpec((MANY,) + shape, lambda i: (first + i, 0, 0, 0))

    width = capacity // 8 * 9 + ROWS_WIDTH
    packed, top, bottom = pl.pallas_call(
        pack_kernel,
        grid=(1,),
        in_specs=[
            whole((8, capacity)),
            whole((8, capacity)),
            whole((capacity,)),
            whole((capacity,)),
            whole((3, capacity)),
            whole((planes, rows, depth)),
            whole((planes, rows, depth)),
            whole((3, planes, rows, depth)),
            whole((1, planes, rows, depth)),
        ],
        out_specs=[
            whole((8, width)),
            whole((6, 1, rows, depth)),
            whole((6, 1, rows, depth)),
        ],
        out_shape=[
            shaped(8, width),
            shaped(6, 1, rows, depth),
            shaped(6, 1, rows, depth),
        ],
        compiler_params=limit,
        name="pack",
    )(
        parcel_cells, parcel_weights, drop_radius, drop_temp, drop_velocity,
        gas_temp, gas_density, gas_velocity, species,
    )
    species_cut, packed = lax.optimization_barrier((species, packed))
    x_up, x_down, y_right, y_left = pl.pallas_call(
        rims_kernel,
        grid=(kinds // MANY,),
        in_specs=[by_kind(0, planes, rows, depth)],
        out_specs=[
            by_kind(0, 2, rows, depth),
            by_kind(0, 2, rows, depth),
            by_kind(0, planes, 2, depth),
            by_kind(0, planes, 2, depth),
        ],
        out_shape=[
            shaped(kinds, 2, rows, depth),
            shaped(kinds, 2, rows, depth),
            shaped(kinds, planes, 2, depth),
            shaped(kinds, planes, 2, depth),
        ],
        compiler_params=limit,
        name="rims",
    )(species_cut)
    field_lo = lax.ppermute(top, "space", ahead)
    field_hi = lax.ppermute(bottom, "space", back)
    tail = RIM_ROWS // 8 * LANES
    sent = pl.pallas_call(
        assemble_kernel,
        grid=(1,),
        in_specs=[hbm, whole((6, 1, rows, depth)), whole((6, 1, rows, depth))],
        out_specs=pl.BlockSpec((8, tail), lambda i: (0, width // tail - 1)),
        out_shape=shaped(8, width),
        input_output_aliases={0: 0},
        compiler_params=little,
        name="assemble",
    )(packed, field_lo, field_hi)
    sent, x_up, x_down, y_right, y_left = lax.optimization_barrier(
        (sent, x_up, x_down, y_right, y_left)
    )
    parcels = lax.all_gather(sent, "group", axis=0)

    x_up, x_down, y_right, y_left, parcels = lax.optimization_barrier(
        (x_up, x_down, y_right, y_left, parcels)
    )
    x_lo = lax.ppermute(x_up, "space", ahead)
    x_hi = lax.ppermute(x_down, "space", back)
    y_lo = lax.ppermute(y_right, "group", g_ahead)

    chunks = pl.cdiv(slots, CHUNK)
    reach = max(chunks * CHUNK, slots + WINDOW)
    main, dep_lo, dep_hi, state, dst, off = pl.pallas_call(
        parcel_kernel,
        grid=(1,),
        in_specs=[
            smem,
            whole((groups, 8, width)),
            whole((6, 1, rows, depth)),
            whole((planes, rows, depth)),
            whole((planes, rows, depth)),
            whole((3, planes, rows, depth)),
            whole((1, planes, rows, depth)),
            whole((6, 1, rows, depth)),
        ],
        out_specs=[
            whole((7, planes, rows, depth)),
            whole((7, 1, rows, depth)),
            whole((7, 1, rows, depth)),
            whole((8, reach)),
            whole((blocks, LANES)),
            whole((8, LANES)),
        ],
        out_shape=[
            shaped(7, planes, rows, depth),
            shaped(7, 1, rows, depth),
            shaped(7, 1, rows, depth),
            shaped(8, reach),
            shaped(blocks, LANES),
            jax.ShapeDtypeStruct((8, LANES), jnp.int32),
        ],
        scratch_shapes=[
            pltpu.VMEM((blocks, LANES), F32),
            pltpu.VMEM((blocks, LANES), F32),
            pltpu.SMEM((8, LANES), jnp.int32),
            pltpu.SemaphoreType.DMA,
            pltpu.VMEM((32, slots), BF16),
            pltpu.VMEM((16, reach), F32),
            pltpu.VMEM((256, LANES), F32),
            pltpu.VMEM((6 * LANES, 768), BF16),
            pltpu.VMEM((chunks, 256, CHUNK), BF16),
            pltpu.VMEM((chunks, 256, CHUNK), BF16),
            pltpu.VMEM((8, reach), F32),
            pltpu.VMEM((8, reach), F32),
            pltpu.VMEM((7 * LANES, 256), F32),
        ],
        compiler_params=limit,
        name="parcels",
    )(parcel_counts, parcels, field_lo, gas_temp, gas_density, gas_velocity, species, field_hi)

    y_lo, y_left, state = lax.optimization_barrier((y_lo, y_left, state))
    y_hi = lax.ppermute(y_left, "group", g_back)

    from_below = lax.ppermute(dep_hi, "space", ahead)
    from_above = lax.ppermute(dep_lo, "space", back)

    spread = pl.pallas_call(
        spread_kernel,
        grid=(1,),
        in_specs=[smem, whole((blocks, LANES)), whole((8, reach))],
        out_specs=[whole((8, capacity))] * groups,
        out_shape=[shaped(8, capacity)] * groups,
        scratch_shapes=[pltpu.VMEM((16, reach), BF16)],
        compiler_params=limit,
        name="spread",
    )(off, dst, state)
    y_lo, y_hi, from_below, from_above, spread = lax.optimization_barrier(
        (y_lo, y_hi, from_below, from_above, spread)
    )
    returned = [spread[0]]
    for d in range(1, groups):
        route = [(i, (i + d) % groups) for i in range(groups)]
        returned.append(lax.ppermute(spread[d], "group", route))
    gas = pl.BlockSpec((planes, rows, depth), lambda i: (0, 0, 0))
    row0 = pl.BlockSpec((None, planes, rows, depth), lambda i: (0, 0, 0, 0))
    all_gas = whole((7, planes, rows, depth))
    rim = whole((7, 1, rows, depth))
    species_next = gas_sources = None
    at = 0
    for c, size in enumerate(PARTS):
        first = at // MANY
        at += size
        out_specs = [by_kind(first, planes, rows, depth)]
        out_shape = [shaped(*species.shape)]
        if c == 0:
            extra, extra_specs = (main, from_below, from_above), [all_gas, rim, rim]
            out_specs.append(all_gas)
            out_shape.append(shaped(7, planes, rows, depth))
        else:
            extra, extra_specs = (gas_sources, species_next), [row0, hbm]
        got = pl.pallas_call(
            functools.partial(transport_kernel, c == 0, first),
            grid=(size // MANY,),
            in_specs=[
                smem,
                by_kind(first, planes, rows, depth),
                by_kind(first, 2, rows, depth),
                by_kind(first, 2, rows, depth),
                by_kind(first, planes, 2, depth),
                by_kind(first, planes, 2, depth),
                row0,
                gas,
            ]
            + extra_specs,
            out_specs=out_specs,
            out_shape=out_shape,
            input_output_aliases={} if c == 0 else {9: 0},
            scratch_shapes=[pltpu.VMEM((MANY, rows + 16, depth), F32)],
            compiler_params=limit,
            name="transport",
        )(diffusion, species, x_lo, x_hi, y_lo, y_hi, gas_velocity, gas_density, *extra)
        species_next = got[0]
        if c == 0:
            gas_sources = got[1]
    species_next, returned = lax.optimization_barrier((species_next, returned))
    new_state = sum(returned[1:], returned[0])
    old_state = jnp.concatenate([drop_radius[None], drop_temp[None], drop_velocity], axis=0)
    slot = lax.axis_index("group") * capacity + jnp.arange(capacity, dtype=jnp.int32)
    live = slot < parcel_counts[0]
    parcel_state = jnp.where(live[None], new_state[0:5], old_state)
    return (species_next, gas_sources, parcel_state)


def solution(mesh):
    in_specs = (
        P(None, "space", "group", None),
        P(),
        P("space", "group", None),
        P("space", "group", None),
        P(None, "space", "group", None),
        P(("space", "group")),
        P(("space", "group")),
        P(None, ("space", "group")),
        P(None, ("space", "group")),
        P(None, ("space", "group")),
        P("space"),
    )
    out_specs = (
        P(None, "space", "group", None),
        P(None, "space", "group", None),
        P(None, ("space", "group")),
    )
    return jax.shard_map(
        per_device, mesh=mesh, in_specs=in_specs, out_specs=out_specs, check_vma=False
    )
```

```python
import functools

import jax
import jax.numpy as jnp
from jax import lax
from jax.experimental import pallas as pl
from jax.experimental.pallas import tpu as pltpu
from jax.sharding import PartitionSpec as P

time_step = 0.05
evap_coef = 0.5
heat_coef = 0.15
latent_coef = 0.2
enthalpy_coef = 1.3
source_coef = 0.5
courant = 0.3

LANES = 128
PARTS = (54,)
MANY = 18
CHUNK = 1536
WINDOW = 256
YPAD = 40
OWN_ROWS = 48
RIM_ROWS = 24
ROWS_WIDTH = (OWN_ROWS + RIM_ROWS) // 8 * LANES
F32 = jnp.float32
BF16 = jnp.bfloat16
NT = (((1,), (1,)), ((), ()))


def halves(value):
    high = value.astype(BF16)
    return high, (value - high.astype(F32)).astype(BF16)


def hat(index, start, fraction):
    away = index - start
    return jnp.where(away == 0.0, 1.0 - fraction, jnp.where(away == 1.0, fraction, 0.0))


def iota(shape, dim):
    return lax.broadcasted_iota(jnp.int32, shape, dim)


def one_hot(dst_row, aligned):
    rel = jnp.broadcast_to(dst_row - aligned.astype(F32), (16, LANES)).astype(BF16)
    rel = jnp.concatenate([rel] * (WINDOW // 16), axis=0)
    places = iota((WINDOW, LANES), 0).astype(F32).astype(BF16)
    return jnp.where(places == rel, jnp.ones_like(rel), jnp.zeros_like(rel))


def cells_of(width):
    return (width - ROWS_WIDTH) // 9 * 8


def physics(interp, radius, drop_temp, velocity):
    heat, density, speed, fuel = interp[0], interp[1], interp[2:5], interp[5]
    slip = [g - v for g, v in zip(speed, velocity)]
    slip_square = slip[0] * slip[0] + slip[1] * slip[1] + slip[2] * slip[2]
    log_flow = jnp.log(1.0 + density * radius * slip_square)
    sherwood = 2.0 + 0.6 * jnp.exp(0.25 * log_flow)
    surface = 0.5 / (1.0 + jnp.exp(-4.0 * (drop_temp - 1.0)))
    evap = evap_coef * radius * density * sherwood * jnp.log((1.0 - fuel) / (1.0 - surface))
    mass = radius * radius * radius
    ratio = 1.0 - time_step * evap / mass
    new_radius = radius * jnp.exp(jnp.log(ratio) * (1.0 / 3.0))
    rate = time_step * (1.0 + 0.15 * jnp.exp(0.35 * log_flow)) / (2.0 * radius * radius)
    change = [rate * s for s in slip]
    new_velocity = [v + c for v, c in zip(velocity, change)]
    heat_rate = heat_coef * sherwood / (radius * radius)
    new_temp = drop_temp + time_step * (
        heat_rate * (heat - drop_temp) - latent_coef * evap / mass
    )
    vapour = time_step * evap
    lost = [mass * (v - n) for v, n in zip(velocity, new_velocity)]
    momentum = [m + vapour * v for m, v in zip(lost, velocity)]
    heat_gain = -time_step * mass * heat_rate * (heat - drop_temp)
    enthalpy = enthalpy_coef * vapour * new_temp
    drag = lost[0] * speed[0] + lost[1] * speed[1] + lost[2] * speed[2]
    return [new_radius, new_temp] + new_velocity, [vapour] + momentum + [heat_gain, enthalpy, drag]


def parcel_kernel(
    count_ref,
    pk_ref,
    lo_ref,
    temp_ref,
    dens_ref,
    vel_ref,
    fuel_ref,
    hi_ref,
    main_ref,
    dlo_ref,
    dhi_ref,
    state_ref,
    own_dst_ref,
    off_ref,
    dst_ref,
    cell_scr,
    off_smem,
    sem,
    pieces,
    cv,
    row_scr,
    ft,
    a_hi,
    a_lo,
    interp,
    src,
    dep,
):
    groups = pk_ref.shape[0]
    each = cells_of(pk_ref.shape[2]) // 8
    capacity = each * 8
    slots = groups * capacity
    blocks = slots // LANES
    count, group = count_ref[0], lax.axis_index("group")

    per_line = each // LANES
    for b in range(blocks):
        q, r = divmod(b, capacity // LANES)
        line, at = divmod(r, per_line)
        at = capacity + at * LANES
        cell_scr[b : b + 1, :] = pk_ref[q, line : line + 1, at : at + LANES]
    cell = cell_scr[...].astype(jnp.int32)
    slot = iota((blocks, LANES), 0) * LANES + iota((blocks, LANES), 1)
    y_of = ((cell >> 7) & 127) - group * 32
    mine = jnp.logical_and(slot < count, jnp.logical_and(y_of >= -1, y_of < 32))
    ones = jnp.where(mine, 1.0, 0.0).astype(BF16)
    before = jnp.where(iota((LANES, LANES), 0) < iota((LANES, LANES), 1), 1.0, 0.0).astype(BF16)
    after = jnp.where(iota((LANES, LANES), 1) < iota((LANES, LANES), 0), 1.0, 0.0).astype(BF16)
    full = jnp.ones((LANES, LANES), BF16)
    within = jnp.dot(ones, before, preferred_element_type=F32)
    row_sum = jnp.dot(ones, full, preferred_element_type=F32).astype(BF16)
    offset = jnp.dot(after, row_sum, preferred_element_type=F32)
    dst = jnp.where(mine, within + offset, -1.0)
    dst_ref[...] = dst
    own_dst_ref[...] = jnp.where(y_of >= 0, dst, -1.0)
    counts = lax.dot_general(jnp.ones((16, LANES), BF16), ones, NT, preferred_element_type=F32)
    counts = counts.astype(BF16)
    starts = jnp.dot(counts, before, preferred_element_type=F32)
    total = jnp.dot(counts, full, preferred_element_type=F32)
    first = iota((8, LANES), 0) == 0
    off_ref[...] = jnp.where(first, starts[0:8], total[0:8]).astype(jnp.int32)
    copy = pltpu.make_async_copy(off_ref, off_smem, sem)
    copy.start()

    def split(q, carry):
        for line in range(8):
            cells = pk_ref[q, line : line + 1, capacity : capacity + each]
            cells = jnp.broadcast_to(cells, (8, each)).astype(jnp.int32)
            row = iota((8, each), 0)
            y_place = ((cells >> 7) & 127) - group * 32
            place = jnp.where(row == 0, cells >> 14, jnp.where(row == 1, y_place, cells & 127))
            values = pk_ref[q, :, line * each : (line + 1) * each]
            high, low = halves(jnp.concatenate([values, place.astype(F32)], axis=0))
            at = pl.ds(pl.multiple_of(q * capacity + line * each, each), each)
            pieces[0:16, at] = high
            pieces[16:32, at] = low
        return carry

    lax.fori_loop(0, groups, split, 0)

    zero = jnp.zeros((256, LANES), F32)
    own = [temp_ref, dens_ref, vel_ref.at[0], vel_ref.at[1], vel_ref.at[2], fuel_ref.at[0]]
    planes = temp_ref.shape[0]
    rows = temp_ref.shape[1]
    row_start = capacity + each
    after_me = jnp.minimum(group + 1, groups - 1)
    before_me = jnp.maximum(group - 1, 0)
    for f in range(6):
        row_scr[...] = zero
        for x in range(planes + 2):
            if x == 0:
                block = lo_ref[f, 0]
            elif x == planes + 1:
                block = hi_ref[f, 0]
            else:
                block = own[f][x - 1]
            row_scr[x * YPAD : x * YPAD + rows, :] = block
            block, line = row_place(planes, f, x, 0)
            at = row_start + block * LANES
            following = pk_ref[after_me, line : line + 1, at : at + LANES]
            row_scr[x * YPAD + rows : x * YPAD + rows + 1, :] = following
            block, line = row_place(planes, f, x, 1)
            at = row_start + block * LANES
            former = pk_ref[before_me, line : line + 1, at : at + LANES]
            row_scr[(x + 1) * YPAD - 1 : (x + 1) * YPAD, :] = former
        high, low = halves(row_scr[...].T)
        at = slice(f * LANES, (f + 1) * LANES)
        ft[at, 0:256] = high
        ft[at, 256:512] = low
        ft[at, 512:768] = high

    cv[...] = jnp.zeros(cv.shape, F32)
    state_ref[...] = jnp.zeros(state_ref.shape, F32)
    dep[...] = jnp.zeros(dep.shape, F32)
    copy.wait()
    live = off_smem[1, 0]

    def compact(i, carry):
        got = []
        for j in range(8):
            b = i * 8 + j
            aligned = (off_smem[0, b] >> 7) << 7
            hot = one_hot(dst_ref[pl.ds(b, 1), :], aligned)
            block = pieces[:, pl.ds(pl.multiple_of(b * LANES, LANES), LANES)]
            got.append((aligned, lax.dot_general(block, hot, NT, preferred_element_type=F32)))
        for aligned, both in got:
            at = pl.ds(pl.multiple_of(aligned, LANES), WINDOW)
            cv[:, at] += both[0:16] + both[16:32]
        return carry

    lax.fori_loop(0, blocks // 8, compact, 0)

    def gather(c, carry):
        at = pl.ds(pl.multiple_of(c * CHUNK, CHUNK), CHUNK)
        valid = c * CHUNK + iota((1, CHUNK), 1) < live
        fx, fy, fz = cv[0:1, at], cv[1:2, at], cv[2:3, at]
        x0, z0 = cv[8:9, at], cv[10:11, at]
        y0 = jnp.where(valid, cv[9:10, at], 1000.0)
        line = iota((YPAD, CHUNK), 0)
        wy = hat(jnp.where(line == YPAD - 1, -1, line).astype(F32), y0, fy)
        parts = [wy * hat(float(x), x0, fx) for x in range(planes + 2)]
        parts.append(jnp.zeros((256 - (planes + 2) * YPAD, CHUNK), F32))
        high, low = halves(jnp.concatenate(parts, axis=0))
        a_hi[c] = high
        a_lo[c] = low
        stacked = jnp.concatenate([high, high, low], axis=0)
        lines = jnp.dot(ft[...], stacked, preferred_element_type=F32)
        wz = hat(iota((LANES, CHUNK), 0).astype(F32), z0, fz)
        for f in range(6):
            interp[f : f + 1, at] = jnp.sum(
                lines[f * LANES : (f + 1) * LANES] * wz, axis=0, keepdims=True
            )
        return carry

    chunks = (live + CHUNK - 1) // CHUNK
    lax.fori_loop(0, chunks, gather, 0)

    def step(c, carry):
        at = pl.ds(pl.multiple_of(c * CHUNK, CHUNK), CHUNK)
        valid = c * CHUNK + iota((1, CHUNK), 1) < live
        inside = [jnp.where(valid, interp[f : f + 1, at], 0.0) for f in range(6)]
        radius = jnp.where(valid, cv[3:4, at], 1.0)
        velocity = [cv[d : d + 1, at] for d in (5, 6, 7)]
        new, sources = physics(inside, radius, cv[4:5, at], velocity)
        for s in range(5):
            state_ref[s : s + 1, at] = jnp.where(valid, new[s], 0.0)
        for k in range(7):
            src[k : k + 1, at] = jnp.where(valid, sources[k], 0.0)
        return carry

    lax.fori_loop(0, (live + CHUNK - 1) // CHUNK, step, 0)

    def deposit(c, carry):
        at = pl.ds(pl.multiple_of(c * CHUNK, CHUNK), CHUNK)
        wz = hat(iota((LANES, CHUNK), 0).astype(F32), cv[10:11, at], cv[2:3, at])
        high, low = halves(jnp.concatenate([wz * src[k : k + 1, at] for k in range(7)], axis=0))
        left = jnp.concatenate([high, low, high], axis=1)
        right = jnp.concatenate([a_hi[c], a_hi[c], a_lo[c]], axis=1)
        dep[...] += lax.dot_general(left, right, NT, preferred_element_type=F32)
        return carry

    lax.fori_loop(0, chunks, deposit, 0)

    for k in range(7):
        cells = dep[k * LANES : (k + 1) * LANES, :].T
        for x in range(planes + 2):
            block = cells[x * YPAD : x * YPAD + rows]
            if x == 0:
                dlo_ref[k, 0] = block
            elif x == planes + 1:
                dhi_ref[k, 0] = block
            else:
                main_ref[k, x - 1] = block


def spread_kernel(off_ref, dst_ref, state_ref, *outs_and_scratch):
    both_scr = outs_and_scratch[-1]
    high, low = halves(state_ref[...])
    both_scr[0:16, :] = jnp.concatenate([high, low], axis=0)
    outs = outs_and_scratch[:-1]
    group = lax.axis_index("group")
    each = dst_ref.shape[0] // len(outs)
    for d, out in enumerate(outs):
        owner = lax.rem(group + d, len(outs))

        def spread(i, carry, owner=owner, out=out):
            for j in range(8):
                b = owner * each + i * 8 + j
                aligned = (off_ref[0, b] >> 7) << 7
                hot = one_hot(dst_ref[pl.ds(b, 1), :], aligned)
                block = both_scr[:, pl.ds(pl.multiple_of(aligned, LANES), WINDOW)]
                got = jnp.dot(block, hot, preferred_element_type=F32)
                at = pl.ds(pl.multiple_of((i * 8 + j) * LANES, LANES), LANES)
                out[:, at] = got[0:8] + got[8:16]
            return carry

        lax.fori_loop(0, each // 8, spread, 0)


def pack_kernel(
    cells_ref,
    weights_ref,
    radius_ref,
    temp_ref,
    velocity_ref,
    gas_temp_ref,
    dens_ref,
    vel_ref,
    fuel_ref,
    packed_ref,
    top_ref,
    bottom_ref,
):
    planes = gas_temp_ref.shape[0]
    own = [gas_temp_ref, dens_ref, vel_ref.at[0], vel_ref.at[1], vel_ref.at[2], fuel_ref.at[0]]
    for f in range(6):
        top_ref[f, 0] = own[f][planes - 1]
        bottom_ref[f, 0] = own[f][0]
    w = [weights_ref[c : c + 1, :] for c in range(8)]
    slots = cells_ref.shape[1]
    each = slots // 8
    packed_ref[0:1, 0:slots] = (w[4] + w[5]) + (w[6] + w[7])
    packed_ref[1:2, 0:slots] = (w[2] + w[3]) + (w[6] + w[7])
    packed_ref[2:3, 0:slots] = (w[1] + w[3]) + (w[5] + w[7])
    packed_ref[3:4, 0:slots] = radius_ref[...].reshape(1, -1)
    packed_ref[4:5, 0:slots] = temp_ref[...].reshape(1, -1)
    packed_ref[5:8, 0:slots] = velocity_ref[...]
    for i in range(8):
        first = cells_ref[0:1, i * each : (i + 1) * each]
        packed_ref[i : i + 1, slots : slots + each] = first.astype(F32)
    rows = gas_temp_ref.shape[1]
    for f in range(6):
        for x in range(planes):
            for side, y in enumerate((0, rows - 1)):
                block, line = row_place(planes, f, x + 1, side)
                at = slots + each + block * LANES
                packed_ref[line : line + 1, at : at + LANES] = own[f][x, y : y + 1, :]


def rims_kernel(species_ref, up_ref, down_ref, right_ref, left_ref):
    planes, rows = species_ref.shape[1:3]
    up_ref[...] = species_ref[:, planes - 2 : planes]
    down_ref[...] = species_ref[:, 0:2]
    right_ref[...] = species_ref[:, :, rows - 2 : rows]
    left_ref[...] = species_ref[:, :, 0:2]


def assemble_kernel(packed_ref, lo_ref, hi_ref, out_ref):
    planes = OWN_ROWS // 12
    rows = lo_ref.shape[2]
    for f in range(6):
        for x, plane in ((0, lo_ref.at[f, 0]), (planes + 1, hi_ref.at[f, 0])):
            for side, y in enumerate((0, rows - 1)):
                block, line = row_place(planes, f, x, side)
                at = (block - OWN_ROWS // 8) * LANES
                out_ref[line : line + 1, at : at + LANES] = plane[y : y + 1, :]


def row_place(planes, f, x, side):
    if 0 < x <= planes:
        return divmod((f * planes + x - 1) * 2 + side, 8)
    return divmod(planes * 12 + (f * 2 + (x > 0)) * 2 + side, 8)


def transport_kernel(
    first_part,
    first_block,
    diff_ref,
    y_ref,
    xlo_ref,
    xhi_ref,
    ylo_ref,
    yhi_ref,
    ux_ref,
    dens_ref,
    *rest,
):
    if first_part:
        main_ref, below_ref, above_ref, out_ref, gas_ref, pad = rest

        @pl.when(pl.program_id(0) == 0)
        def _():
            last = main_ref.shape[1] - 1
            for k in range(main_ref.shape[0]):
                for x in range(last + 1):
                    total = main_ref[k, x]
                    if x == 0:
                        total = total + below_ref[k, 0]
                    if x == last:
                        total = total + above_ref[k, 0]
                    gas_ref[k, x] = total

        vap_ref = gas_ref.at[0]
    else:
        vap_ref, _, out_ref, pad = rest
    species, planes, rows, depth = y_ref.shape
    at = iota((rows, depth), 1)
    left1 = jnp.where(at >= 1, 16.0, 0.0)
    left2 = jnp.where(at >= 2, -1.0, 0.0)
    right1 = jnp.where(at < depth - 1, 16.0, 0.0)
    right2 = jnp.where(at < depth - 2, -1.0, 0.0)
    first = (first_block + pl.program_id(0)) * species
    for x in range(planes):
        speed = ux_ref[x] * (courant / 12.0)
        gain = source_coef * vap_ref[x] / dens_ref[x]

        for s in range(species):
            d12 = diff_ref[first + s] * (1.0 / 12.0)

            def plane(i, s=s):
                if i < 0:
                    return xlo_ref[s, i + 2]
                if i >= planes:
                    return xhi_ref[s, i - planes]
                return y_ref[s, i]

            center = plane(x)
            up1, up2, dn1, dn2 = plane(x + 1), plane(x + 2), plane(x - 1), plane(x - 2)
            pad[s, 6:8, :] = ylo_ref[s, x]
            pad[s, 8 : 8 + rows, :] = center
            pad[s, 8 + rows : 10 + rows, :] = yhi_ref[s, x]
            near = up1 + dn1 + pad[s, 7 : 7 + rows, :] + pad[s, 9 : 9 + rows, :]
            far = up2 + dn2 + pad[s, 6 : 6 + rows, :] + pad[s, 10 : 10 + rows, :]
            along = (
                left1 * pltpu.roll(center, 1, 1)
                + right1 * pltpu.roll(center, depth - 1, 1)
                + left2 * pltpu.roll(center, 2, 1)
                + right2 * pltpu.roll(center, depth - 2, 1)
            )
            slope = 8.0 * (up1 - dn1) - (up2 - dn2)
            flag = jnp.where(first + s == 0, 1.0, 0.0)
            laplace = 16.0 * near - far + along - 90.0 * center
            out_ref[s, x] = center + d12 * laplace - speed * slope + gain * (flag - center)


def per_device(
    species,
    diffusion,
    gas_temp,
    gas_density,
    gas_velocity,
    drop_radius,
    drop_temp,
    drop_velocity,
    parcel_cells,
    parcel_weights,
    parcel_counts,
):
    count_s = lax.axis_size("space")
    groups = lax.axis_size("group")
    planes, rows, depth = gas_temp.shape
    kinds = species.shape[0]
    capacity = drop_radius.shape[0]
    slots = capacity * groups
    blocks = slots // LANES
    ahead = [(i, i + 1) for i in range(count_s - 1)]
    back = [(b, a) for a, b in ahead]
    g_ahead = [(i, i + 1) for i in range(groups - 1)]
    g_back = [(b, a) for a, b in g_ahead]

    whole = lambda shape: pl.BlockSpec(shape, lambda i, n=len(shape): (0,) * n)
    smem = pl.BlockSpec(memory_space=pltpu.SMEM)
    hbm = pl.BlockSpec(memory_space=pl.ANY)
    shaped = lambda *shape: jax.ShapeDtypeStruct(shape, F32)
    limit = pltpu.CompilerParams(vmem_limit_bytes=63 * 2**20)
    little = pltpu.CompilerParams(vmem_limit_bytes=2 * 2**20)

    def by_kind(first, *shape):
        return pl.BlockSpec((MANY,) + shape, lambda i: (first + i, 0, 0, 0))

    width = capacity // 8 * 9 + ROWS_WIDTH
    packed, top, bottom = pl.pallas_call(
        pack_kernel,
        grid=(1,),
        in_specs=[
            whole((8, capacity)),
            whole((8, capacity)),
            whole((capacity,)),
            whole((capacity,)),
            whole((3, capacity)),
            whole((planes, rows, depth)),
            whole((planes, rows, depth)),
            whole((3, planes, rows, depth)),
            whole((1, planes, rows, depth)),
        ],
        out_specs=[
            whole((8, width)),
            whole((6, 1, rows, depth)),
            whole((6, 1, rows, depth)),
        ],
        out_shape=[
            shaped(8, width),
            shaped(6, 1, rows, depth),
            shaped(6, 1, rows, depth),
        ],
        compiler_params=limit,
        name="pack",
    )(
        parcel_cells, parcel_weights, drop_radius, drop_temp, drop_velocity,
        gas_temp, gas_density, gas_velocity, species,
    )
    species_cut, packed = lax.optimization_barrier((species, packed))
    x_up, x_down, y_right, y_left = pl.pallas_call(
        rims_kernel,
        grid=(kinds // MANY,),
        in_specs=[by_kind(0, planes, rows, depth)],
        out_specs=[
            by_kind(0, 2, rows, depth),
            by_kind(0, 2, rows, depth),
            by_kind(0, planes, 2, depth),
            by_kind(0, planes, 2, depth),
        ],
        out_shape=[
            shaped(kinds, 2, rows, depth),
            shaped(kinds, 2, rows, depth),
            shaped(kinds, planes, 2, depth),
            shaped(kinds, planes, 2, depth),
        ],
        compiler_params=limit,
        name="rims",
    )(species_cut)
    field_lo = lax.ppermute(top, "space", ahead)
    field_hi = lax.ppermute(bottom, "space", back)
    tail = RIM_ROWS // 8 * LANES
    sent = pl.pallas_call(
        assemble_kernel,
        grid=(1,),
        in_specs=[hbm, whole((6, 1, rows, depth)), whole((6, 1, rows, depth))],
        out_specs=pl.BlockSpec((8, tail), lambda i: (0, width // tail - 1)),
        out_shape=shaped(8, width),
        input_output_aliases={0: 0},
        compiler_params=little,
        name="assemble",
    )(packed, field_lo, field_hi)
    sent, x_up, x_down, y_right, y_left = lax.optimization_barrier(
        (sent, x_up, x_down, y_right, y_left)
    )
    parcels = lax.all_gather(sent, "group", axis=0)

    x_up, x_down, y_right, y_left, parcels = lax.optimization_barrier(
        (x_up, x_down, y_right, y_left, parcels)
    )
    y_lo = lax.ppermute(y_right, "group", g_ahead)
    y_hi = lax.ppermute(y_left, "group", g_back)
    x_up, x_down, y_lo = lax.optimization_barrier((x_up, x_down, y_lo))
    x_lo = lax.ppermute(x_up, "space", ahead)
    x_hi = lax.ppermute(x_down, "space", back)

    chunks = pl.cdiv(slots, CHUNK)
    reach = max(chunks * CHUNK, slots + WINDOW)
    main, dep_lo, dep_hi, state, dst, off = pl.pallas_call(
        parcel_kernel,
        grid=(1,),
        in_specs=[
            smem,
            whole((groups, 8, width)),
            whole((6, 1, rows, depth)),
            whole((planes, rows, depth)),
            whole((planes, rows, depth)),
            whole((3, planes, rows, depth)),
            whole((1, planes, rows, depth)),
            whole((6, 1, rows, depth)),
        ],
        out_specs=[
            whole((7, planes, rows, depth)),
            whole((7, 1, rows, depth)),
            whole((7, 1, rows, depth)),
            whole((8, reach)),
            whole((blocks, LANES)),
            whole((8, LANES)),
        ],
        out_shape=[
            shaped(7, planes, rows, depth),
            shaped(7, 1, rows, depth),
            shaped(7, 1, rows, depth),
            shaped(8, reach),
            shaped(blocks, LANES),
            jax.ShapeDtypeStruct((8, LANES), jnp.int32),
        ],
        scratch_shapes=[
            pltpu.VMEM((blocks, LANES), F32),
            pltpu.VMEM((blocks, LANES), F32),
            pltpu.SMEM((8, LANES), jnp.int32),
            pltpu.SemaphoreType.DMA,
            pltpu.VMEM((32, slots), BF16),
            pltpu.VMEM((16, reach), F32),
            pltpu.VMEM((256, LANES), F32),
            pltpu.VMEM((6 * LANES, 768), BF16),
            pltpu.VMEM((chunks, 256, CHUNK), BF16),
            pltpu.VMEM((chunks, 256, CHUNK), BF16),
            pltpu.VMEM((8, reach), F32),
            pltpu.VMEM((8, reach), F32),
            pltpu.VMEM((7 * LANES, 256), F32),
        ],
        compiler_params=limit,
        name="parcels",
    )(parcel_counts, parcels, field_lo, gas_temp, gas_density, gas_velocity, species, field_hi)

    from_below = lax.ppermute(dep_hi, "space", ahead)
    from_above = lax.ppermute(dep_lo, "space", back)

    spread = pl.pallas_call(
        spread_kernel,
        grid=(1,),
        in_specs=[smem, whole((blocks, LANES)), whole((8, reach))],
        out_specs=[whole((8, capacity))] * groups,
        out_shape=[shaped(8, capacity)] * groups,
        scratch_shapes=[pltpu.VMEM((16, reach), BF16)],
        compiler_params=limit,
        name="spread",
    )(off, dst, state)
    y_lo, y_hi, from_below, from_above, spread = lax.optimization_barrier(
        (y_lo, y_hi, from_below, from_above, spread)
    )
    returned = [spread[0]]
    for d in range(1, groups):
        route = [(i, (i + d) % groups) for i in range(groups)]
        returned.append(lax.ppermute(spread[d], "group", route))
    gas = pl.BlockSpec((planes, rows, depth), lambda i: (0, 0, 0))
    row0 = pl.BlockSpec((None, planes, rows, depth), lambda i: (0, 0, 0, 0))
    all_gas = whole((7, planes, rows, depth))
    rim = whole((7, 1, rows, depth))
    species_next = gas_sources = None
    at = 0
    for c, size in enumerate(PARTS):
        first = at // MANY
        at += size
        out_specs = [by_kind(first, planes, rows, depth)]
        out_shape = [shaped(*species.shape)]
        if c == 0:
            extra, extra_specs = (main, from_below, from_above), [all_gas, rim, rim]
            out_specs.append(all_gas)
            out_shape.append(shaped(7, planes, rows, depth))
        else:
            extra, extra_specs = (gas_sources, species_next), [row0, hbm]
        got = pl.pallas_call(
            functools.partial(transport_kernel, c == 0, first),
            grid=(size // MANY,),
            in_specs=[
                smem,
                by_kind(first, planes, rows, depth),
                by_kind(first, 2, rows, depth),
                by_kind(first, 2, rows, depth),
                by_kind(first, planes, 2, depth),
                by_kind(first, planes, 2, depth),
                row0,
                gas,
            ]
            + extra_specs,
            out_specs=out_specs,
            out_shape=out_shape,
            input_output_aliases={} if c == 0 else {9: 0},
            scratch_shapes=[pltpu.VMEM((MANY, rows + 16, depth), F32)],
            compiler_params=limit,
            name="transport",
        )(diffusion, species, x_lo, x_hi, y_lo, y_hi, gas_velocity, gas_density, *extra)
        species_next = got[0]
        if c == 0:
            gas_sources = got[1]
    species_next, returned = lax.optimization_barrier((species_next, returned))
    new_state = sum(returned[1:], returned[0])
    old_state = jnp.concatenate([drop_radius[None], drop_temp[None], drop_velocity], axis=0)
    slot = lax.axis_index("group") * capacity + jnp.arange(capacity, dtype=jnp.int32)
    live = slot < parcel_counts[0]
    parcel_state = jnp.where(live[None], new_state[0:5], old_state)
    return (species_next, gas_sources, parcel_state)


def solution(mesh):
    in_specs = (
        P(None, "space", "group", None),
        P(),
        P("space", "group", None),
        P("space", "group", None),
        P(None, "space", "group", None),
        P(("space", "group")),
        P(("space", "group")),
        P(None, ("space", "group")),
        P(None, ("space", "group")),
        P(None, ("space", "group")),
        P("space"),
    )
    out_specs = (
        P(None, "space", "group", None),
        P(None, "space", "group", None),
        P(None, ("space", "group")),
    )
    return jax.shard_map(
        per_device, mesh=mesh, in_specs=in_specs, out_specs=out_specs, check_vma=False
    )
```
